32 devices in a mesh: seq: 16 (over z, y, x), head: 2 (over core).
Axes of the slice: x: 2, y: 2, z: 4, core: 2. Of those that a mesh axis runs over, the one named last changes fastest.
Arguments:
- probe_vectors: bfloat16 [2048, 4096], P('seq', 'head'), may hold values from -170 to 170
- mentor_address_vectors: bfloat16 [2048, 1024], P('seq', 'head'), may hold values from -7 to 7
- mentor_content_vectors: bfloat16 [2048, 1024], P('seq', 'head'), may hold values from -6 to 6
- previous_position_blend: float32 [4, 32, 128], P(None, 'head'), may hold values from 0 to 1
- feature_fading_exponent: float32 [32, 128], P('head'), may hold values from -9.5 to -2.5
- fading_narrowing_matrix: float32 [32, 128, 64], P('head'), may hold values from -0.5 to 0.5
- fading_widening_matrix: float32 [32, 64, 128], P('head'), may hold values from -0.75 to 0.75
- diagonal_extra_amount: float32 [32, 128], P('head'), may hold values from -1 to 1
Outputs:
- grad_mix: float32 [4, 32, 128], P(None, 'head')
- grad_decay: float32 [32, 128], P('head')
- grad_down: float32 [32, 128, 64], P('head')
- grad_up: float32 [32, 64, 128], P('head')
- grad_bonus: float32 [32, 128], P('head')
The draws below stay inside these ranges and needn't reach their ends.
All inputs are finite; a program needn't handle non-finite values.
Results may differ from the reference program's by a relative error of at most 0.0035.
Values may be sent and summed in bfloat16 or wider, within the bound.
No kernel may reach another device: no remote copies, remote signals or barrier semaphores. Data moves between devices by JAX's collectives and lax.ppermute only.
A program may use at most 128 MiB of HBM per device.

```python
import math
import jax
import jax.numpy as jnp
from jax import lax

PER_GROUP_WIDTH = 128
KVH = 8
HQG = 4
DECAY_RANK = 64
ASKER_COUNT = 32
TOKENS = 2048


def paired_keys(key, nudge):
    base = jnp.clip(jax.random.normal(key, (TOKENS, KVH * PER_GROUP_WIDTH), jnp.float32), -6.0, 6.0)
    noise = jnp.clip(jax.random.normal(jax.random.fold_in(key, 7), (TOKENS, KVH * PER_GROUP_WIDTH), jnp.float32), -6.0, 6.0)
    positions = jnp.arange(TOKENS, dtype=jnp.int32)
    chosen = ((positions + 20) % 97 == 50) & (positions >= 20)
    source = jnp.clip(positions - 20, 0, TOKENS - 1)
    moved = base[source] + 0.1 * noise
    weight_row = jnp.where(chosen, nudge, 0.0)[:, None]
    return base + weight_row * (moved - base)


def draw_mentor_address_vectors(key, part):
    nudge = 0.0
    return paired_keys(key, nudge).astype(jnp.bfloat16)


def draw_probe_vectors(key, part):
    strength = 0.0
    shared = paired_keys(key, strength)
    key = jax.random.fold_in(key, 3)
    base = 3.0 * jnp.clip(jax.random.normal(key, (TOKENS, ASKER_COUNT * PER_GROUP_WIDTH), jnp.float32), -6.0, 6.0)
    positions = jnp.arange(TOKENS, dtype=jnp.int32)
    chosen = (positions % 97 == 50) & (positions >= 40)
    source = jnp.clip(positions - 40, 0, TOKENS - 1)
    scales = 10.0 + 5.0 * jnp.arange(HQG, dtype=jnp.float32)
    aligned = (shared[source].reshape(TOKENS, KVH, 1, PER_GROUP_WIDTH) * scales[None, None, :, None]).reshape(TOKENS, ASKER_COUNT * PER_GROUP_WIDTH)
    weight_row = jnp.where(chosen, strength, 0.0)[:, None]
    return (base + weight_row * (aligned - base)).astype(jnp.bfloat16)


def levels(rng, dims, cuts, low, largest):
    def one(axis_at, shards_of):
        steps = jax.random.uniform(jax.random.fold_in(jax.random.fold_in(rng, 6), axis_at), (shards_of,), jnp.float32, low / len(cuts), largest / len(cuts))
        return jnp.repeat(jnp.exp(steps), dims[axis_at] // shards_of).reshape((-1,) + (1,) * (len(dims) - axis_at - 1))

    level = one(*cuts[0])
    for cut in cuts[1:]:
        level = level * one(*cut)
    return level


def gaussian(stream_key, shape, deviation, limit, cuts=(), kind=jnp.bfloat16):
    values = deviation * jax.random.normal(stream_key, shape, jnp.float32)
    if cuts:
        values = values * levels(stream_key, shape, cuts, -0.22, 0.18)
    return jnp.clip(values, -limit, limit).astype(kind)


def setup_inputs(seed: int = 0) -> dict:
    streams_of = jax.random.split(jax.random.key(seed), 9)
    probe_vectors = draw_probe_vectors(jax.random.fold_in(streams_of[8], 71), 0)
    mentor_address_vectors = draw_mentor_address_vectors(jax.random.fold_in(streams_of[8], 71), 0)
    mentor_content_vectors = gaussian(streams_of[2], (TOKENS, KVH * PER_GROUP_WIDTH), 1.0, 6.0, ((0, 16), (1, 2)))
    previous_position_blend = jnp.clip(1.0 * jax.random.uniform(streams_of[3], (4, ASKER_COUNT, PER_GROUP_WIDTH), jnp.float32) ** levels(streams_of[3], (4, ASKER_COUNT, PER_GROUP_WIDTH), ((1, 2),), -0.2, 0.2), 0.0, 1.0)
    feature_fading_exponent = jnp.clip(-9.5 + 7.0 * jax.random.uniform(streams_of[4], (ASKER_COUNT, PER_GROUP_WIDTH), jnp.float32) ** levels(streams_of[4], (ASKER_COUNT, PER_GROUP_WIDTH), ((0, 2),), -0.2, 0.2), -9.5, -2.5)
    fading_narrowing_matrix = gaussian(streams_of[5], (ASKER_COUNT, PER_GROUP_WIDTH, DECAY_RANK), PER_GROUP_WIDTH ** -0.5, 0.5, ((0, 2),), jnp.float32)
    fading_widening_matrix = gaussian(streams_of[6], (ASKER_COUNT, DECAY_RANK, PER_GROUP_WIDTH), DECAY_RANK ** -0.5, 0.75, ((0, 2),), jnp.float32)
    diagonal_extra_amount = jnp.clip(jax.random.uniform(streams_of[7], (ASKER_COUNT, PER_GROUP_WIDTH), jnp.float32, -1.0, 1.0) * levels(streams_of[7], (ASKER_COUNT, PER_GROUP_WIDTH), ((0, 2),), -0.4, 0.0), -1.0, 1.0)
    return dict(probe_vectors=probe_vectors, mentor_address_vectors=mentor_address_vectors, mentor_content_vectors=mentor_content_vectors, previous_position_blend=previous_position_blend, feature_fading_exponent=feature_fading_exponent, fading_narrowing_matrix=fading_narrowing_matrix, fading_widening_matrix=fading_widening_matrix, diagonal_extra_amount=diagonal_extra_amount)


highest_precision = lax.Precision.HIGHEST
neg_large = -1e+30
norm_eps = 0.00064

def teacher_attention(probe_vectors, mentor_address_vectors, mentor_content_vectors):
    block_len = math.gcd(512, TOKENS)
    blocks = TOKENS // block_len
    query_blocks = probe_vectors.reshape(blocks, block_len, KVH, HQG, PER_GROUP_WIDTH)
    key_blocks = mentor_address_vectors.reshape(blocks, block_len, KVH, PER_GROUP_WIDTH)
    value_blocks = mentor_content_vectors.reshape(blocks, block_len, KVH, PER_GROUP_WIDTH)
    scale_factor = 1.0 / math.sqrt(PER_GROUP_WIDTH)

    def one_block(block_id):
        query_part = query_blocks[block_id].astype(jnp.float32)
        query_pos = block_id * block_len + jnp.arange(block_len, dtype=jnp.int32)

        def visit(key_id, carried_memory):
            row_max, row_sum, accum = carried_memory
            key_part = key_blocks[key_id].astype(jnp.float32)
            value_part = value_blocks[key_id].astype(jnp.float32)
            scores = jnp.einsum('qghd,kgd->ghqk', query_part, key_part, precision=highest_precision) * scale_factor
            key_pos = key_id * block_len + jnp.arange(block_len, dtype=jnp.int32)
            visible = query_pos[:, None] >= key_pos[None, :]
            scores = jnp.where(visible, scores, neg_large)
            new_max = jnp.maximum(row_max, lax.optimization_barrier(jnp.max(scores, axis=-1)))
            probs = jnp.where(visible, jnp.exp(scores - new_max[..., None]), 0.0)
            rescale = jnp.exp(row_max - new_max)
            row_sum = row_sum * rescale + lax.optimization_barrier(jnp.sum(probs, axis=-1))
            rounded = lax.optimization_barrier(probs.astype(jnp.bfloat16)).astype(jnp.float32)
            accum = accum * jnp.transpose(rescale, (2, 0, 1))[..., None] + jnp.einsum('ghqk,kgd->qghd', rounded, value_part, precision=highest_precision)
            return (new_max, row_sum, accum)
        start_state = (jnp.full((KVH, HQG, block_len), neg_large, jnp.float32), jnp.zeros((KVH, HQG, block_len), jnp.float32), jnp.zeros((block_len, KVH, HQG, PER_GROUP_WIDTH), jnp.float32))
        row_max, row_sum, accum = lax.fori_loop(0, block_id + 1, visit, start_state)
        return (accum / jnp.transpose(row_sum, (2, 0, 1))[..., None]).astype(jnp.bfloat16)
    outputs = lax.map(one_block, jnp.arange(blocks, dtype=jnp.int32))
    return outputs.reshape(TOKENS, ASKER_COUNT, PER_GROUP_WIDTH)

def previous(values_in):
    return jnp.concatenate([jnp.zeros_like(values_in[:1]), values_in[:-1]], axis=0)

def group_norm(values_in):
    centre = lax.optimization_barrier(jnp.mean(values_in, axis=-1, keepdims=True))
    centered = values_in - centre
    spread = lax.optimization_barrier(jnp.mean(centered * centered, axis=-1, keepdims=True))
    return centered * lax.rsqrt(spread + norm_eps)

def scaled_memory_segment(diagonal_extra_vector, memory_matrix, hidden_activations):
    gate_vectors, lagged_address_blend, lagged_content_blend, token_log_decay = hidden_activations
    block_len = gate_vectors.shape[0]
    inclusive = jnp.cumsum(token_log_decay, axis=0)
    exclusive = inclusive - token_log_decay
    carried_in = jnp.einsum('thi,hij->thj', gate_vectors * jnp.exp(exclusive), memory_matrix, precision=highest_precision)
    position = jnp.arange(block_len, dtype=jnp.int32)
    before = (position[:, None] > position[None, :])[:, :, None, None]
    spread = jnp.where(before, exclusive[:, None] - inclusive[None, :], 0.0)
    factor = jnp.where(before, jnp.exp(spread), 0.0)
    scores = jnp.einsum('thi,shi,tshi->hts', gate_vectors, lagged_address_blend, factor, precision=highest_precision)
    inner_part = jnp.einsum('hts,shj->thj', scores, lagged_content_blend, precision=highest_precision)
    diagonal_contribution = lax.optimization_barrier(jnp.sum(gate_vectors * diagonal_extra_vector * lagged_address_blend, axis=-1))[..., None] * lagged_content_blend
    block_total = inclusive[-1]
    new_state = jnp.exp(block_total)[:, :, None] * memory_matrix + jnp.einsum('shi,shj->hij', lagged_address_blend * jnp.exp(block_total - inclusive), lagged_content_blend, precision=highest_precision)
    return (new_state, carried_in + inner_part + diagonal_contribution)

def student_attention(learner_settings, probe_vectors, mentor_address_vectors, mentor_content_vectors):
    previous_position_blend, feature_fading_exponent, fading_narrowing_matrix, fading_widening_matrix, diagonal_extra_amount = learner_settings
    query_f = probe_vectors.astype(jnp.float32).reshape(TOKENS, ASKER_COUNT, PER_GROUP_WIDTH)
    key_f = jnp.repeat(mentor_address_vectors.astype(jnp.float32).reshape(TOKENS, KVH, PER_GROUP_WIDTH), HQG, axis=1)
    value_f = jnp.repeat(mentor_content_vectors.astype(jnp.float32).reshape(TOKENS, KVH, PER_GROUP_WIDTH), HQG, axis=1)
    gate_vectors = query_f + previous_position_blend[0] * (previous(query_f) - query_f)
    lagged_address_blend = key_f + previous_position_blend[1] * (previous(key_f) - key_f)
    lagged_content_blend = value_f + previous_position_blend[2] * (previous(value_f) - value_f)
    decay_input = query_f + previous_position_blend[3] * (previous(query_f) - query_f)
    low_rank_decay = jnp.tanh(jnp.einsum('ydj,dja->yda', decay_input, fading_narrowing_matrix, precision=highest_precision))
    token_log_decay = -jnp.exp(feature_fading_exponent + jnp.einsum('dby,byp->dbp', low_rank_decay, fading_widening_matrix, precision=highest_precision))
    block_len = math.gcd(64, TOKENS)
    blocks = TOKENS // block_len

    def split_blocks(array_in):
        return array_in.reshape(blocks, block_len, ASKER_COUNT, PER_GROUP_WIDTH)

    def advance(memory_matrix, hidden_activations):
        return jax.checkpoint(scaled_memory_segment)(diagonal_extra_amount, memory_matrix, hidden_activations)
    start_state = jnp.zeros((ASKER_COUNT, PER_GROUP_WIDTH, PER_GROUP_WIDTH), jnp.float32)
    final_state, outputs = lax.scan(advance, start_state, (split_blocks(gate_vectors), split_blocks(lagged_address_blend), split_blocks(lagged_content_blend), split_blocks(token_log_decay)))
    return outputs.reshape(TOKENS, ASKER_COUNT, PER_GROUP_WIDTH)

def reference(probe_vectors, mentor_address_vectors, mentor_content_vectors, previous_position_blend, feature_fading_exponent, fading_narrowing_matrix, fading_widening_matrix, diagonal_extra_amount):
    teacher_out = teacher_attention(probe_vectors, mentor_address_vectors, mentor_content_vectors).astype(jnp.float32)

    def loss_of(learner_settings):
        student_norm = group_norm(student_attention(learner_settings, probe_vectors, mentor_address_vectors, mentor_content_vectors))
        difference = student_norm - teacher_out
        return jnp.sum(difference * difference) / TOKENS
    learner_settings = (previous_position_blend, feature_fading_exponent, fading_narrowing_matrix, fading_widening_matrix, diagonal_extra_amount)
    loss_value, pullback = jax.vjp(loss_of, learner_settings)
    grads, = pullback(jnp.ones_like(loss_value))
    return (grads[0], grads[1], grads[2], grads[3], grads[4])
```

```python
import math

import jax
import jax.numpy as jnp
from jax import lax
from jax.experimental import pallas as pl
from jax.experimental.pallas import tpu as pltpu
from jax.sharding import PartitionSpec as P

NORM_EPS = 0.00064
NEG_LARGE = -1e30
CHUNK = 128
SAFE_EXPONENT = 30.0
PACK_TAIL = 8

f32 = jnp.float32
bf16 = jnp.bfloat16

NN = (((1,), (0,)), ((), ()))
NT = (((1,), (1,)), ((), ()))
TN = (((0,), (0,)), ((), ()))


def dot(a, b, dims):
    return lax.dot_general(a, b, dims, preferred_element_type=f32)


def split2(x):
    high = x.astype(bf16)
    return high, (x - high.astype(f32)).astype(bf16)


def split3(x):
    high = x.astype(bf16)
    rest = x - high.astype(f32)
    middle = rest.astype(bf16)
    return high, middle, (rest - middle.astype(f32)).astype(bf16)


def dot3(a, b, dims):
    return dot(a[0], b[0], dims) + (dot(a[0], b[1], dims) + dot(a[1], b[0], dims))


def dot4(a, b, dims):
    return dot(a[0], b[0], dims) + (
        (dot(a[0], b[1], dims) + dot(a[1], b[0], dims)) + dot(a[1], b[1], dims)
    )


def joined(parts):
    return parts[0].astype(f32) + parts[1].astype(f32)


def exact_sums(zero_one, x):
    high, middle, low = split3(x)
    return dot(zero_one, high, NN) + (dot(zero_one, middle, NN) + dot(zero_one, low, NN))


def row_ids(shape):
    return lax.broadcasted_iota(jnp.int32, shape, 0)


def lane_ids(shape):
    return lax.broadcasted_iota(jnp.int32, shape, 1)


def zero_one(condition):
    return jnp.where(condition, 1.0, 0.0).astype(bf16)


def with_shift(ref, start, rows):
    now = ref[pl.ds(start, rows), :].astype(f32)
    tail = ref[pl.ds(pl.multiple_of(jnp.maximum(start - 16, 0), 16), 16), :].astype(f32)[15:16]
    tail = jnp.where(start > 0, tail, 0.0)
    earlier = jnp.where(row_ids(now.shape) == 0, tail, pltpu.roll(now, 1, 0))
    return now, earlier - now


def teacher_phase(q_ref, k_ref, v_ref, teach, scores, q_rows, k_rows):
    tokens, width = q_ref.shape
    scale = 1.0 / math.sqrt(width)

    def q_block(i, _):
        start = pl.multiple_of(i * q_rows, q_rows)
        q = q_ref[pl.ds(start, q_rows), :]
        blocks = (start + q_rows + k_rows - 1) // k_rows

        def score_block(j, top):
            first = pl.multiple_of(j * k_rows, k_rows)
            s = dot(q, k_ref[pl.ds(first, k_rows), :], NT) * scale
            seen = start + row_ids(s.shape) >= first + lane_ids(s.shape)
            s = jnp.where(seen, s, NEG_LARGE)
            scores[j] = s
            for n in range(k_rows // 128):
                top = jnp.maximum(top, s[:, n * 128 : (n + 1) * 128])
            return top

        top = lax.fori_loop(0, blocks, score_block, jnp.full((q_rows, 128), NEG_LARGE, f32))
        row_top = jnp.max(top, axis=1, keepdims=True)

        def value_block(j, carry):
            total, accum = carry
            first = pl.multiple_of(j * k_rows, k_rows)
            p = jnp.exp(scores[j] - row_top)
            for n in range(k_rows // 128):
                total = total + p[:, n * 128 : (n + 1) * 128]
            return total, accum + dot(p.astype(bf16), v_ref[pl.ds(first, k_rows), :], NN)

        total, accum = lax.fori_loop(
            0,
            blocks,
            value_block,
            (jnp.zeros((q_rows, 128), f32), jnp.zeros((q_rows, width), f32)),
        )
        teach[pl.ds(start, q_rows), :] = (accum / jnp.sum(total, axis=1, keepdims=True)).astype(
            bf16
        )
        return 0

    lax.fori_loop(0, tokens // q_rows, q_block, 0)


def decay_phase(q_ref, down, up, fade, mix, lw_s, ex_s, hid_s, rows):
    tokens, width = q_ref.shape
    square = (CHUNK, CHUNK)
    before = zero_one(row_ids(square) > lane_ids(square))

    def block(i, worst):
        start = pl.multiple_of(i * rows, rows)
        q, q_step = with_shift(q_ref, start, rows)
        hid = jnp.tanh(dot3(split2(q + mix[3] * q_step), down, NN))
        lw = -jnp.exp(fade + dot3(split2(hid), up, NN))
        hid_s[pl.ds(start, rows), :] = hid
        lw_s[pl.ds(start, rows), :] = lw
        for n in range(rows // CHUNK):
            part = lw[n * CHUNK : (n + 1) * CHUNK]
            ex = exact_sums(before, part)
            ex_s[pl.ds(pl.multiple_of(start + n * CHUNK, CHUNK), CHUNK), :] = ex
            middle = ex[CHUNK // 2 : CHUNK // 2 + 1]
            total = ex[CHUNK - 1 :] + part[CHUNK - 1 :]
            worst = jnp.maximum(worst, jnp.maximum(-middle, middle - total))
        return worst

    return lax.fori_loop(0, tokens // rows, block, jnp.zeros((1, width), f32))


def level_parts(level, lw, r, k):
    square = (CHUNK, CHUNK)
    t, m = row_ids(square), lane_ids(square)
    edge = ((t >> (level + 1)) << (level + 1)) + (1 << level) - 1
    upper = ((t >> level) & 1) == 1
    lower = ((t >> level) & 1) == 0
    span = zero_one((upper & (m > edge) & (m < t)) | (lower & (m > t) & (m <= edge)))
    factor = jnp.exp(exact_sums(span, lw))
    upper_rows = ((row_ids(r.shape) >> level) & 1) == 1
    r_factor = jnp.where(upper_rows, factor, 0.0)
    k_factor = jnp.where(upper_rows, 0.0, factor)
    same = (t >> (level + 1)) == (m >> (level + 1))
    return r_factor, k_factor, split2(r * r_factor), split2(k * k_factor), same, span


def student_phase(fast, refs, mix, bonus, down, up, scratch, out_ref, unroll):
    q_ref, k_ref, v_ref = refs
    teach, lw_s, ex_s, hid_s, state_s, g_s, a_hi_s, a_lo_s = scratch
    tokens, width = q_ref.shape
    chunks = tokens // CHUNK
    levels = CHUNK.bit_length() - 1
    square = (CHUNK, CHUNK)
    t, m = row_ids(square), lane_ids(square)
    below = t > m
    after, before = zero_one(t < m), zero_one(below)
    gain = 2.0 / tokens

    def load(c):
        start = pl.multiple_of(c * CHUNK, CHUNK)
        rows = pl.ds(start, CHUNK)
        q, q_step = with_shift(q_ref, start, CHUNK)
        k0, k_step = with_shift(k_ref, start, CHUNK)
        v0, v_step = with_shift(v_ref, start, CHUNK)
        r = q + mix[0] * q_step
        k = k0 + mix[1] * k_step
        v = v0 + mix[2] * v_step
        lw, ex = lw_s[rows, :], ex_s[rows, :]
        total = ex[CHUNK - 1 :] + lw[CHUNK - 1 :]
        if fast:
            middle = ex[CHUNK // 2 : CHUNK // 2 + 1]
            r_factor = jnp.exp(ex - middle)
            k_factor = jnp.exp(middle - ex - lw)
            into, out = jnp.exp(middle), jnp.exp(total - middle)
        else:
            r_factor = jnp.exp(ex)
            k_factor = jnp.exp(exact_sums(after, lw))
            into = out = None
        return rows, q, q_step, k_step, v_step, r, k, v, lw, total, r_factor, k_factor, into, out

    def scaled(x, by):
        return x if by is None else x * by

    def forward(c, state):
        rows, _, _, _, _, r, k, v, lw, total, r_factor, k_factor, into, out = load(c)
        rs, ks, vs = split2(r * r_factor), split2(k * k_factor), split2(v)
        if fast:
            a = jnp.where(below, dot3(rs, ks, NT), 0.0)
        else:

            def one_level(level, a):
                _, _, r_part, k_part, block, _ = level_parts(level, lw, r, k)
                return a + jnp.where(block, dot3(r_part, k_part, NT), 0.0)

            a = lax.fori_loop(0, levels, one_level, jnp.zeros(square, f32))
        own = jnp.sum(r * bonus * k, axis=1, keepdims=True)
        a = split2(a)
        state_s[c] = state
        o = own * v + dot3(a, vs, NN) + dot3(rs, split2(scaled(state, into)), NT)
        o = o - jnp.mean(o, axis=1, keepdims=True)
        rate = lax.rsqrt(jnp.mean(o * o, axis=1, keepdims=True) + NORM_EPS)
        normed = o * rate
        g = gain * (normed - teach[rows, :].astype(f32))
        g = g - jnp.mean(g, axis=1, keepdims=True) - normed * jnp.mean(
            g * normed, axis=1, keepdims=True
        )
        g_s[rows, :] = g * rate
        a_hi_s[rows, :] = a[0]
        a_lo_s[rows, :] = a[1]
        return state * jnp.exp(total) + scaled(dot3(vs, ks, TN), out)

    def forward_some(i, state):
        for n in range(unroll):
            state = forward(i * unroll + n, state)
        return state

    state = lax.fori_loop(0, chunks // unroll, forward_some, jnp.zeros((width, width), f32))
    state_s[chunks] = state

    def backward(c, carry):
        cot, up_sum, down_sum, sums = carry
        rows, q, q_step, k_step, v_step, r, k, v, lw, total, r_factor, k_factor, into, out = load(c)
        rs, ks, vs = split2(r * r_factor), split2(k * k_factor), split2(v)
        g = g_s[rows, :]
        gs = split2(g)
        a = (a_hi_s[rows, :], a_lo_s[rows, :])
        pair = dot3(gs, vs, NT)
        cot_out = split2(scaled(cot, out))
        dr = r_factor * dot3(gs, split2(scaled(state_s[c], into)), NN)
        dk = k_factor * dot3(vs, cot_out, NN)
        dv = dot3(a, gs, TN) + dot3(ks, cot_out, NT)
        from_later, from_earlier = r * dr, k * dk
        dlw = jnp.sum(state_s[c] * jnp.exp(total) * cot, axis=0, keepdims=True)
        if fast:
            pairs = split2(jnp.where(below, pair, 0.0))
            dr_in, dk_in = dot4(pairs, ks, NN), dot4(pairs, rs, TN)
            k_in = joined(ks) * dk_in
            from_later = from_later + (joined(rs) * dr_in - k_in)
            dlw = dlw - k_in
            dr = dr + r_factor * dr_in
            dk = dk + k_factor * dk_in
        else:

            def one_level(level, parts):
                dr, dk, dlw = parts
                r_by, k_by, r_part, k_part, block, span = level_parts(level, lw, r, k)
                pairs = split2(jnp.where(block & below, pair, 0.0))
                dr_in = r_by * dot3(pairs, k_part, NN)
                dk_in = k_by * dot3(pairs, r_part, TN)
                inside = split3(r * dr_in + k * dk_in)
                return dr + dr_in, dk + dk_in, dlw + sum(dot(span, part, TN) for part in inside)

            dr, dk, dlw = lax.fori_loop(
                0, levels, one_level, (dr, dk, jnp.broadcast_to(dlw, r.shape))
            )
        dlw = dlw + exact_sums(after, from_later) + exact_sums(before, from_earlier)
        dv = dv + jnp.sum(r * bonus * k, axis=1, keepdims=True) * g
        own = jnp.sum(v * g, axis=1, keepdims=True)
        own_r, own_k = own * r, own * k
        dr = dr + bonus * own_k
        dk = dk + bonus * own_r
        dpre = dlw * lw
        hid = hid_s[rows, :]
        dpres = split2(dpre)
        dz = dot3(dpres, up, NT) * (1.0 - hid * hid)
        dzs = split2(dz)
        dxw = dot3(dzs, down, NT)
        up_sum = up_sum + dot3(split2(hid), dpres, TN)
        down_sum = down_sum + dot3(dzs, split2(q + mix[3] * q_step), TN)
        parts = (dr * q_step, dk * k_step, dv * v_step, dxw * q_step, dpre, own_r * k)
        sums = tuple(
            old + jnp.sum(new.reshape(CHUNK // 8, 8, width), axis=0)
            for old, new in zip(sums, parts)
        )
        cot = cot * jnp.exp(total) + scaled(dot3(gs, rs, TN), into)
        return cot, up_sum, down_sum, sums

    def backward_some(i, carry):
        for n in range(unroll):
            carry = backward(chunks - 1 - (i * unroll + n), carry)
        return carry

    rank = hid_s.shape[1]
    empty = jnp.zeros((rank, width), f32)
    start = (jnp.zeros((width, width), f32), empty, empty, (jnp.zeros((8, width), f32),) * 6)
    _, up_sum, down_sum, sums = lax.fori_loop(0, chunks // unroll, backward_some, start)
    out_ref[:rank, :] = up_sum
    out_ref[rank : 2 * rank, :] = down_sum
    for n, part in enumerate(sums):
        out_ref[2 * rank + n : 2 * rank + n + 1, :] = jnp.sum(part, axis=0, keepdims=True)
    out_ref[2 * rank + 6 :, :] = jnp.zeros((PACK_TAIL - 6, width), f32)


def head_kernel(
    head_ref, qkv_ref, mix_ref, fade_ref, down_ref, up_ref, bonus_ref, out_ref, *scratch
):
    scores, teach, lw_s, ex_s, hid_s, *rest = scratch
    tokens = qkv_ref.shape[0]
    width = up_ref.shape[2]
    refs = tuple(qkv_ref.at[:, pl.ds(n * width, width)] for n in range(3))
    head = head_ref[0] + pl.program_id(0)
    mix = [mix_ref[n, pl.ds(head, 1), :] for n in range(4)]
    bonus = bonus_ref[pl.ds(head, 1), :]
    down, up = split2(down_ref[0]), split2(up_ref[0])
    rows = math.gcd(512, tokens)
    worst = decay_phase(
        refs[0], down, up, fade_ref[pl.ds(head, 1), :], mix, lw_s, ex_s, hid_s, rows
    )
    teacher_phase(*refs, teach, scores, math.gcd(256, tokens), math.gcd(512, tokens))
    safe = jnp.max(worst) <= SAFE_EXPONENT
    held = (teach, lw_s, ex_s, hid_s, *rest)

    @pl.when(safe)
    def _():
        student_phase(True, refs, mix, bonus, down, up, held, out_ref.at[0], 2)

    @pl.when(jnp.logical_not(safe))
    def _():
        student_phase(False, refs, mix, bonus, down, up, held, out_ref.at[0], 1)


def head_grads(qkv, first_head, mix, fade, down, up, bonus):
    tokens, columns = qkv.shape
    heads, width, rank = down.shape
    count = columns // (3 * width)
    whole = lambda *_: (0, 0)
    spec = pltpu.PrefetchScalarGridSpec(
        num_scalar_prefetch=1,
        grid=(count,),
        in_specs=[
            pl.BlockSpec((tokens, 3 * width), lambda i, h: (0, i)),
            pl.BlockSpec(mix.shape, lambda i, h: (0, 0, 0)),
            pl.BlockSpec(fade.shape, whole),
            pl.BlockSpec((1, width, rank), lambda i, h: (h[0] + i, 0, 0)),
            pl.BlockSpec((1, rank, width), lambda i, h: (h[0] + i, 0, 0)),
            pl.BlockSpec(bonus.shape, whole),
        ],
        out_specs=pl.BlockSpec((1, 2 * rank + PACK_TAIL, width), lambda i, h: (i, 0, 0)),
        scratch_shapes=[
            pltpu.VMEM(
                (tokens // math.gcd(512, tokens), math.gcd(256, tokens), math.gcd(512, tokens)), f32
            ),
            pltpu.VMEM((tokens, width), bf16),
            pltpu.VMEM((tokens, width), f32),
            pltpu.VMEM((tokens, width), f32),
            pltpu.VMEM((tokens, rank), f32),
            pltpu.VMEM((tokens // CHUNK + 1, width, width), f32),
            pltpu.VMEM((tokens, width), f32),
            pltpu.VMEM((tokens, CHUNK), bf16),
            pltpu.VMEM((tokens, CHUNK), bf16),
        ],
    )
    return pl.pallas_call(
        head_kernel,
        out_shape=jax.ShapeDtypeStruct((count, 2 * rank + PACK_TAIL, width), f32),
        grid_spec=spec,
        compiler_params=pltpu.CompilerParams(
            vmem_limit_bytes=58 * 1024 * 1024, dimension_semantics=("arbitrary",)
        ),
    )(first_head, qkv, mix, fade, down, up, bonus)


def shards(
    probe_vectors,
    mentor_address_vectors,
    mentor_content_vectors,
    previous_position_blend,
    feature_fading_exponent,
    fading_narrowing_matrix,
    fading_widening_matrix,
    diagonal_extra_amount,
):
    tok_rows = probe_vectors.shape[0]
    heads, width, rank = fading_narrowing_matrix.shape
    groups = mentor_address_vectors.shape[1] // width
    place = lax.axis_index("seq")
    count = lax.axis_size("seq")
    copies = max(1, count // heads)
    per_device = max(1, heads // count)
    assert heads * copies == per_device * count
    q = probe_vectors.reshape(tok_rows, heads, 1, width)
    k = jnp.repeat(
        mentor_address_vectors.reshape(tok_rows, groups, 1, width), heads // groups, axis=1
    )
    v = jnp.repeat(
        mentor_content_vectors.reshape(tok_rows, groups, 1, width), heads // groups, axis=1
    )
    qkv = jnp.concatenate([q, k, v], axis=2).reshape(tok_rows, heads, 3 * width)
    qkv = jnp.repeat(qkv, copies, axis=1).reshape(tok_rows, heads * copies * 3 * width)
    qkv = lax.all_to_all(qkv, "seq", split_axis=1, concat_axis=0, tiled=True)
    first_head = (place // copies) * per_device
    packed = head_grads(
        qkv,
        first_head.astype(jnp.int32).reshape(1),
        previous_position_blend,
        feature_fading_exponent,
        fading_narrowing_matrix,
        fading_widening_matrix,
        diagonal_extra_amount,
    )
    packed = lax.all_gather(packed, "seq", axis=0, tiled=True)[::copies]
    grad_up = packed[:, :rank]
    grad_down = jnp.swapaxes(packed[:, rank : 2 * rank], 1, 2)
    tail = packed[:, 2 * rank :]
    grad_mix = jnp.swapaxes(tail[:, :4], 0, 1)
    return grad_mix, tail[:, 4], grad_down, grad_up, tail[:, 5]


def solution(mesh):
    return jax.shard_map(
        shards,
        mesh=mesh,
        in_specs=(
            P("seq", "head"),
            P("seq", "head"),
            P("seq", "head"),
            P(None, "head", None),
            P("head", None),
            P("head", None, None),
            P("head", None, None),
            P("head", None),
        ),
        out_specs=(
            P(None, "head", None),
            P("head", None),
            P("head", None, None),
            P("head", None, None),
            P("head", None),
        ),
        check_vma=False,
    )
```

```python
import math

import jax
import jax.numpy as jnp
from jax import lax
from jax.experimental import pallas as pl
from jax.experimental.pallas import tpu as pltpu
from jax.sharding import PartitionSpec as P

NORM_EPS = 0.00064
NEG_LARGE = -1e30
SAFE_EXPONENT = 30.0
PACK_TAIL = 16
LOG2_E = math.log2(math.e)

f32 = jnp.float32
bf16 = jnp.bfloat16

NN = (((1,), (0,)), ((), ()))
NT = (((1,), (1,)), ((), ()))
TN = (((0,), (0,)), ((), ()))


def dot(a, b, dims):
    return lax.dot_general(a, b, dims, preferred_element_type=f32)


def split2(x):
    high = x.astype(bf16)
    return high, (x - high.astype(f32)).astype(bf16)


def split3(x):
    high = x.astype(bf16)
    rest = x - high.astype(f32)
    middle = rest.astype(bf16)
    return high, middle, (rest - middle.astype(f32)).astype(bf16)


def dot3(a, b, dims):
    return dot(a[0], b[0], dims) + (dot(a[0], b[1], dims) + dot(a[1], b[0], dims))


def dot4(a, b, dims):
    return dot(a[0], b[0], dims) + (
        (dot(a[0], b[1], dims) + dot(a[1], b[0], dims)) + dot(a[1], b[1], dims)
    )


def joined(parts):
    return parts[0].astype(f32) + parts[1].astype(f32)


def exact_sums(zero_one, x):
    high, middle, low = split3(x)
    return dot(zero_one, high, NN) + (dot(zero_one, middle, NN) + dot(zero_one, low, NN))


def row_ids(shape):
    return lax.broadcasted_iota(jnp.int32, shape, 0)


def lane_ids(shape):
    return lax.broadcasted_iota(jnp.int32, shape, 1)


def zero_one(condition):
    return jnp.where(condition, 1.0, 0.0).astype(bf16)


def with_shift(ref, first, slabs=1):
    _, rows, width = ref.shape
    now = ref[pl.ds(first, slabs)].astype(f32).reshape(slabs * rows, width)
    tail = ref[jnp.maximum(first - 1, 0), rows - 16 :, :].astype(f32)[15:16]
    tail = jnp.where(first > 0, tail, 0.0)
    earlier = jnp.where(row_ids(now.shape) == 0, tail, pltpu.roll(now, 1, 0))
    return now, earlier - now


def slabs_of(ref, first, slabs):
    _, rows, width = ref.shape
    return ref[pl.ds(first, slabs)].reshape(slabs * rows, width)


def teacher_phase(q_ref, k_ref, v_ref, teach, scores, q_slabs, k_slabs):
    slabs, slab, width = q_ref.shape
    q_rows, k_rows = q_slabs * slab, k_slabs * slab
    scale = LOG2_E / math.sqrt(width)

    def q_block(i, _):
        q = slabs_of(q_ref, i * q_slabs, q_slabs)
        last = (i * q_slabs + q_slabs - 1) // k_slabs

        def score_block(j, top, edge=False):
            s = dot(q, slabs_of(k_ref, j * k_slabs, k_slabs), NT) * scale
            if edge:
                seen = i * q_rows + row_ids(s.shape) >= j * k_rows + lane_ids(s.shape)
                s = jnp.where(seen, s, NEG_LARGE)
            scores[j] = s
            for n in range(k_rows // 128):
                top = jnp.maximum(top, s[:, n * 128 : (n + 1) * 128])
            return top

        top = lax.fori_loop(0, last, score_block, jnp.full((q_rows, 128), NEG_LARGE, f32))
        top = score_block(last, top, True)
        row_top = jnp.max(top, axis=1, keepdims=True)

        def value_block(j, carry):
            total, accum = carry
            p = jnp.exp2(scores[j] - row_top)
            for n in range(k_rows // 128):
                total = total + p[:, n * 128 : (n + 1) * 128]
            return total, accum + dot(p.astype(bf16), slabs_of(v_ref, j * k_slabs, k_slabs), NN)

        total, accum = lax.fori_loop(
            0,
            last + 1,
            value_block,
            (jnp.zeros((q_rows, 128), f32), jnp.zeros((q_rows, width), f32)),
        )
        out = accum / jnp.sum(total, axis=1, keepdims=True)
        teach[pl.ds(i * q_slabs, q_slabs)] = out.astype(bf16).reshape(q_slabs, slab, width)
        return 0

    lax.fori_loop(0, slabs // q_slabs, q_block, 0)


def decay_phase(q_ref, down, up, fade, mix, lw_s, ex_s, hid_s, slabs):
    count, slab, width = q_ref.shape
    square = (slab, slab)
    before = zero_one(row_ids(square) > lane_ids(square))

    def block(i, worst):
        first = i * slabs
        q, q_step = with_shift(q_ref, first, slabs)
        hid = jnp.tanh(dot3(split2(q + mix[3] * q_step), down, NT))
        lw = -jnp.exp(fade + dot3(split2(hid), up, NN))
        hid_s[pl.ds(first, slabs)] = hid.reshape(slabs, slab, hid.shape[1])
        lw_s[pl.ds(first, slabs)] = lw.reshape(slabs, slab, width)
        for n in range(slabs):
            part = lw[n * slab : (n + 1) * slab]
            ex = exact_sums(before, part)
            ex_s[first + n] = ex
            middle = ex[slab // 2 : slab // 2 + 1]
            total = ex[slab - 1 :] + part[slab - 1 :]
            worst = jnp.maximum(worst, jnp.maximum(-middle, middle - total))
        return worst

    return lax.fori_loop(0, count // slabs, block, jnp.zeros((1, width), f32))


def level_parts(level, lw, r, k):
    square = (lw.shape[0], lw.shape[0])
    t, m = row_ids(square), lane_ids(square)
    edge = ((t >> (level + 1)) << (level + 1)) + (1 << level) - 1
    upper = ((t >> level) & 1) == 1
    lower = ((t >> level) & 1) == 0
    span = zero_one((upper & (m > edge) & (m < t)) | (lower & (m > t) & (m <= edge)))
    factor = jnp.exp(exact_sums(span, lw))
    upper_rows = ((row_ids(r.shape) >> level) & 1) == 1
    r_factor = jnp.where(upper_rows, factor, 0.0)
    k_factor = jnp.where(upper_rows, 0.0, factor)
    same = (t >> (level + 1)) == (m >> (level + 1))
    return r_factor, k_factor, split2(r * r_factor), split2(k * k_factor), same, span


def student_phase(fast, refs, mix, bonus, down, up, scratch, unroll):
    q_ref, k_ref, v_ref = refs
    teach, lw_s, ex_s, hid_s, state_s, g_s, a_hi_s, a_lo_s = scratch
    chunks, slab, width = q_ref.shape
    tokens = chunks * slab
    levels = slab.bit_length() - 1
    square = (slab, slab)
    t, m = row_ids(square), lane_ids(square)
    below = t > m
    after, before = zero_one(t < m), zero_one(below)
    gain = 2.0 / tokens

    def load(c):
        q, q_step = with_shift(q_ref, c)
        k0, k_step = with_shift(k_ref, c)
        v0, v_step = with_shift(v_ref, c)
        r = q + mix[0] * q_step
        k = k0 + mix[1] * k_step
        v = v0 + mix[2] * v_step
        lw, ex = lw_s[c], ex_s[c]
        total = ex[slab - 1 :] + lw[slab - 1 :]
        if fast:
            middle = ex[slab // 2 : slab // 2 + 1]
            r_factor = jnp.exp(ex - middle)
            k_factor = jnp.exp(middle - ex - lw)
            into, out = jnp.exp(middle), jnp.exp(total - middle)
        else:
            r_factor = jnp.exp(ex)
            k_factor = jnp.exp(exact_sums(after, lw))
            into = out = None
        return q, q_step, k_step, v_step, r, k, v, lw, total, r_factor, k_factor, into, out

    def scaled(x, by):
        return x if by is None else x * by

    def forward(c, state):
        _, _, _, _, r, k, v, lw, total, r_factor, k_factor, into, out = load(c)
        rs, ks, vs = split2(r * r_factor), split2(k * k_factor), split2(v)
        if fast:
            a = jnp.where(below, dot3(rs, ks, NT), 0.0)
        else:

            def one_level(level, a):
                _, _, r_part, k_part, block, _ = level_parts(level, lw, r, k)
                return a + jnp.where(block, dot3(r_part, k_part, NT), 0.0)

            a = lax.fori_loop(0, levels, one_level, jnp.zeros(square, f32))
        own = jnp.sum(r * bonus * k, axis=1, keepdims=True)
        a = split2(a)
        state_s[c] = state
        o = own * v + dot3(a, vs, NN) + dot3(rs, split2(scaled(state, into)), NT)
        o = o - jnp.mean(o, axis=1, keepdims=True)
        rate = lax.rsqrt(jnp.mean(o * o, axis=1, keepdims=True) + NORM_EPS)
        normed = o * rate
        g = gain * (normed - teach[c].astype(f32))
        g = g - jnp.mean(g, axis=1, keepdims=True) - normed * jnp.mean(
            g * normed, axis=1, keepdims=True
        )
        g_s[c] = g * rate
        a_hi_s[c] = a[0]
        a_lo_s[c] = a[1]
        return state * jnp.exp(total) + scaled(dot3(vs, ks, TN), out)

    def forward_some(i, state):
        for n in range(unroll):
            state = forward(i * unroll + n, state)
        return state

    state = lax.fori_loop(0, chunks // unroll, forward_some, jnp.zeros((width, width), f32))
    state_s[chunks] = state

    def backward(c, carry):
        cot, up_sum, down_sum, sums = carry
        q, q_step, k_step, v_step, r, k, v, lw, total, r_factor, k_factor, into, out = load(c)
        rs, ks, vs = split2(r * r_factor), split2(k * k_factor), split2(v)
        g = g_s[c]
        gs = split2(g)
        a = (a_hi_s[c], a_lo_s[c])
        pair = dot3(gs, vs, NT)
        cot_out = split2(scaled(cot, out))
        dr = r_factor * dot3(gs, split2(scaled(state_s[c], into)), NN)
        dk = k_factor * dot3(vs, cot_out, NN)
        dv = dot3(a, gs, TN) + dot3(ks, cot_out, NT)
        from_later, from_earlier = r * dr, k * dk
        dlw = jnp.sum(state_s[c] * jnp.exp(total) * cot, axis=0, keepdims=True)
        if fast:
            pairs = split2(jnp.where(below, pair, 0.0))
            dr_in, dk_in = dot4(pairs, ks, NN), dot4(pairs, rs, TN)
            k_in = joined(ks) * dk_in
            from_later = from_later + (joined(rs) * dr_in - k_in)
            dlw = dlw - k_in
            dr = dr + r_factor * dr_in
            dk = dk + k_factor * dk_in
        else:

            def one_level(level, parts):
                dr, dk, dlw = parts
                r_by, k_by, r_part, k_part, block, span = level_parts(level, lw, r, k)
                pairs = split2(jnp.where(block & below, pair, 0.0))
                dr_in = r_by * dot3(pairs, k_part, NN)
                dk_in = k_by * dot3(pairs, r_part, TN)
                inside = split3(r * dr_in + k * dk_in)
                return dr + dr_in, dk + dk_in, dlw + sum(dot(span, part, TN) for part in inside)

            dr, dk, dlw = lax.fori_loop(
                0, levels, one_level, (dr, dk, jnp.broadcast_to(dlw, r.shape))
            )
        dlw = dlw + exact_sums(after, from_later) + exact_sums(before, from_earlier)
        dv = dv + jnp.sum(r * bonus * k, axis=1, keepdims=True) * g
        own = jnp.sum(v * g, axis=1, keepdims=True)
        own_r, own_k = own * r, own * k
        dr = dr + bonus * own_k
        dk = dk + bonus * own_r
        dpre = dlw * lw
        hid = hid_s[c]
        dpres = split2(dpre)
        dz = dot3(dpres, up, NT) * (1.0 - hid * hid)
        dzs = split2(dz)
        dxw = dot3(dzs, down, NN)
        up_sum = up_sum + dot3(split2(hid), dpres, TN)
        down_sum = down_sum + dot3(dzs, split2(q + mix[3] * q_step), TN)
        parts = (dr * q_step, dk * k_step, dv * v_step, dxw * q_step, dpre, own_r * k)
        sums = tuple(
            old + jnp.sum(new.reshape(slab // 8, 8, width), axis=0)
            for old, new in zip(sums, parts)
        )
        cot = cot * jnp.exp(total) + scaled(dot3(gs, rs, TN), into)
        return cot, up_sum, down_sum, sums

    def backward_some(i, carry):
        for n in range(unroll):
            carry = backward(chunks - 1 - (i * unroll + n), carry)
        return carry

    rank = hid_s.shape[2]
    empty = jnp.zeros((rank, width), f32)
    start = (jnp.zeros((width, width), f32), empty, empty, (jnp.zeros((8, width), f32),) * 6)
    _, up_sum, down_sum, sums = lax.fori_loop(0, chunks // unroll, backward_some, start)
    tail = [split2(jnp.sum(part, axis=0, keepdims=True)) for part in sums]
    tail = [high.astype(f32) for high, _ in tail] + [low.astype(f32) for _, low in tail]
    tail.append(jnp.zeros((PACK_TAIL - len(tail), width), f32))
    return jnp.concatenate([up_sum, down_sum, *tail], axis=0)


def head_kernel(
    head_ref, qkv_ref, mix_ref, fade_ref, down_ref, up_ref, bonus_ref, out_ref, *scratch
):
    scores, teach, lw_s, ex_s, hid_s, *rest = scratch
    slabs = qkv_ref.shape[0]
    refs = tuple(qkv_ref.at[:, n] for n in range(3))
    head = head_ref[0] + pl.program_id(0)
    mix = [mix_ref[n, pl.ds(head, 1), :] for n in range(4)]
    bonus = bonus_ref[pl.ds(head, 1), :]
    down, up = split2(down_ref[...]), split2(up_ref[...])
    fade = fade_ref[pl.ds(head, 1), :]
    worst = decay_phase(refs[0], down, up, fade, mix, lw_s, ex_s, hid_s, math.gcd(4, slabs))
    teacher_phase(*refs, teach, scores, math.gcd(2, slabs), math.gcd(4, slabs))
    safe = jnp.max(worst) <= SAFE_EXPONENT
    held = (teach, lw_s, ex_s, hid_s, *rest)

    def finish(fast, unroll):
        grads = student_phase(fast, refs, mix, bonus, down, up, held, unroll).astype(bf16)

        def copy_out(n, _):
            out_ref[n] = grads
            return 0

        lax.fori_loop(0, out_ref.shape[0], copy_out, 0)

    @pl.when(safe)
    def _():
        finish(True, math.gcd(4, slabs))

    @pl.when(jnp.logical_not(safe))
    def _():
        finish(False, 1)


def head_grads(qkv, first_head, mix, fade, down_t, up, bonus):
    slabs, count, _, slab, width = qkv.shape
    rank = up.shape[1]
    packed_rows = 2 * rank + PACK_TAIL
    whole = lambda *_: (0, 0)
    own = lambda i, h: (h[0] + i, 0, 0)
    q_slabs, k_slabs = math.gcd(2, slabs), math.gcd(4, slabs)
    spec = pltpu.PrefetchScalarGridSpec(
        num_scalar_prefetch=1,
        grid=(count,),
        in_specs=[
            pl.BlockSpec((slabs, None, 3, slab, width), lambda i, h: (0, i, 0, 0, 0)),
            pl.BlockSpec(mix.shape, lambda i, h: (0, 0, 0)),
            pl.BlockSpec(fade.shape, whole),
            pl.BlockSpec((None, rank, width), own),
            pl.BlockSpec((None, rank, width), own),
            pl.BlockSpec(bonus.shape, whole),
        ],
        out_specs=pl.BlockSpec((slabs, None, packed_rows, width), lambda i, h: (0, i, 0, 0)),
        scratch_shapes=[
            pltpu.VMEM((slabs // k_slabs, q_slabs * slab, k_slabs * slab), f32),
            pltpu.VMEM((slabs, slab, width), bf16),
            pltpu.VMEM((slabs, slab, width), f32),
            pltpu.VMEM((slabs, slab, width), f32),
            pltpu.VMEM((slabs, slab, rank), f32),
            pltpu.VMEM((slabs + 1, width, width), f32),
            pltpu.VMEM((slabs, slab, width), f32),
            pltpu.VMEM((slabs, slab, slab), bf16),
            pltpu.VMEM((slabs, slab, slab), bf16),
        ],
    )
    return pl.pallas_call(
        head_kernel,
        out_shape=jax.ShapeDtypeStruct((slabs, count, packed_rows, width), bf16),
        grid_spec=spec,
        compiler_params=pltpu.CompilerParams(
            vmem_limit_bytes=58 * 1024 * 1024, dimension_semantics=("arbitrary",)
        ),
    )(first_head, qkv, mix, fade, down_t, up, bonus)


def pack_kernel(q_ref, k_ref, v_ref, out_ref):
    slots, _, _, width = out_ref.shape
    heads, groups = q_ref.shape[1] // width, k_ref.shape[1] // width
    for slot in range(slots):
        head = slot * heads // slots
        group = head * groups // heads
        for n, (ref, at) in enumerate(((q_ref, head), (k_ref, group), (v_ref, group))):
            out_ref[slot, n] = ref[:, at * width : (at + 1) * width]


def unpack_kernel(packed_ref, mix_ref, decay_ref, down_ref, up_ref, bonus_ref):
    heads, rank, _ = up_ref.shape
    copies = packed_ref.shape[0] // heads
    for head in range(heads):
        packed = packed_ref[head * copies].astype(f32)
        up_ref[head] = packed[:rank]
        down_ref[head] = packed[rank : 2 * rank]
        tail = packed[2 * rank :]
        tail = tail[:6] + tail[6:12]
        for n in range(4):
            mix_ref[n, head : head + 1, :] = tail[n : n + 1]
        decay_ref[head : head + 1, :] = tail[4:5]
        bonus_ref[head : head + 1, :] = tail[5:6]


def shards(
    probe_vectors,
    mentor_address_vectors,
    mentor_content_vectors,
    previous_position_blend,
    feature_fading_exponent,
    fading_narrowing_matrix,
    fading_widening_matrix,
    diagonal_extra_amount,
):
    slab = probe_vectors.shape[0]
    heads, width, rank = fading_narrowing_matrix.shape
    place = lax.axis_index("seq")
    count = lax.axis_size("seq")
    copies = max(1, count // heads)
    per_device = max(1, heads // count)
    assert heads * copies == per_device * count
    vmem = pl.BlockSpec(memory_space=pltpu.VMEM)
    slots = jax.ShapeDtypeStruct((heads * copies, 3, slab, width), bf16)
    qkv = pl.pallas_call(pack_kernel, out_shape=slots, in_specs=[vmem] * 3, out_specs=vmem)(
        probe_vectors, mentor_address_vectors, mentor_content_vectors
    )
    qkv = qkv.reshape(count, per_device, 3, slab, width)
    qkv = lax.all_to_all(qkv, "seq", split_axis=0, concat_axis=0, tiled=True)
    first_head = (place // copies) * per_device
    packed = head_grads(
        qkv,
        first_head.astype(jnp.int32).reshape(1),
        previous_position_blend,
        feature_fading_exponent,
        jnp.swapaxes(fading_narrowing_matrix, 1, 2),
        fading_widening_matrix,
        diagonal_extra_amount,
    )
    packed = lax.all_to_all(packed, "seq", split_axis=0, concat_axis=0, tiled=True)
    packed = packed.reshape(heads * copies, 2 * rank + PACK_TAIL, width)
    vector = jax.ShapeDtypeStruct((heads, width), f32)
    matrix = jax.ShapeDtypeStruct((heads, rank, width), f32)
    mix, decay, down_t, up, bonus = pl.pallas_call(
        unpack_kernel,
        out_shape=(
            jax.ShapeDtypeStruct((4, heads, width), f32),
            vector,
            matrix,
            matrix,
            vector,
        ),
        in_specs=[vmem],
        out_specs=[vmem] * 5,
    )(packed)
    return mix, decay, jnp.swapaxes(down_t, 1, 2), up, bonus


def solution(mesh):
    return jax.shard_map(
        shards,
        mesh=mesh,
        in_specs=(
            P("seq", "head"),
            P("seq", "head"),
            P("seq", "head"),
            P(None, "head", None),
            P("head", None),
            P("head", None, None),
            P("head", None, None),
            P("head", None),
        ),
        out_specs=(
            P(None, "head", None),
            P("head", None),
            P("head", None, None),
            P("head", None, None),
            P("head", None),
        ),
        check_vma=False,
    )
```

```python
import math

import jax
import jax.numpy as jnp
from jax import lax
from jax.experimental import pallas as pl
from jax.experimental.pallas import tpu as pltpu
from jax.sharding import PartitionSpec as P

NORM_EPS = 0.00064
NEG_LARGE = -1e30
SAFE_EXPONENT = 30.0
PACK_TAIL = 16
LOG2_E = math.log2(math.e)

f32 = jnp.float32
bf16 = jnp.bfloat16

NN = (((1,), (0,)), ((), ()))
NT = (((1,), (1,)), ((), ()))
TN = (((0,), (0,)), ((), ()))


def dot(a, b, dims):
    return lax.dot_general(a, b, dims, preferred_element_type=f32)


def split2(x):
    high = x.astype(bf16)
    return high, (x - high.astype(f32)).astype(bf16)


def split3(x):
    high = x.astype(bf16)
    rest = x - high.astype(f32)
    middle = rest.astype(bf16)
    return high, middle, (rest - middle.astype(f32)).astype(bf16)


def stacked(parts, contracted):
    return jnp.concatenate(parts, axis=contracted)


def dot3(a, b, dims):
    (at,), (bt,) = dims[0]
    return dot(stacked((a[0], a[1], a[0]), at), stacked((b[0], b[0], b[1]), bt), dims)


def dot4(a, b, dims):
    (at,), (bt,) = dims[0]
    return dot(stacked((*a, *a), at), stacked((b[0], b[0], b[1], b[1]), bt), dims)


def joined(parts):
    return parts[0].astype(f32) + parts[1].astype(f32)


def sums_of(zero_one, parts):
    return dot(stacked((zero_one,) * len(parts), 1), stacked(parts, 0), NN)


def row_ids(shape):
    return lax.broadcasted_iota(jnp.int32, shape, 0)


def lane_ids(shape):
    return lax.broadcasted_iota(jnp.int32, shape, 1)


def zero_one(condition):
    return jnp.where(condition, 1.0, 0.0).astype(bf16)


def with_shift(ref, first, slabs=1):
    _, rows, width = ref.shape
    now = ref[pl.ds(first, slabs)].astype(f32).reshape(slabs * rows, width)
    tail = ref[jnp.maximum(first - 1, 0), rows - 16 :, :].astype(f32)[15:16]
    tail = jnp.where(first > 0, tail, 0.0)
    earlier = jnp.where(row_ids(now.shape) == 0, tail, pltpu.roll(now, 1, 0))
    return now, earlier - now


def slabs_of(ref, first, slabs):
    _, rows, width = ref.shape
    return ref[pl.ds(first, slabs)].reshape(slabs * rows, width)


def teacher_phase(q_ref, k_ref, v_ref, teach, scores):
    slabs, slab, width = q_ref.shape
    _, q_rows, k_rows = scores.shape
    q_slabs, k_slabs = q_rows // slab, k_rows // slab
    scale = LOG2_E / math.sqrt(width)

    def q_block(i, _):
        q = slabs_of(q_ref, i * q_slabs, q_slabs)
        last = (i * q_slabs + q_slabs - 1) // k_slabs

        def score_block(j, top, edge=False):
            s = dot(q, slabs_of(k_ref, j * k_slabs, k_slabs), NT) * scale
            if edge:
                seen = i * q_rows + row_ids(s.shape) >= j * k_rows + lane_ids(s.shape)
                s = jnp.where(seen, s, NEG_LARGE)
            scores[j] = s
            for n in range(k_rows // 128):
                top = jnp.maximum(top, s[:, n * 128 : (n + 1) * 128])
            return top

        top = lax.fori_loop(0, last, score_block, jnp.full((q_rows, 128), NEG_LARGE, f32))
        top = score_block(last, top, True)
        row_top = jnp.max(top, axis=1, keepdims=True)

        def value_block(j, carry):
            total, accum = carry
            p = jnp.exp2(scores[j] - row_top)
            for n in range(k_rows // 128):
                total = total + p[:, n * 128 : (n + 1) * 128]
            return total, accum + dot(p.astype(bf16), slabs_of(v_ref, j * k_slabs, k_slabs), NN)

        total, accum = lax.fori_loop(
            0,
            last + 1,
            value_block,
            (jnp.zeros((q_rows, 128), f32), jnp.zeros((q_rows, width), f32)),
        )
        out = accum / jnp.sum(total, axis=1, keepdims=True)
        teach[pl.ds(i * q_slabs, q_slabs)] = out.astype(bf16).reshape(q_slabs, slab, width)
        return 0

    lax.fori_loop(0, slabs // q_slabs, q_block, 0)


def decay_phase(q_ref, down, up, fade, mix, lw_s, ex_s, hid_s, slabs):
    count, slab, width = q_ref.shape
    square = (slab, slab)
    before = zero_one(row_ids(square) > lane_ids(square))

    def block(i, worst):
        first = i * slabs
        q, q_step = with_shift(q_ref, first, slabs)
        hid = jnp.tanh(dot3(split2(q + mix[3] * q_step), down, NT))
        lw = -jnp.exp(fade + dot3(split2(hid), up, NN))
        hid_s[pl.ds(first, slabs)] = hid.reshape(slabs, slab, hid.shape[1])
        lw_s[pl.ds(first, slabs)] = lw.reshape(slabs, slab, width)
        for n in range(slabs):
            part = lw[n * slab : (n + 1) * slab]
            ex = sums_of(before, split3(part))
            ex_s[first + n] = ex
            middle = ex[slab // 2 : slab // 2 + 1]
            total = ex[slab - 1 :] + part[slab - 1 :]
            worst = jnp.maximum(worst, jnp.maximum(-middle, middle - total))
        return worst

    return lax.fori_loop(0, count // slabs, block, jnp.zeros((1, width), f32))


def level_parts(level, lw, r, k):
    square = (lw.shape[0], lw.shape[0])
    t, m = row_ids(square), lane_ids(square)
    edge = ((t >> (level + 1)) << (level + 1)) + (1 << level) - 1
    upper = ((t >> level) & 1) == 1
    lower = ((t >> level) & 1) == 0
    span = zero_one((upper & (m > edge) & (m < t)) | (lower & (m > t) & (m <= edge)))
    factor = jnp.exp(sums_of(span, split3(lw)))
    upper_rows = ((row_ids(r.shape) >> level) & 1) == 1
    r_factor = jnp.where(upper_rows, factor, 0.0)
    k_factor = jnp.where(upper_rows, 0.0, factor)
    same = (t >> (level + 1)) == (m >> (level + 1))
    return r_factor, k_factor, split2(r * r_factor), split2(k * k_factor), same, span


def halves(x):
    width = x.shape[1] // 2
    return x[:, :width], x[:, width:]


def student_phase(fast, refs, mix, bonus, down, up, scratch, unroll):
    q_ref, k_ref, v_ref = refs
    teach, lw_s, ex_s, hid_s, state_s, g_s, a_s, r_s, k_s, v_s = scratch
    chunks, slab, width = q_ref.shape
    tokens = chunks * slab
    levels = slab.bit_length() - 1
    square = (slab, slab)
    t, m = row_ids(square), lane_ids(square)
    below = t > m
    after, before = zero_one(t < m), zero_one(below)
    gain = 2.0 / tokens

    def load(c):
        q, q_step = with_shift(q_ref, c)
        k0, k_step = with_shift(k_ref, c)
        v0, v_step = with_shift(v_ref, c)
        r = q + mix[0] * q_step
        k = k0 + mix[1] * k_step
        v = v0 + mix[2] * v_step
        lw, ex = lw_s[c], ex_s[c]
        total = ex[slab - 1 :] + lw[slab - 1 :]
        if fast:
            middle = ex[slab // 2 : slab // 2 + 1]
            r_factor = jnp.exp(ex - middle)
            k_factor = jnp.exp(middle - ex - lw)
            into, out = jnp.exp(middle), jnp.exp(total - middle)
        else:
            r_factor = jnp.exp(ex)
            k_factor = jnp.exp(sums_of(after, split3(lw)))
            into = out = None
        return q, q_step, k_step, v_step, r, k, v, lw, total, r_factor, k_factor, into, out

    def scaled(x, by):
        return x if by is None else x * by

    def forward(c, state):
        _, _, _, _, r, k, v, lw, total, r_factor, k_factor, into, out = load(c)
        rs, ks, vs = split2(r * r_factor), split2(k * k_factor), split2(v)
        if fast:
            a = jnp.where(below, dot3(rs, ks, NT), 0.0)
        else:

            def one_level(level, a):
                _, _, r_part, k_part, block, _ = level_parts(level, lw, r, k)
                return a + jnp.where(block, dot3(r_part, k_part, NT), 0.0)

            a = lax.fori_loop(0, levels, one_level, jnp.zeros(square, f32))
        own = jnp.sum(r * bonus * k, axis=1, keepdims=True)
        a = split2(a)
        state_s[c] = state
        o = own * v + dot3(a, vs, NN) + dot3(rs, split2(scaled(state, into)), NT)
        o = o - jnp.mean(o, axis=1, keepdims=True)
        rate = lax.rsqrt(jnp.mean(o * o, axis=1, keepdims=True) + NORM_EPS)
        normed = o * rate
        g = gain * (normed - teach[c].astype(f32))
        g = g - jnp.mean(g, axis=1, keepdims=True) - normed * jnp.mean(
            g * normed, axis=1, keepdims=True
        )
        g_s[c] = g * rate
        for held, parts in ((a_s, a), (r_s, rs), (k_s, ks), (v_s, vs)):
            held[c] = jnp.concatenate(parts, axis=1)
        return state * jnp.exp(total) + scaled(dot3(vs, ks, TN), out)

    def forward_some(i, state):
        for n in range(unroll):
            state = forward(i * unroll + n, state)
        return state

    lax.fori_loop(0, chunks // unroll, forward_some, jnp.zeros((width, width), f32))

    def backward(c, carry):
        cot, up_sum, down_sum, sums = carry
        q, q_step, k_step, v_step, r, k, v, lw, total, r_factor, k_factor, into, out = load(c)
        a, rs, ks, vs = (halves(held[c]) for held in (a_s, r_s, k_s, v_s))
        g = g_s[c]
        gs = split2(g)
        pair = dot3(gs, vs, NT)
        cot_out = split2(scaled(cot, out))
        state_in = split2(scaled(state_s[c], into))
        k_hat = joined(ks)
        dv = dot3(a, gs, TN) + dot3(ks, cot_out, NT)
        dk = dot3(vs, cot_out, NN)
        from_earlier = k_hat * dk
        dlw = jnp.sum(state_s[c] * jnp.exp(total) * cot, axis=0, keepdims=True)
        if fast:
            pairs = split2(jnp.where(below, pair, 0.0))
            dr = dot(
                stacked((gs[0], gs[1], pairs[0], pairs[1], gs[0], pairs[0], pairs[1]), 1),
                stacked((state_in[0], state_in[0], ks[0], ks[0], state_in[1], ks[1], ks[1]), 0),
                NN,
            )
            dk_in = dot4(pairs, rs, TN)
            k_in = k_hat * dk_in
            from_later = joined(rs) * dr - k_in
            dlw = dlw - k_in
            dr = r_factor * dr
            dk = k_factor * (dk + dk_in)
        else:
            dr = dot3(gs, state_in, NN)
            from_later = joined(rs) * dr
            dr = r_factor * dr
            dk = k_factor * dk

            def one_level(level, parts):
                dr, dk, dlw = parts
                r_by, k_by, r_part, k_part, block, span = level_parts(level, lw, r, k)
                pairs = split2(jnp.where(block & below, pair, 0.0))
                dr_in = r_by * dot3(pairs, k_part, NN)
                dk_in = k_by * dot3(pairs, r_part, TN)
                inside = split3(r * dr_in + k * dk_in)
                return dr + dr_in, dk + dk_in, dlw + sum(dot(span, part, TN) for part in inside)

            dr, dk, dlw = lax.fori_loop(
                0, levels, one_level, (dr, dk, jnp.broadcast_to(dlw, r.shape))
            )
        both = tuple(
            jnp.concatenate(pair, axis=0) for pair in zip(split3(from_later), split3(from_earlier))
        )
        dlw = dlw + sums_of(jnp.concatenate([after, before], axis=1), both)
        dv = dv + jnp.sum(r * bonus * k, axis=1, keepdims=True) * g
        own = jnp.sum(v * g, axis=1, keepdims=True)
        own_r, own_k = own * r, own * k
        dr = dr + bonus * own_k
        dk = dk + bonus * own_r
        dpre = dlw * lw
        hid = hid_s[c]
        dpres = split2(dpre)
        dz = dot3(dpres, up, NT) * (1.0 - hid * hid)
        dzs = split2(dz)
        dxw = dot3(dzs, down, NN)
        up_sum = up_sum + dot3(split2(hid), dpres, TN)
        down_sum = down_sum + dot3(dzs, split2(q + mix[3] * q_step), TN)
        parts = (dr * q_step, dk * k_step, dv * v_step, dxw * q_step, dpre, own_r * k)
        sums = tuple(
            old + jnp.sum(new.reshape(slab // 8, 8, width), axis=0)
            for old, new in zip(sums, parts)
        )
        cot = cot * jnp.exp(total) + scaled(dot3(gs, rs, TN), into)
        return cot, up_sum, down_sum, sums

    def backward_some(i, carry):
        for n in range(unroll):
            carry = backward(chunks - 1 - (i * unroll + n), carry)
        return carry

    rank = down[0].shape[0]
    empty = jnp.zeros((rank, width), f32)
    start = (jnp.zeros((width, width), f32), empty, empty, (jnp.zeros((8, width), f32),) * 6)
    _, up_sum, down_sum, sums = lax.fori_loop(0, chunks // unroll, backward_some, start)
    tail = [split2(jnp.sum(part, axis=0, keepdims=True)) for part in sums]
    tail = [high.astype(f32) for high, _ in tail] + [low.astype(f32) for _, low in tail]
    tail.append(jnp.zeros((PACK_TAIL - len(tail), width), f32))
    return jnp.concatenate([up_sum, down_sum, *tail], axis=0)


def head_kernel(
    head_ref, qkv_ref, mix_ref, fade_ref, down_ref, up_ref, bonus_ref, out_ref, *scratch
):
    scores, *held = scratch
    slabs, per_device = qkv_ref.shape[:2]
    rank = up_ref.shape[1]
    for at in range(per_device):
        refs = tuple(qkv_ref.at[:, at, n] for n in range(3))
        head = head_ref[0] + at
        mix = [mix_ref[n, pl.ds(head, 1), :] for n in range(4)]
        bonus = bonus_ref[pl.ds(head, 1), :]
        fade = fade_ref[pl.ds(head, 1), :]
        down, up = split2(down_ref[head]), split2(up_ref[head])
        worst = decay_phase(refs[0], down, up, fade, mix, *held[1:4], math.gcd(4, slabs))
        teacher_phase(*refs, held[0], scores)
        safe = jnp.max(worst) <= SAFE_EXPONENT

        def finish(fast, unroll):
            grads = student_phase(fast, refs, mix, bonus, down, up, held, unroll).astype(bf16)

            def copy_out(n, _):
                out_ref[n, at] = grads
                return 0

            lax.fori_loop(0, slabs, copy_out, 0)

        @pl.when(safe)
        def _():
            finish(True, math.gcd(4, slabs))

        @pl.when(jnp.logical_not(safe))
        def _():
            finish(False, 1)


def head_grads(qkv, first_head, mix, fade, down_t, up, bonus):
    slabs, per_device, _, slab, width = qkv.shape
    rank = up.shape[1]
    packed_rows = 2 * rank + PACK_TAIL
    k_slabs = math.gcd(4, slabs)
    q_slabs = k_slabs if slabs <= 16 else 1
    vmem = pl.BlockSpec(memory_space=pltpu.VMEM)
    return pl.pallas_call(
        head_kernel,
        out_shape=jax.ShapeDtypeStruct((slabs, per_device, packed_rows, width), bf16),
        in_specs=[pl.BlockSpec(memory_space=pltpu.SMEM)] + [vmem] * 6,
        out_specs=vmem,
        scratch_shapes=[
            pltpu.VMEM((slabs // k_slabs, q_slabs * slab, k_slabs * slab), f32),
            pltpu.VMEM((slabs, slab, width), bf16),
            pltpu.VMEM((slabs, slab, width), f32),
            pltpu.VMEM((slabs, slab, width), f32),
            pltpu.VMEM((slabs, slab, rank), f32),
            pltpu.VMEM((slabs, width, width), f32),
            pltpu.VMEM((slabs, slab, width), f32),
            pltpu.VMEM((slabs, slab, 2 * slab), bf16),
            pltpu.VMEM((slabs, slab, 2 * width), bf16),
            pltpu.VMEM((slabs, slab, 2 * width), bf16),
            pltpu.VMEM((slabs, slab, 2 * width), bf16),
        ],
        compiler_params=pltpu.CompilerParams(
            vmem_limit_bytes=(36 if slabs <= 16 else 60) * 1024 * 1024
        ),
    )(first_head, qkv, mix, fade, down_t, up, bonus)


def pack_kernel(q_ref, k_ref, v_ref, out_ref):
    slots, _, _, width = out_ref.shape
    heads, groups = q_ref.shape[1] // width, k_ref.shape[1] // width
    for slot in range(slots):
        head = slot * heads // slots
        group = head * groups // heads
        for n, (ref, at) in enumerate(((q_ref, head), (k_ref, group), (v_ref, group))):
            out_ref[slot, n] = ref[:, at * width : (at + 1) * width]


def unpack_kernel(packed_ref, mix_ref, decay_ref, down_ref, up_ref, bonus_ref):
    heads, rank, _ = up_ref.shape
    copies = packed_ref.shape[0] // heads
    for head in range(heads):
        packed = packed_ref[head * copies].astype(f32)
        up_ref[head] = packed[:rank]
        down_ref[head] = packed[rank : 2 * rank]
        tail = packed[2 * rank :]
        tail = tail[:6] + tail[6:12]
        for n in range(4):
            mix_ref[n, head : head + 1, :] = tail[n : n + 1]
        decay_ref[head : head + 1, :] = tail[4:5]
        bonus_ref[head : head + 1, :] = tail[5:6]


def shards(
    probe_vectors,
    mentor_address_vectors,
    mentor_content_vectors,
    previous_position_blend,
    feature_fading_exponent,
    fading_narrowing_matrix,
    fading_widening_matrix,
    diagonal_extra_amount,
):
    slab = probe_vectors.shape[0]
    heads, width, rank = fading_narrowing_matrix.shape
    place = lax.axis_index("seq")
    count = lax.axis_size("seq")
    copies = max(1, count // heads)
    per_device = max(1, heads // count)
    assert heads * copies == per_device * count
    vmem = pl.BlockSpec(memory_space=pltpu.VMEM)
    slots = jax.ShapeDtypeStruct((heads * copies, 3, slab, width), bf16)
    qkv = pl.pallas_call(pack_kernel, out_shape=slots, in_specs=[vmem] * 3, out_specs=vmem)(
        probe_vectors, mentor_address_vectors, mentor_content_vectors
    )
    qkv = qkv.reshape(count, per_device, 3, slab, width)
    qkv = lax.all_to_all(qkv, "seq", split_axis=0, concat_axis=0, tiled=True)
    first_head = (place // copies) * per_device
    packed = head_grads(
        qkv,
        first_head.astype(jnp.int32).reshape(1),
        previous_position_blend,
        feature_fading_exponent,
        jnp.swapaxes(fading_narrowing_matrix, 1, 2),
        fading_widening_matrix,
        diagonal_extra_amount,
    )
    packed = lax.all_to_all(packed, "seq", split_axis=0, concat_axis=0, tiled=True)
    packed = packed.reshape(heads * copies, 2 * rank + PACK_TAIL, width)
    vector = jax.ShapeDtypeStruct((heads, width), f32)
    matrix = jax.ShapeDtypeStruct((heads, rank, width), f32)
    mix, decay, down_t, up, bonus = pl.pallas_call(
        unpack_kernel,
        out_shape=(
            jax.ShapeDtypeStruct((4, heads, width), f32),
            vector,
            matrix,
            matrix,
            vector,
        ),
        in_specs=[vmem],
        out_specs=[vmem] * 5,
    )(packed)
    return mix, decay, jnp.swapaxes(down_t, 1, 2), up, bonus


def solution(mesh):
    return jax.shard_map(
        shards,
        mesh=mesh,
        in_specs=(
            P("seq", "head"),
            P("seq", "head"),
            P("seq", "head"),
            P(None, "head", None),
            P("head", None),
            P("head", None, None),
            P("head", None, None),
            P("head", None),
        ),
        out_specs=(
            P(None, "head", None),
            P("head", None),
            P("head", None, None),
            P("head", None, None),
            P("head", None),
        ),
        check_vma=False,
    )
```

```python
import math

import jax
import jax.numpy as jnp
from jax import lax
from jax.experimental import pallas as pl
from jax.experimental.pallas import tpu as pltpu
from jax.sharding import PartitionSpec as P

NORM_EPS = 0.00064
NEG_LARGE = -1e30
SAFE_EXPONENT = 30.0
PACK_TAIL = 16
LOG2_E = math.log2(math.e)

f32 = jnp.float32
bf16 = jnp.bfloat16

NN = (((1,), (0,)), ((), ()))
NT = (((1,), (1,)), ((), ()))
TN = (((0,), (0,)), ((), ()))


def dot(a, b, dims):
    return lax.dot_general(a, b, dims, preferred_element_type=f32)


def split2(x):
    high = x.astype(bf16)
    return high, (x - high.astype(f32)).astype(bf16)


def split3(x):
    high = x.astype(bf16)
    rest = x - high.astype(f32)
    middle = rest.astype(bf16)
    return high, middle, (rest - middle.astype(f32)).astype(bf16)


def stacked(parts, contracted):
    return jnp.concatenate(parts, axis=contracted)


def dot3(a, b, dims):
    (at,), (bt,) = dims[0]
    return dot(stacked((a[0], a[1], a[0]), at), stacked((b[0], b[0], b[1]), bt), dims)


def dot4(a, b, dims):
    (at,), (bt,) = dims[0]
    return dot(stacked((*a, *a), at), stacked((b[0], b[0], b[1], b[1]), bt), dims)


def joined(parts):
    return parts[0].astype(f32) + parts[1].astype(f32)


def sums_of(zero_one, parts):
    return dot(stacked((zero_one,) * len(parts), 1), stacked(parts, 0), NN)


def row_ids(shape):
    return lax.broadcasted_iota(jnp.int32, shape, 0)


def lane_ids(shape):
    return lax.broadcasted_iota(jnp.int32, shape, 1)


def zero_one(condition):
    return jnp.where(condition, 1.0, 0.0).astype(bf16)


def with_shift(at, first, slabs=1):
    now = slabs_of(at, first, slabs).astype(f32)
    last = at(jnp.maximum(first - 1, 0))
    tail = last[last.shape[0] - 16 :].astype(f32)[15:16]
    tail = jnp.where(first > 0, tail, 0.0)
    earlier = jnp.where(row_ids(now.shape) == 0, tail, pltpu.roll(now, 1, 0))
    return now, earlier - now


def slabs_of(at, first, slabs):
    return jnp.concatenate([at(first + n) for n in range(slabs)], axis=0)


def teacher_phase(q_at, k_at, v_at, teach, scores):
    slabs, slab, width = teach.shape
    _, q_rows, k_rows = scores.shape
    q_slabs, k_slabs = q_rows // slab, k_rows // slab
    scale = LOG2_E / math.sqrt(width)

    def q_block(i, _):
        q = slabs_of(q_at, i * q_slabs, q_slabs)
        last = (i * q_slabs + q_slabs - 1) // k_slabs

        def score_block(j, top, edge=False):
            s = dot(q, slabs_of(k_at, j * k_slabs, k_slabs), NT) * scale
            if edge:
                seen = i * q_rows + row_ids(s.shape) >= j * k_rows + lane_ids(s.shape)
                s = jnp.where(seen, s, NEG_LARGE)
            scores[j] = s
            for n in range(k_rows // 128):
                top = jnp.maximum(top, s[:, n * 128 : (n + 1) * 128])
            return top

        top = lax.fori_loop(0, last, score_block, jnp.full((q_rows, 128), NEG_LARGE, f32))
        top = score_block(last, top, True)
        row_top = jnp.max(top, axis=1, keepdims=True)

        def value_block(j, carry):
            total, accum = carry
            p = jnp.exp2(scores[j] - row_top)
            for n in range(k_rows // 128):
                total = total + p[:, n * 128 : (n + 1) * 128]
            return total, accum + dot(p.astype(bf16), slabs_of(v_at, j * k_slabs, k_slabs), NN)

        total, accum = lax.fori_loop(
            0,
            last + 1,
            value_block,
            (jnp.zeros((q_rows, 128), f32), jnp.zeros((q_rows, width), f32)),
        )
        out = accum / jnp.sum(total, axis=1, keepdims=True)
        teach[pl.ds(i * q_slabs, q_slabs)] = out.astype(bf16).reshape(q_slabs, slab, width)
        return 0

    lax.fori_loop(0, slabs // q_slabs, q_block, 0)


def decay_phase(q_at, down, up, fade, mix, lw_s, ex_s, hid_s, slabs):
    count, slab, width = lw_s.shape
    square = (slab, slab)
    before = zero_one(row_ids(square) > lane_ids(square))

    def block(i, worst):
        first = i * slabs
        q, q_step = with_shift(q_at, first, slabs)
        hid = jnp.tanh(dot3(split2(q + mix[3] * q_step), down, NT))
        lw = -jnp.exp(fade + dot3(split2(hid), up, NN))
        hid_s[pl.ds(first, slabs)] = hid.reshape(slabs, slab, hid.shape[1])
        lw_s[pl.ds(first, slabs)] = lw.reshape(slabs, slab, width)
        for n in range(slabs):
            part = lw[n * slab : (n + 1) * slab]
            ex = sums_of(before, split3(part))
            ex_s[first + n] = ex
            middle = ex[slab // 2 : slab // 2 + 1]
            total = ex[slab - 1 :] + part[slab - 1 :]
            worst = jnp.maximum(worst, jnp.maximum(-middle, middle - total))
        return worst

    return lax.fori_loop(0, count // slabs, block, jnp.zeros((1, width), f32))


def level_parts(level, lw, r, k):
    square = (lw.shape[0], lw.shape[0])
    t, m = row_ids(square), lane_ids(square)
    edge = ((t >> (level + 1)) << (level + 1)) + (1 << level) - 1
    upper = ((t >> level) & 1) == 1
    lower = ((t >> level) & 1) == 0
    span = zero_one((upper & (m > edge) & (m < t)) | (lower & (m > t) & (m <= edge)))
    factor = jnp.exp(sums_of(span, split3(lw)))
    upper_rows = ((row_ids(r.shape) >> level) & 1) == 1
    r_factor = jnp.where(upper_rows, factor, 0.0)
    k_factor = jnp.where(upper_rows, 0.0, factor)
    same = (t >> (level + 1)) == (m >> (level + 1))
    return r_factor, k_factor, split2(r * r_factor), split2(k * k_factor), same, span


def halves(x):
    width = x.shape[1] // 2
    return x[:, :width], x[:, width:]


def student_phase(fast, refs, mix, bonus, down, up, scratch, unroll):
    q_at, k_at, v_at = refs
    teach, lw_s, ex_s, hid_s, state_s, g_s, a_s, r_s, k_s, v_s = scratch
    chunks, slab, width = lw_s.shape
    tokens = chunks * slab
    levels = slab.bit_length() - 1
    square = (slab, slab)
    t, m = row_ids(square), lane_ids(square)
    below = t > m
    after, before = zero_one(t < m), zero_one(below)
    gain = 2.0 / tokens

    def load(c):
        q, q_step = with_shift(q_at, c)
        k0, k_step = with_shift(k_at, c)
        v0, v_step = with_shift(v_at, c)
        r = q + mix[0] * q_step
        k = k0 + mix[1] * k_step
        v = v0 + mix[2] * v_step
        lw, ex = lw_s[c], ex_s[c]
        total = ex[slab - 1 :] + lw[slab - 1 :]
        if fast:
            middle = ex[slab // 2 : slab // 2 + 1]
            r_factor = jnp.exp(ex - middle)
            k_factor = jnp.exp(middle - ex - lw)
            into, out = jnp.exp(middle), jnp.exp(total - middle)
        else:
            r_factor = jnp.exp(ex)
            k_factor = jnp.exp(sums_of(after, split3(lw)))
            into = out = None
        return q, q_step, k_step, v_step, r, k, v, lw, total, r_factor, k_factor, into, out

    def scaled(x, by):
        return x if by is None else x * by

    def forward(c, state):
        _, _, _, _, r, k, v, lw, total, r_factor, k_factor, into, out = load(c)
        rs, ks, vs = split2(r * r_factor), split2(k * k_factor), split2(v)
        if fast:
            a = jnp.where(below, dot3(rs, ks, NT), 0.0)
        else:

            def one_level(level, a):
                _, _, r_part, k_part, block, _ = level_parts(level, lw, r, k)
                return a + jnp.where(block, dot3(r_part, k_part, NT), 0.0)

            a = lax.fori_loop(0, levels, one_level, jnp.zeros(square, f32))
        own = jnp.sum(r * bonus * k, axis=1, keepdims=True)
        a = split2(a)
        state_s[c] = state
        o = own * v + dot3(a, vs, NN) + dot3(rs, split2(scaled(state, into)), NT)
        o = o - jnp.mean(o, axis=1, keepdims=True)
        rate = lax.rsqrt(jnp.mean(o * o, axis=1, keepdims=True) + NORM_EPS)
        normed = o * rate
        g = gain * (normed - teach[c].astype(f32))
        g = g - jnp.mean(g, axis=1, keepdims=True) - normed * jnp.mean(
            g * normed, axis=1, keepdims=True
        )
        g_s[c] = g * rate
        for held, parts in ((a_s, a), (r_s, rs), (k_s, ks), (v_s, vs)):
            held[c] = jnp.concatenate(parts, axis=1)
        return state * jnp.exp(total) + scaled(dot3(vs, ks, TN), out)

    def forward_some(i, state):
        for n in range(unroll):
            state = forward(i * unroll + n, state)
        return state

    lax.fori_loop(0, chunks // unroll, forward_some, jnp.zeros((width, width), f32))

    def backward(c, carry):
        cot, up_sum, down_sum, sums = carry
        q, q_step, k_step, v_step, r, k, v, lw, total, r_factor, k_factor, into, out = load(c)
        a, rs, ks, vs = (halves(held[c]) for held in (a_s, r_s, k_s, v_s))
        g = g_s[c]
        gs = split2(g)
        pair = dot3(gs, vs, NT)
        cot_out = split2(scaled(cot, out))
        state_in = split2(scaled(state_s[c], into))
        k_hat = joined(ks)
        dv = dot3(a, gs, TN) + dot3(ks, cot_out, NT)
        dk = dot3(vs, cot_out, NN)
        from_earlier = k_hat * dk
        dlw = jnp.sum(state_s[c] * jnp.exp(total) * cot, axis=0, keepdims=True)
        if fast:
            pairs = split2(jnp.where(below, pair, 0.0))
            dr = dot(
                stacked((gs[0], gs[1], pairs[0], pairs[1], gs[0], pairs[0], pairs[1]), 1),
                stacked((state_in[0], state_in[0], ks[0], ks[0], state_in[1], ks[1], ks[1]), 0),
                NN,
            )
            dk_in = dot4(pairs, rs, TN)
            k_in = k_hat * dk_in
            from_later = joined(rs) * dr - k_in
            dlw = dlw - k_in
            dr = r_factor * dr
            dk = k_factor * (dk + dk_in)
        else:
            dr = dot3(gs, state_in, NN)
            from_later = joined(rs) * dr
            dr = r_factor * dr
            dk = k_factor * dk

            def one_level(level, parts):
                dr, dk, dlw = parts
                r_by, k_by, r_part, k_part, block, span = level_parts(level, lw, r, k)
                pairs = split2(jnp.where(block & below, pair, 0.0))
                dr_in = r_by * dot3(pairs, k_part, NN)
                dk_in = k_by * dot3(pairs, r_part, TN)
                inside = split3(r * dr_in + k * dk_in)
                return dr + dr_in, dk + dk_in, dlw + sum(dot(span, part, TN) for part in inside)

            dr, dk, dlw = lax.fori_loop(
                0, levels, one_level, (dr, dk, jnp.broadcast_to(dlw, r.shape))
            )
        both = tuple(
            jnp.concatenate(pair, axis=0) for pair in zip(split3(from_later), split3(from_earlier))
        )
        dlw = dlw + sums_of(jnp.concatenate([after, before], axis=1), both)
        dv = dv + jnp.sum(r * bonus * k, axis=1, keepdims=True) * g
        own = jnp.sum(v * g, axis=1, keepdims=True)
        own_r, own_k = own * r, own * k
        dr = dr + bonus * own_k
        dk = dk + bonus * own_r
        dpre = dlw * lw
        hid = hid_s[c]
        dpres = split2(dpre)
        dz = dot3(dpres, up, NT) * (1.0 - hid * hid)
        dzs = split2(dz)
        dxw = dot3(dzs, down, NN)
        up_sum = up_sum + dot3(split2(hid), dpres, TN)
        down_sum = down_sum + dot3(dzs, split2(q + mix[3] * q_step), TN)
        parts = (dr * q_step, dk * k_step, dv * v_step, dxw * q_step, dpre, own_r * k)
        sums = tuple(
            old + jnp.sum(new.reshape(slab // 8, 8, width), axis=0)
            for old, new in zip(sums, parts)
        )
        cot = cot * jnp.exp(total) + scaled(dot3(gs, rs, TN), into)
        return cot, up_sum, down_sum, sums

    def backward_some(i, carry):
        for n in range(unroll):
            carry = backward(chunks - 1 - (i * unroll + n), carry)
        return carry

    rank = down[0].shape[0]
    empty = jnp.zeros((rank, width), f32)
    start = (jnp.zeros((width, width), f32), empty, empty, (jnp.zeros((8, width), f32),) * 6)
    _, up_sum, down_sum, sums = lax.fori_loop(0, chunks // unroll, backward_some, start)
    tail = [split2(jnp.sum(part, axis=0, keepdims=True)) for part in sums]
    tail = [high.astype(f32) for high, _ in tail] + [low.astype(f32) for _, low in tail]
    tail.append(jnp.zeros((PACK_TAIL - len(tail), width), f32))
    return jnp.concatenate([up_sum, down_sum, *tail], axis=0)


def settings_of(head, mix_ref, bonus_ref=None):
    mix = [mix_ref[n, pl.ds(head, 1), :] for n in range(4)]
    return mix if bonus_ref is None else (mix, bonus_ref[pl.ds(head, 1), :])


def decay_kernel(
    head_ref, q_ref, mix_ref, fade_ref, down_ref, up_ref, lw_ref, ex_ref, hid_ref, worst_ref
):
    slabs, per_device = q_ref.shape[:2]
    for n in range(per_device):
        head = head_ref[0] + n
        worst_ref[n] = decay_phase(
            lambda c, n=n: q_ref[c, n],
            split2(down_ref[head]),
            split2(up_ref[head]),
            fade_ref[pl.ds(head, 1), :],
            settings_of(head, mix_ref),
            lw_ref.at[n],
            ex_ref.at[n],
            hid_ref.at[n],
            math.gcd(4, slabs),
        )


def head_kernel(
    head_ref, q_ref, kv_ref, lw_ref, ex_ref, hid_ref, worst_ref, mix_ref, down_ref, up_ref,
    bonus_ref, out_ref, scores, teach, *held
):
    slabs, per_device = q_ref.shape[:2]
    near, _, shared = kv_ref.shape[:3]
    for n in range(per_device):
        head = head_ref[0] + n
        mix, bonus = settings_of(head, mix_ref, bonus_ref)
        down, up = split2(down_ref[head]), split2(up_ref[head])
        group = n * shared // per_device
        refs = (
            lambda c, n=n: q_ref[c, n],
            lambda c, group=group: kv_ref[lax.rem(c, near), c // near, group, 0],
            lambda c, group=group: kv_ref[lax.rem(c, near), c // near, group, 1],
        )
        teacher_phase(*refs, teach, scores)
        safe = jnp.max(worst_ref[n]) <= SAFE_EXPONENT
        scratch = (teach, lw_ref.at[n], ex_ref.at[n], hid_ref.at[n], *held)

        def finish(fast, unroll):
            grads = student_phase(fast, refs, mix, bonus, down, up, scratch, unroll).astype(bf16)

            def copy_out(at, _):
                out_ref[at, n] = grads
                return 0

            lax.fori_loop(0, slabs, copy_out, 0)

        @pl.when(safe)
        def _():
            finish(True, math.gcd(4, slabs))

        @pl.when(jnp.logical_not(safe))
        def _():
            finish(False, 1)


def head_decays(q, first_head, mix, fade, down_t, up):
    slabs, per_device, slab, width = q.shape
    rank = up.shape[1]
    vmem = pl.BlockSpec(memory_space=pltpu.VMEM)
    wide = jax.ShapeDtypeStruct((per_device, slabs, slab, width), f32)
    narrow = jax.ShapeDtypeStruct((per_device, slabs, slab, rank), f32)
    return pl.pallas_call(
        decay_kernel,
        out_shape=(wide, wide, narrow, jax.ShapeDtypeStruct((per_device, 1, width), f32)),
        in_specs=[pl.BlockSpec(memory_space=pltpu.SMEM)] + [vmem] * 5,
        out_specs=[vmem] * 4,
        cost_estimate=pl.CostEstimate(
            flops=12 * slabs * slab * width * width,
            bytes_accessed=16 * slabs * slab * width,
            transcendentals=2 * slabs * slab * width,
        ),
        compiler_params=pltpu.CompilerParams(
            vmem_limit_bytes=(12 if slabs <= 16 else 32) * 1024 * 1024
        ),
    )(first_head, q, mix, fade, down_t, up)


def head_grads(q, kv, decays, first_head, mix, down_t, up, bonus):
    slabs, per_device, slab, width = q.shape
    rank = up.shape[1]
    packed_rows = 2 * rank + PACK_TAIL
    k_slabs = math.gcd(4, slabs)
    q_slabs = k_slabs if slabs <= 16 else 1
    vmem = pl.BlockSpec(memory_space=pltpu.VMEM)
    return pl.pallas_call(
        head_kernel,
        out_shape=jax.ShapeDtypeStruct((slabs, per_device, packed_rows, width), bf16),
        in_specs=[pl.BlockSpec(memory_space=pltpu.SMEM)] + [vmem] * 10,
        out_specs=vmem,
        scratch_shapes=[
            pltpu.VMEM((slabs // k_slabs, q_slabs * slab, k_slabs * slab), f32),
            pltpu.VMEM((slabs, slab, width), bf16),
            pltpu.VMEM((slabs, width, width), f32),
            pltpu.VMEM((slabs, slab, width), f32),
            pltpu.VMEM((slabs, slab, 2 * slab), bf16),
            pltpu.VMEM((slabs, slab, 2 * width), bf16),
            pltpu.VMEM((slabs, slab, 2 * width), bf16),
            pltpu.VMEM((slabs, slab, 2 * width), bf16),
        ],
        compiler_params=pltpu.CompilerParams(
            vmem_limit_bytes=(36 if slabs <= 16 else 60) * 1024 * 1024
        ),
    )(first_head, q, kv, *decays, mix, down_t, up, bonus)


def pack_queries(q_ref, out_ref):
    slots, _, width = out_ref.shape
    heads = q_ref.shape[1] // width
    for slot in range(slots):
        head = slot * heads // slots
        out_ref[slot] = q_ref[:, head * width : (head + 1) * width]


def pack_memory(k_ref, v_ref, out_ref):
    groups, _, _, width = out_ref.shape
    for group in range(groups):
        out_ref[group, 0] = k_ref[:, group * width : (group + 1) * width]
        out_ref[group, 1] = v_ref[:, group * width : (group + 1) * width]


def to_group_holders(packed, count):
    groups, _, slab, width = packed.shape
    far = math.gcd(groups, count)
    near = count // far
    shared = groups // far
    packed = packed.reshape(far, shared, 2, slab, width)
    if far > 1:
        lines = [[p + near * z for z in range(far)] for p in range(near)]
        packed = lax.all_to_all(
            packed, "seq", split_axis=0, concat_axis=0, tiled=True, axis_index_groups=lines
        )
    if near > 1:
        planes = [[p + near * z for p in range(near)] for z in range(far)]
        packed = jnp.broadcast_to(packed[None], (near, *packed.shape))
        packed = lax.all_to_all(
            packed, "seq", split_axis=0, concat_axis=0, tiled=True, axis_index_groups=planes
        )
    else:
        packed = packed[None]
    return packed


def unpack_kernel(packed_ref, mix_ref, decay_ref, down_ref, up_ref, bonus_ref):
    heads, rank, _ = up_ref.shape
    copies = packed_ref.shape[0] // heads
    for head in range(heads):
        packed = packed_ref[head * copies].astype(f32)
        up_ref[head] = packed[:rank]
        down_ref[head] = packed[rank : 2 * rank]
        tail = packed[2 * rank :]
        tail = tail[:6] + tail[6:12]
        for n in range(4):
            mix_ref[n, head : head + 1, :] = tail[n : n + 1]
        decay_ref[head : head + 1, :] = tail[4:5]
        bonus_ref[head : head + 1, :] = tail[5:6]


def shards(
    probe_vectors,
    mentor_address_vectors,
    mentor_content_vectors,
    previous_position_blend,
    feature_fading_exponent,
    fading_narrowing_matrix,
    fading_widening_matrix,
    diagonal_extra_amount,
):
    slab = probe_vectors.shape[0]
    heads, width, rank = fading_narrowing_matrix.shape
    place = lax.axis_index("seq")
    count = lax.axis_size("seq")
    copies = max(1, count // heads)
    per_device = max(1, heads // count)
    assert heads * copies == per_device * count
    groups = mentor_address_vectors.shape[1] // width
    vmem = pl.BlockSpec(memory_space=pltpu.VMEM)
    kv = pl.pallas_call(
        pack_memory,
        out_shape=jax.ShapeDtypeStruct((groups, 2, slab, width), bf16),
        in_specs=[vmem] * 2,
        out_specs=vmem,
    )(mentor_address_vectors, mentor_content_vectors)
    kv = to_group_holders(kv, count)
    q = pl.pallas_call(
        pack_queries,
        out_shape=jax.ShapeDtypeStruct((heads * copies, slab, width), bf16),
        in_specs=[vmem],
        out_specs=vmem,
    )(probe_vectors)
    q = q.reshape(count, per_device, slab, width)
    q = lax.all_to_all(q, "seq", split_axis=0, concat_axis=0, tiled=True)
    first_head = ((place // copies) * per_device).astype(jnp.int32).reshape(1)
    down_t = jnp.swapaxes(fading_narrowing_matrix, 1, 2)
    decays = head_decays(
        q,
        first_head,
        previous_position_blend,
        feature_fading_exponent,
        down_t,
        fading_widening_matrix,
    )
    packed = head_grads(
        q,
        kv,
        decays,
        first_head,
        previous_position_blend,
        down_t,
        fading_widening_matrix,
        diagonal_extra_amount,
    )
    packed = lax.all_to_all(packed, "seq", split_axis=0, concat_axis=0, tiled=True)
    packed = packed.reshape(heads * copies, 2 * rank + PACK_TAIL, width)
    vector = jax.ShapeDtypeStruct((heads, width), f32)
    matrix = jax.ShapeDtypeStruct((heads, rank, width), f32)
    mix, decay, down_t, up, bonus = pl.pallas_call(
        unpack_kernel,
        out_shape=(
            jax.ShapeDtypeStruct((4, heads, width), f32),
            vector,
            matrix,
            matrix,
            vector,
        ),
        in_specs=[vmem],
        out_specs=[vmem] * 5,
    )(packed)
    return mix, decay, jnp.swapaxes(down_t, 1, 2), up, bonus


def solution(mesh):
    return jax.shard_map(
        shards,
        mesh=mesh,
        in_specs=(
            P("seq", "head"),
            P("seq", "head"),
            P("seq", "head"),
            P(None, "head", None),
            P("head", None),
            P("head", None, None),
            P("head", None, None),
            P("head", None),
        ),
        out_specs=(
            P(None, "head", None),
            P("head", None),
            P("head", None, None),
            P("head", None, None),
            P("head", None),
        ),
        check_vma=False,
    )
```

```python
import math

import jax
import jax.numpy as jnp
from jax import lax
from jax.experimental import pallas as pl
from jax.experimental.pallas import tpu as pltpu
from jax.sharding import PartitionSpec as P

NORM_EPS = 0.00064
NEG_LARGE = -1e30
SAFE_EXPONENT = 30.0
PACK_TAIL = 16
LOG2_E = math.log2(math.e)

f32 = jnp.float32
bf16 = jnp.bfloat16

NN = (((1,), (0,)), ((), ()))
NT = (((1,), (1,)), ((), ()))
TN = (((0,), (0,)), ((), ()))


def dot(a, b, dims):
    return lax.dot_general(a, b, dims, preferred_element_type=f32)


def split2(x):
    high = x.astype(bf16)
    return high, (x - high.astype(f32)).astype(bf16)


def split3(x):
    high = x.astype(bf16)
    rest = x - high.astype(f32)
    middle = rest.astype(bf16)
    return high, middle, (rest - middle.astype(f32)).astype(bf16)


def stacked(parts, contracted):
    return jnp.concatenate(parts, axis=contracted)


def dot3(a, b, dims):
    (at,), (bt,) = dims[0]
    return dot(stacked((a[0], a[1], a[0]), at), stacked((b[0], b[0], b[1]), bt), dims)


def dot4(a, b, dims):
    (at,), (bt,) = dims[0]
    return dot(stacked((*a, *a), at), stacked((b[0], b[0], b[1], b[1]), bt), dims)


def joined(parts):
    return parts[0].astype(f32) + parts[1].astype(f32)


def sums_of(zero_one, parts):
    return dot(stacked((zero_one,) * len(parts), 1), stacked(parts, 0), NN)


def row_ids(shape):
    return lax.broadcasted_iota(jnp.int32, shape, 0)


def lane_ids(shape):
    return lax.broadcasted_iota(jnp.int32, shape, 1)


def zero_one(condition):
    return jnp.where(condition, 1.0, 0.0).astype(bf16)


def with_shift(at, first, slabs=1):
    now = slabs_of(at, first, slabs).astype(f32)
    last = at(jnp.maximum(first - 1, 0))
    tail = last[last.shape[0] - 16 :].astype(f32)[15:16]
    tail = jnp.where(first > 0, tail, 0.0)
    earlier = jnp.where(row_ids(now.shape) == 0, tail, pltpu.roll(now, 1, 0))
    return now, earlier - now


def slabs_of(at, first, slabs):
    return jnp.concatenate([at(first + n) for n in range(slabs)], axis=0)


def teacher_phase(q_at, k_at, v_at, teach, scores):
    slabs, slab, width = teach.shape
    _, q_rows, k_rows = scores.shape
    q_slabs, k_slabs = q_rows // slab, k_rows // slab
    scale = LOG2_E / math.sqrt(width)

    def q_block(i, _):
        q = slabs_of(q_at, i * q_slabs, q_slabs)
        last = (i * q_slabs + q_slabs - 1) // k_slabs

        def score_block(j, top, edge=False):
            s = dot(q, slabs_of(k_at, j * k_slabs, k_slabs), NT) * scale
            if edge:
                seen = i * q_rows + row_ids(s.shape) >= j * k_rows + lane_ids(s.shape)
                s = jnp.where(seen, s, NEG_LARGE)
            scores[j] = s
            for n in range(k_rows // 128):
                top = jnp.maximum(top, s[:, n * 128 : (n + 1) * 128])
            return top

        top = lax.fori_loop(0, last, score_block, jnp.full((q_rows, 128), NEG_LARGE, f32))
        top = score_block(last, top, True)
        row_top = jnp.max(top, axis=1, keepdims=True)

        def value_block(j, carry):
            total, accum = carry
            p = jnp.exp2(scores[j] - row_top)
            for n in range(k_rows // 128):
                total = total + p[:, n * 128 : (n + 1) * 128]
            return total, accum + dot(p.astype(bf16), slabs_of(v_at, j * k_slabs, k_slabs), NN)

        total, accum = lax.fori_loop(
            0,
            last + 1,
            value_block,
            (jnp.zeros((q_rows, 128), f32), jnp.zeros((q_rows, width), f32)),
        )
        out = accum / jnp.sum(total, axis=1, keepdims=True)
        teach[pl.ds(i * q_slabs, q_slabs)] = out.astype(bf16).reshape(q_slabs, slab, width)
        return 0

    lax.fori_loop(0, slabs // q_slabs, q_block, 0)


def decay_phase(q_at, down, up, fade, mix, lw_s, ex_s, hid_s, slabs):
    count, slab, width = lw_s.shape
    square = (slab, slab)
    before = zero_one(row_ids(square) > lane_ids(square))

    def block(i, worst):
        first = i * slabs
        q, q_step = with_shift(q_at, first, slabs)
        hid = jnp.tanh(dot3(split2(q + mix[3] * q_step), down, NT))
        lw = -jnp.exp(fade + dot3(split2(hid), up, NN))
        hid_s[pl.ds(first, slabs)] = hid.reshape(slabs, slab, hid.shape[1])
        lw_s[pl.ds(first, slabs)] = lw.reshape(slabs, slab, width)
        for n in range(slabs):
            part = lw[n * slab : (n + 1) * slab]
            ex = sums_of(before, split3(part))
            ex_s[first + n] = ex
            middle = ex[slab // 2 : slab // 2 + 1]
            total = ex[slab - 1 :] + part[slab - 1 :]
            worst = jnp.maximum(worst, jnp.maximum(-middle, middle - total))
        return worst

    return lax.fori_loop(0, count // slabs, block, jnp.zeros((1, width), f32))


def level_parts(level, lw, r, k):
    square = (lw.shape[0], lw.shape[0])
    t, m = row_ids(square), lane_ids(square)
    edge = ((t >> (level + 1)) << (level + 1)) + (1 << level) - 1
    upper = ((t >> level) & 1) == 1
    lower = ((t >> level) & 1) == 0
    span = zero_one((upper & (m > edge) & (m < t)) | (lower & (m > t) & (m <= edge)))
    factor = jnp.exp(sums_of(span, split3(lw)))
    upper_rows = ((row_ids(r.shape) >> level) & 1) == 1
    r_factor = jnp.where(upper_rows, factor, 0.0)
    k_factor = jnp.where(upper_rows, 0.0, factor)
    same = (t >> (level + 1)) == (m >> (level + 1))
    return r_factor, k_factor, split2(r * r_factor), split2(k * k_factor), same, span


def halves(x):
    width = x.shape[1] // 2
    return x[:, :width], x[:, width:]


def student_phase(fast, refs, mix, bonus, down, up, scratch, unroll):
    q_at, k_at, v_at = refs
    teach, lw_s, ex_s, hid_s, state_s, g_s, a_s, r_s, k_s, v_s = scratch
    chunks, slab, width = lw_s.shape
    tokens = chunks * slab
    levels = slab.bit_length() - 1
    square = (slab, slab)
    t, m = row_ids(square), lane_ids(square)
    below = t > m
    after, before = zero_one(t < m), zero_one(below)
    gain = 2.0 / tokens

    def load(c):
        q, q_step = with_shift(q_at, c)
        k0, k_step = with_shift(k_at, c)
        v0, v_step = with_shift(v_at, c)
        r = q + mix[0] * q_step
        k = k0 + mix[1] * k_step
        v = v0 + mix[2] * v_step
        lw, ex = lw_s[c], ex_s[c]
        total = ex[slab - 1 :] + lw[slab - 1 :]
        if fast:
            middle = ex[slab // 2 : slab // 2 + 1]
            r_factor = jnp.exp(ex - middle)
            k_factor = jnp.exp(middle - ex - lw)
            into, out = jnp.exp(middle), jnp.exp(total - middle)
        else:
            r_factor = jnp.exp(ex)
            k_factor = jnp.exp(sums_of(after, split3(lw)))
            into = out = None
        return q, q_step, k_step, v_step, r, k, v, lw, total, r_factor, k_factor, into, out

    def scaled(x, by):
        return x if by is None else x * by

    def forward(c, state):
        _, _, _, _, r, k, v, lw, total, r_factor, k_factor, into, out = load(c)
        rs, ks, vs = split2(r * r_factor), split2(k * k_factor), split2(v)
        if fast:
            a = jnp.where(below, dot3(rs, ks, NT), 0.0)
        else:

            def one_level(level, a):
                _, _, r_part, k_part, block, _ = level_parts(level, lw, r, k)
                return a + jnp.where(block, dot3(r_part, k_part, NT), 0.0)

            a = lax.fori_loop(0, levels, one_level, jnp.zeros(square, f32))
        own = jnp.sum(r * bonus * k, axis=1, keepdims=True)
        a = split2(a)
        state_s[c] = state
        o = own * v + dot3(a, vs, NN) + dot3(rs, split2(scaled(state, into)), NT)
        o = o - jnp.mean(o, axis=1, keepdims=True)
        rate = lax.rsqrt(jnp.mean(o * o, axis=1, keepdims=True) + NORM_EPS)
        normed = o * rate
        g = gain * (normed - teach[c].astype(f32))
        g = g - jnp.mean(g, axis=1, keepdims=True) - normed * jnp.mean(
            g * normed, axis=1, keepdims=True
        )
        g_s[c] = g * rate
        for held, parts in ((a_s, a), (r_s, rs), (k_s, ks), (v_s, vs)):
            held[c] = jnp.concatenate(parts, axis=1)
        return state * jnp.exp(total) + scaled(dot3(vs, ks, TN), out)

    def forward_some(i, state):
        for n in range(unroll):
            state = forward(i * unroll + n, state)
        return state

    lax.fori_loop(0, chunks // unroll, forward_some, jnp.zeros((width, width), f32))

    def backward(c, carry):
        cot, up_sum, down_sum, sums = carry
        q, q_step, k_step, v_step, r, k, v, lw, total, r_factor, k_factor, into, out = load(c)
        a, rs, ks, vs = (halves(held[c]) for held in (a_s, r_s, k_s, v_s))
        g = g_s[c]
        gs = split2(g)
        pair = dot3(gs, vs, NT)
        cot_out = split2(scaled(cot, out))
        state_in = split2(scaled(state_s[c], into))
        k_hat = joined(ks)
        dv = dot3(a, gs, TN) + dot3(ks, cot_out, NT)
        dk = dot3(vs, cot_out, NN)
        from_earlier = k_hat * dk
        dlw = jnp.sum(state_s[c] * jnp.exp(total) * cot, axis=0, keepdims=True)
        if fast:
            pairs = split2(jnp.where(below, pair, 0.0))
            dr = dot(
                stacked((gs[0], gs[1], pairs[0], pairs[1], gs[0], pairs[0], pairs[1]), 1),
                stacked((state_in[0], state_in[0], ks[0], ks[0], state_in[1], ks[1], ks[1]), 0),
                NN,
            )
            dk_in = dot4(pairs, rs, TN)
            k_in = k_hat * dk_in
            from_later = joined(rs) * dr - k_in
            dlw = dlw - k_in
            dr = r_factor * dr
            dk = k_factor * (dk + dk_in)
        else:
            dr = dot3(gs, state_in, NN)
            from_later = joined(rs) * dr
            dr = r_factor * dr
            dk = k_factor * dk

            def one_level(level, parts):
                dr, dk, dlw = parts
                r_by, k_by, r_part, k_part, block, span = level_parts(level, lw, r, k)
                pairs = split2(jnp.where(block & below, pair, 0.0))
                dr_in = r_by * dot3(pairs, k_part, NN)
                dk_in = k_by * dot3(pairs, r_part, TN)
                inside = split3(r * dr_in + k * dk_in)
                return dr + dr_in, dk + dk_in, dlw + sum(dot(span, part, TN) for part in inside)

            dr, dk, dlw = lax.fori_loop(
                0, levels, one_level, (dr, dk, jnp.broadcast_to(dlw, r.shape))
            )
        both = tuple(
            jnp.concatenate(pair, axis=0) for pair in zip(split3(from_later), split3(from_earlier))
        )
        dlw = dlw + sums_of(jnp.concatenate([after, before], axis=1), both)
        dv = dv + jnp.sum(r * bonus * k, axis=1, keepdims=True) * g
        own = jnp.sum(v * g, axis=1, keepdims=True)
        own_r, own_k = own * r, own * k
        dr = dr + bonus * own_k
        dk = dk + bonus * own_r
        dpre = dlw * lw
        hid = hid_s[c]
        dpres = split2(dpre)
        dz = dot3(dpres, up, NT) * (1.0 - hid * hid)
        dzs = split2(dz)
        dxw = dot3(dzs, down, NN)
        up_sum = up_sum + dot3(split2(hid), dpres, TN)
        down_sum = down_sum + dot3(dzs, split2(q + mix[3] * q_step), TN)
        parts = (dr * q_step, dk * k_step, dv * v_step, dxw * q_step, dpre, own_r * k)
        sums = tuple(
            old + jnp.sum(new.reshape(slab // 8, 8, width), axis=0)
            for old, new in zip(sums, parts)
        )
        cot = cot * jnp.exp(total) + scaled(dot3(gs, rs, TN), into)
        return cot, up_sum, down_sum, sums

    def backward_some(i, carry):
        for n in range(unroll):
            carry = backward(chunks - 1 - (i * unroll + n), carry)
        return carry

    rank = down[0].shape[0]
    empty = jnp.zeros((rank, width), f32)
    start = (jnp.zeros((width, width), f32), empty, empty, (jnp.zeros((8, width), f32),) * 6)
    _, up_sum, down_sum, sums = lax.fori_loop(0, chunks // unroll, backward_some, start)
    tail = [split2(jnp.sum(part, axis=0, keepdims=True)) for part in sums]
    tail = [high.astype(f32) for high, _ in tail] + [low.astype(f32) for _, low in tail]
    tail.append(jnp.zeros((PACK_TAIL - len(tail), width), f32))
    return jnp.concatenate([up_sum, down_sum, *tail], axis=0)


def settings_of(head, mix_ref, bonus_ref=None):
    mix = [mix_ref[n, pl.ds(head, 1), :] for n in range(4)]
    return mix if bonus_ref is None else (mix, bonus_ref[pl.ds(head, 1), :])


def head_kernel(head_ref, q_ref, mix_ref, fade_ref, down_ref, up_ref, bonus_ref, *rest):
    slabs, per_device = q_ref.shape[:2]
    pieces, (out_ref, scores, *held, kv_s) = rest[:-13], rest[-13:]
    near, _, shared = kv_s.shape[:3]
    if len(pieces) == near:
        for n, piece in enumerate(pieces):
            kv_s[head_ref[1] ^ n] = piece[...]
        kv_ref = kv_s
    else:
        (kv_ref,) = pieces
    for n in range(per_device):
        head = head_ref[0] + n
        mix, bonus = settings_of(head, mix_ref, bonus_ref)
        fade = fade_ref[pl.ds(head, 1), :]
        down, up = split2(down_ref[head]), split2(up_ref[head])
        group = n * shared // per_device
        refs = (
            lambda c, n=n: q_ref[c, n],
            lambda c, group=group: kv_ref[lax.rem(c, near), c // near, group, 0],
            lambda c, group=group: kv_ref[lax.rem(c, near), c // near, group, 1],
        )
        worst = decay_phase(refs[0], down, up, fade, mix, *held[1:4], math.gcd(4, slabs))
        teacher_phase(*refs, held[0], scores)
        safe = jnp.max(worst) <= SAFE_EXPONENT

        def finish(fast, unroll):
            grads = student_phase(fast, refs, mix, bonus, down, up, held, unroll).astype(bf16)

            def copy_out(at, _):
                out_ref[at, n] = grads
                return 0

            lax.fori_loop(0, slabs, copy_out, 0)

        @pl.when(safe)
        def _():
            finish(True, math.gcd(4, slabs))

        @pl.when(jnp.logical_not(safe))
        def _():
            finish(False, 1)


def head_grads(q, pieces, place, mix, fade, down_t, up, bonus):
    slabs, per_device, slab, width = q.shape
    rank = up.shape[1]
    packed_rows = 2 * rank + PACK_TAIL
    k_slabs = math.gcd(4, slabs)
    small = slabs <= 16
    q_slabs = k_slabs if small else 1
    gathered = pieces[0].ndim == 6
    kv_shape = pieces[0].shape if gathered else (len(pieces), *pieces[0].shape)
    vmem = pl.BlockSpec(memory_space=pltpu.VMEM)
    return pl.pallas_call(
        head_kernel,
        out_shape=jax.ShapeDtypeStruct((slabs, per_device, packed_rows, width), bf16),
        in_specs=[pl.BlockSpec(memory_space=pltpu.SMEM)] + [vmem] * (6 + len(pieces)),
        out_specs=vmem,
        scratch_shapes=[
            pltpu.VMEM((slabs // k_slabs, q_slabs * slab, k_slabs * slab), f32),
            pltpu.VMEM((slabs, slab, width), bf16),
            pltpu.VMEM((slabs, slab, width), f32),
            pltpu.VMEM((slabs, slab, width), f32),
            pltpu.VMEM((slabs, slab, rank), f32),
            pltpu.VMEM((slabs, width, width), f32),
            pltpu.VMEM((slabs, slab, width), f32),
            pltpu.VMEM((slabs, slab, 2 * slab), bf16),
            pltpu.VMEM((slabs, slab, 2 * width), bf16),
            pltpu.VMEM((slabs, slab, 2 * width), bf16),
            pltpu.VMEM((slabs, slab, 2 * width), bf16),
            pltpu.VMEM((*kv_shape[:3], 1, 16, 128) if gathered else kv_shape, bf16),
        ],
        compiler_params=pltpu.CompilerParams(
            vmem_limit_bytes=(36 if small else 60) * 1024 * 1024
        ),
    )(place, q, mix, fade, down_t, up, bonus, *pieces)


def pack_queries(q_ref, out_ref):
    slots, _, width = out_ref.shape
    heads = q_ref.shape[1] // width
    for slot in range(slots):
        head = slot * heads // slots
        out_ref[slot] = q_ref[:, head * width : (head + 1) * width]


def pack_memory(k_ref, v_ref, out_ref):
    groups, _, _, width = out_ref.shape
    for group in range(groups):
        out_ref[group, 0] = k_ref[:, group * width : (group + 1) * width]
        out_ref[group, 1] = v_ref[:, group * width : (group + 1) * width]


def to_group_holders(packed, count):
    groups, _, slab, width = packed.shape
    far = math.gcd(groups, count)
    near = count // far
    shared = groups // far
    packed = packed.reshape(far, shared, 2, slab, width)
    if far > 1:
        lines = [[p + near * z for z in range(far)] for p in range(near)]
        packed = lax.all_to_all(
            packed, "seq", split_axis=0, concat_axis=0, tiled=True, axis_index_groups=lines
        )
    if near & (near - 1) == 0 and near <= 8:
        pieces = [packed]
        for n in range(1, near):
            pairs = [(d, d ^ n) for d in range(count)]
            pieces.append(lax.ppermute(packed, "seq", pairs))
        return pieces
    planes = [[p + near * z for p in range(near)] for z in range(far)]
    packed = jnp.broadcast_to(packed[None], (near, *packed.shape))
    return [
        lax.all_to_all(
            packed, "seq", split_axis=0, concat_axis=0, tiled=True, axis_index_groups=planes
        )
    ]


def unpack_kernel(packed_ref, mix_ref, decay_ref, down_ref, up_ref, bonus_ref):
    heads, rank, _ = up_ref.shape
    copies = packed_ref.shape[0] // heads
    for head in range(heads):
        packed = packed_ref[head * copies].astype(f32)
        up_ref[head] = packed[:rank]
        down_ref[head] = packed[rank : 2 * rank]
        tail = packed[2 * rank :]
        tail = tail[:6] + tail[6:12]
        for n in range(4):
            mix_ref[n, head : head + 1, :] = tail[n : n + 1]
        decay_ref[head : head + 1, :] = tail[4:5]
        bonus_ref[head : head + 1, :] = tail[5:6]


def shards(
    probe_vectors,
    mentor_address_vectors,
    mentor_content_vectors,
    previous_position_blend,
    feature_fading_exponent,
    fading_narrowing_matrix,
    fading_widening_matrix,
    diagonal_extra_amount,
):
    slab = probe_vectors.shape[0]
    heads, width, rank = fading_narrowing_matrix.shape
    place = lax.axis_index("seq")
    count = lax.axis_size("seq")
    copies = max(1, count // heads)
    per_device = max(1, heads // count)
    assert heads * copies == per_device * count
    groups = mentor_address_vectors.shape[1] // width
    vmem = pl.BlockSpec(memory_space=pltpu.VMEM)
    kv = pl.pallas_call(
        pack_memory,
        out_shape=jax.ShapeDtypeStruct((groups, 2, slab, width), bf16),
        in_specs=[vmem] * 2,
        out_specs=vmem,
    )(mentor_address_vectors, mentor_content_vectors)
    pieces = to_group_holders(kv, count)
    q = pl.pallas_call(
        pack_queries,
        out_shape=jax.ShapeDtypeStruct((heads * copies, slab, width), bf16),
        in_specs=[vmem],
        out_specs=vmem,
    )(probe_vectors)
    q = q.reshape(count, per_device, slab, width)
    q = lax.all_to_all(q, "seq", split_axis=0, concat_axis=0, tiled=True)
    first_head = (place // copies) * per_device
    near = count // math.gcd(groups, count)
    packed = head_grads(
        q,
        pieces,
        jnp.stack([first_head, lax.rem(place, near)]).astype(jnp.int32),
        previous_position_blend,
        feature_fading_exponent,
        jnp.swapaxes(fading_narrowing_matrix, 1, 2),
        fading_widening_matrix,
        diagonal_extra_amount,
    )
    packed = lax.all_to_all(packed, "seq", split_axis=0, concat_axis=0, tiled=True)
    packed = packed.reshape(heads * copies, 2 * rank + PACK_TAIL, width)
    vector = jax.ShapeDtypeStruct((heads, width), f32)
    matrix = jax.ShapeDtypeStruct((heads, rank, width), f32)
    mix, decay, down_t, up, bonus = pl.pallas_call(
        unpack_kernel,
        out_shape=(
            jax.ShapeDtypeStruct((4, heads, width), f32),
            vector,
            matrix,
            matrix,
            vector,
        ),
        in_specs=[vmem],
        out_specs=[vmem] * 5,
    )(packed)
    return mix, decay, jnp.swapaxes(down_t, 1, 2), up, bonus


def solution(mesh):
    return jax.shard_map(
        shards,
        mesh=mesh,
        in_specs=(
            P("seq", "head"),
            P("seq", "head"),
            P("seq", "head"),
            P(None, "head", None),
            P("head", None),
            P("head", None, None),
            P("head", None, None),
            P("head", None),
        ),
        out_specs=(
            P(None, "head", None),
            P("head", None),
            P("head", None, None),
            P("head", None, None),
            P("head", None),
        ),
        check_vma=False,
    )
```

```python
import math

import jax
import jax.numpy as jnp
from jax import lax
from jax.experimental import pallas as pl
from jax.experimental.pallas import tpu as pltpu
from jax.sharding import PartitionSpec as P

NORM_EPS = 0.00064
NEG_LARGE = -1e30
SAFE_EXPONENT = 30.0
PACK_TAIL = 16
LOG2_E = math.log2(math.e)

f32 = jnp.float32
bf16 = jnp.bfloat16

NN = (((1,), (0,)), ((), ()))
NT = (((1,), (1,)), ((), ()))
TN = (((0,), (0,)), ((), ()))


def dot(a, b, dims):
    return lax.dot_general(a, b, dims, preferred_element_type=f32)


def split2(x):
    high = x.astype(bf16)
    return high, (x - high.astype(f32)).astype(bf16)


def split3(x):
    high = x.astype(bf16)
    rest = x - high.astype(f32)
    middle = rest.astype(bf16)
    return high, middle, (rest - middle.astype(f32)).astype(bf16)


def stacked(parts, contracted):
    return jnp.concatenate(parts, axis=contracted)


def dot3(a, b, dims):
    (at,), (bt,) = dims[0]
    return dot(stacked((a[0], a[1], a[0]), at), stacked((b[0], b[0], b[1]), bt), dims)


def dot4(a, b, dims):
    (at,), (bt,) = dims[0]
    return dot(stacked((*a, *a), at), stacked((b[0], b[0], b[1], b[1]), bt), dims)


def joined(parts):
    return parts[0].astype(f32) + parts[1].astype(f32)


def sums_of(zero_one, parts):
    return dot(stacked((zero_one,) * len(parts), 1), stacked(parts, 0), NN)


def row_ids(shape):
    return lax.broadcasted_iota(jnp.int32, shape, 0)


def lane_ids(shape):
    return lax.broadcasted_iota(jnp.int32, shape, 1)


def zero_one(condition):
    return jnp.where(condition, 1.0, 0.0).astype(bf16)


def with_shift(at, first, slabs=1):
    now = slabs_of(at, first, slabs).astype(f32)
    last = at(jnp.maximum(first - 1, 0))
    tail = last[last.shape[0] - 16 :].astype(f32)[15:16]
    tail = jnp.where(first > 0, tail, 0.0)
    earlier = jnp.where(row_ids(now.shape) == 0, tail, pltpu.roll(now, 1, 0))
    return now, earlier - now


def slabs_of(at, first, slabs):
    return jnp.concatenate([at(first + n) for n in range(slabs)], axis=0)


def teacher_phase(q_at, k_at, v_at, teach, scores):
    slabs, slab, width = teach.shape
    _, q_rows, k_rows = scores.shape
    q_slabs, k_slabs = q_rows // slab, k_rows // slab
    scale = LOG2_E / math.sqrt(width)

    def q_block(i, _):
        q = slabs_of(q_at, i * q_slabs, q_slabs)
        last = (i * q_slabs + q_slabs - 1) // k_slabs

        def score_block(j, top, edge=False):
            s = dot(q, slabs_of(k_at, j * k_slabs, k_slabs), NT) * scale
            if edge:
                seen = i * q_rows + row_ids(s.shape) >= j * k_rows + lane_ids(s.shape)
                s = jnp.where(seen, s, NEG_LARGE)
            scores[j] = s
            for n in range(k_rows // 128):
                top = jnp.maximum(top, s[:, n * 128 : (n + 1) * 128])
            return top

        top = lax.fori_loop(0, last, score_block, jnp.full((q_rows, 128), NEG_LARGE, f32))
        top = score_block(last, top, True)
        row_top = jnp.max(top, axis=1, keepdims=True)

        def value_block(j, carry):
            total, accum = carry
            p = jnp.exp2(scores[j] - row_top)
            for n in range(k_rows // 128):
                total = total + p[:, n * 128 : (n + 1) * 128]
            return total, accum + dot(p.astype(bf16), slabs_of(v_at, j * k_slabs, k_slabs), NN)

        total, accum = lax.fori_loop(
            0,
            last + 1,
            value_block,
            (jnp.zeros((q_rows, 128), f32), jnp.zeros((q_rows, width), f32)),
        )
        out = accum / jnp.sum(total, axis=1, keepdims=True)
        teach[pl.ds(i * q_slabs, q_slabs)] = out.astype(bf16).reshape(q_slabs, slab, width)
        return 0

    lax.fori_loop(0, slabs // q_slabs, q_block, 0)


def decay_phase(q_at, down, up, fade, mix, lw_s, ex_s, hid_s, slabs):
    count, slab, width = lw_s.shape
    square = (slab, slab)
    before = zero_one(row_ids(square) > lane_ids(square))

    def block(i, worst):
        first = i * slabs
        q, q_step = with_shift(q_at, first, slabs)
        hid = jnp.tanh(dot3(split2(q + mix[3] * q_step), down, NT))
        lw = -jnp.exp(fade + dot3(split2(hid), up, NN))
        hid_s[pl.ds(first, slabs)] = hid.reshape(slabs, slab, hid.shape[1])
        lw_s[pl.ds(first, slabs)] = lw.reshape(slabs, slab, width)
        for n in range(slabs):
            part = lw[n * slab : (n + 1) * slab]
            ex = sums_of(before, split3(part))
            ex_s[first + n] = ex
            middle = ex[slab // 2 : slab // 2 + 1]
            total = ex[slab - 1 :] + part[slab - 1 :]
            worst = jnp.maximum(worst, jnp.maximum(-middle, middle - total))
        return worst

    return lax.fori_loop(0, count // slabs, block, jnp.zeros((1, width), f32))


def level_parts(level, lw, r, k):
    square = (lw.shape[0], lw.shape[0])
    t, m = row_ids(square), lane_ids(square)
    edge = ((t >> (level + 1)) << (level + 1)) + (1 << level) - 1
    upper = ((t >> level) & 1) == 1
    lower = ((t >> level) & 1) == 0
    span = zero_one((upper & (m > edge) & (m < t)) | (lower & (m > t) & (m <= edge)))
    factor = jnp.exp(sums_of(span, split3(lw)))
    upper_rows = ((row_ids(r.shape) >> level) & 1) == 1
    r_factor = jnp.where(upper_rows, factor, 0.0)
    k_factor = jnp.where(upper_rows, 0.0, factor)
    same = (t >> (level + 1)) == (m >> (level + 1))
    return r_factor, k_factor, split2(r * r_factor), split2(k * k_factor), same, span


def halves(x):
    width = x.shape[1] // 2
    return x[:, :width], x[:, width:]


def student_phase(fast, refs, mix, bonus, down, up, scratch, unroll):
    q_at, k_at, v_at = refs
    teach, lw_s, ex_s, hid_s, state_s, g_s, a_s, r_s, k_s, v_s = scratch
    chunks, slab, width = lw_s.shape
    tokens = chunks * slab
    levels = slab.bit_length() - 1
    square = (slab, slab)
    t, m = row_ids(square), lane_ids(square)
    below = t > m
    after, before = zero_one(t < m), zero_one(below)
    gain = 2.0 / tokens

    def load(c):
        q, q_step = with_shift(q_at, c)
        k0, k_step = with_shift(k_at, c)
        v0, v_step = with_shift(v_at, c)
        r = q + mix[0] * q_step
        k = k0 + mix[1] * k_step
        v = v0 + mix[2] * v_step
        lw, ex = lw_s[c], ex_s[c]
        total = ex[slab - 1 :] + lw[slab - 1 :]
        if fast:
            middle = ex[slab // 2 : slab // 2 + 1]
            r_factor = jnp.exp(ex - middle)
            k_factor = jnp.exp(middle - ex - lw)
            into, out = jnp.exp(middle), jnp.exp(total - middle)
        else:
            r_factor = jnp.exp(ex)
            k_factor = jnp.exp(sums_of(after, split3(lw)))
            into = out = None
        return q, q_step, k_step, v_step, r, k, v, lw, total, r_factor, k_factor, into, out

    def scaled(x, by):
        return x if by is None else x * by

    def forward(c, state):
        _, _, _, _, r, k, v, lw, total, r_factor, k_factor, into, out = load(c)
        rs, ks, vs = split2(r * r_factor), split2(k * k_factor), split2(v)
        if fast:
            a = jnp.where(below, dot3(rs, ks, NT), 0.0)
        else:

            def one_level(level, a):
                _, _, r_part, k_part, block, _ = level_parts(level, lw, r, k)
                return a + jnp.where(block, dot3(r_part, k_part, NT), 0.0)

            a = lax.fori_loop(0, levels, one_level, jnp.zeros(square, f32))
        own = jnp.sum(r * bonus * k, axis=1, keepdims=True)
        a = split2(a)
        state_s[c] = state
        o = own * v + dot3(a, vs, NN) + dot3(rs, split2(scaled(state, into)), NT)
        o = o - jnp.mean(o, axis=1, keepdims=True)
        rate = lax.rsqrt(jnp.mean(o * o, axis=1, keepdims=True) + NORM_EPS)
        normed = o * rate
        g = gain * (normed - teach[c].astype(f32))
        g = g - jnp.mean(g, axis=1, keepdims=True) - normed * jnp.mean(
            g * normed, axis=1, keepdims=True
        )
        g_s[c] = g * rate
        for held, parts in ((a_s, a), (r_s, rs), (k_s, ks), (v_s, vs)):
            held[c] = jnp.concatenate(parts, axis=1)
        return state * jnp.exp(total) + scaled(dot3(vs, ks, TN), out)

    def forward_some(i, state):
        for n in range(unroll):
            state = forward(i * unroll + n, state)
        return state

    lax.fori_loop(0, chunks // unroll, forward_some, jnp.zeros((width, width), f32))

    def backward(c, carry):
        cot, up_sum, down_sum, sums = carry
        q, q_step, k_step, v_step, r, k, v, lw, total, r_factor, k_factor, into, out = load(c)
        a, rs, ks, vs = (halves(held[c]) for held in (a_s, r_s, k_s, v_s))
        g = g_s[c]
        gs = split2(g)
        pair = dot3(gs, vs, NT)
        cot_out = split2(scaled(cot, out))
        state_in = split2(scaled(state_s[c], into))
        k_hat = joined(ks)
        dv = dot3(a, gs, TN) + dot3(ks, cot_out, NT)
        dk = dot3(vs, cot_out, NN)
        from_earlier = k_hat * dk
        dlw = jnp.sum(state_s[c] * jnp.exp(total) * cot, axis=0, keepdims=True)
        if fast:
            pairs = split2(jnp.where(below, pair, 0.0))
            dr = dot(
                stacked((gs[0], gs[1], pairs[0], pairs[1], gs[0], pairs[0], pairs[1]), 1),
                stacked((state_in[0], state_in[0], ks[0], ks[0], state_in[1], ks[1], ks[1]), 0),
                NN,
            )
            dk_in = dot4(pairs, rs, TN)
            k_in = k_hat * dk_in
            from_later = joined(rs) * dr - k_in
            dlw = dlw - k_in
            dr = r_factor * dr
            dk = k_factor * (dk + dk_in)
        else:
            dr = dot3(gs, state_in, NN)
            from_later = joined(rs) * dr
            dr = r_factor * dr
            dk = k_factor * dk

            def one_level(level, parts):
                dr, dk, dlw = parts
                r_by, k_by, r_part, k_part, block, span = level_parts(level, lw, r, k)
                pairs = split2(jnp.where(block & below, pair, 0.0))
                dr_in = r_by * dot3(pairs, k_part, NN)
                dk_in = k_by * dot3(pairs, r_part, TN)
                inside = split3(r * dr_in + k * dk_in)
                return dr + dr_in, dk + dk_in, dlw + sum(dot(span, part, TN) for part in inside)

            dr, dk, dlw = lax.fori_loop(
                0, levels, one_level, (dr, dk, jnp.broadcast_to(dlw, r.shape))
            )
        both = tuple(
            jnp.concatenate(pair, axis=0) for pair in zip(split3(from_later), split3(from_earlier))
        )
        dlw = dlw + sums_of(jnp.concatenate([after, before], axis=1), both)
        dv = dv + jnp.sum(r * bonus * k, axis=1, keepdims=True) * g
        own = jnp.sum(v * g, axis=1, keepdims=True)
        own_r, own_k = own * r, own * k
        dr = dr + bonus * own_k
        dk = dk + bonus * own_r
        dpre = dlw * lw
        hid = hid_s[c]
        dpres = split2(dpre)
        dz = dot3(dpres, up, NT) * (1.0 - hid * hid)
        dzs = split2(dz)
        dxw = dot3(dzs, down, NN)
        up_sum = up_sum + dot3(split2(hid), dpres, TN)
        down_sum = down_sum + dot3(dzs, split2(q + mix[3] * q_step), TN)
        parts = (dr * q_step, dk * k_step, dv * v_step, dxw * q_step, dpre, own_r * k)
        sums = tuple(
            old + jnp.sum(new.reshape(slab // 8, 8, width), axis=0)
            for old, new in zip(sums, parts)
        )
        cot = cot * jnp.exp(total) + scaled(dot3(gs, rs, TN), into)
        return cot, up_sum, down_sum, sums

    def backward_some(i, carry):
        for n in range(unroll):
            carry = backward(chunks - 1 - (i * unroll + n), carry)
        return carry

    rank = down[0].shape[0]
    empty = jnp.zeros((rank, width), f32)
    start = (jnp.zeros((width, width), f32), empty, empty, (jnp.zeros((8, width), f32),) * 6)
    _, up_sum, down_sum, sums = lax.fori_loop(0, chunks // unroll, backward_some, start)
    tail = [split2(jnp.sum(part, axis=0, keepdims=True)) for part in sums]
    tail = [high.astype(f32) for high, _ in tail] + [low.astype(f32) for _, low in tail]
    tail.append(jnp.zeros((PACK_TAIL - len(tail), width), f32))
    return jnp.concatenate([up_sum, down_sum, *tail], axis=0)


def settings_of(head, mix_ref, bonus_ref):
    mix = [mix_ref[n, pl.ds(head, 1), :] for n in range(4)]
    return mix, bonus_ref[pl.ds(head, 1), :]


def in_order(pieces, scratch, place):
    if len(pieces) == 1:
        return pieces[0]
    for n, piece in enumerate(pieces):
        scratch[place ^ n] = piece[...]
    return scratch


def head_kernel(head_ref, q_ref, mix_ref, fade_ref, down_ref, up_ref, bonus_ref, *rest):
    slabs, per_device = q_ref.shape[:2]
    pieces, (out_ref, scores, *held, kv_s) = rest[:-13], rest[-13:]
    kv_ref = in_order(pieces, kv_s, head_ref[1])
    copies, shared = out_ref.shape[0], kv_ref.shape[1]
    for n in range(per_device):
        head = head_ref[0] + n
        mix, bonus = settings_of(head, mix_ref, bonus_ref)
        fade = fade_ref[pl.ds(head, 1), :]
        down, up = split2(down_ref[head]), split2(up_ref[head])
        group = n * shared // per_device
        refs = (
            lambda c, n=n: q_ref[c, n],
            lambda c, group=group: kv_ref[c, group, 0],
            lambda c, group=group: kv_ref[c, group, 1],
        )
        worst = decay_phase(refs[0], down, up, fade, mix, *held[1:4], math.gcd(4, slabs))
        teacher_phase(*refs, held[0], scores)
        safe = jnp.max(worst) <= SAFE_EXPONENT

        def finish(fast, unroll):
            grads = student_phase(fast, refs, mix, bonus, down, up, held, unroll).astype(bf16)

            def copy_out(at, _):
                out_ref[at, n] = grads
                return 0

            lax.fori_loop(0, copies, copy_out, 0)

        @pl.when(safe)
        def _():
            finish(True, math.gcd(4, slabs))

        @pl.when(jnp.logical_not(safe))
        def _():
            finish(False, 1)


def head_grads(q, pieces, place, mix, fade, down_t, up, bonus, copies):
    slabs, per_device, slab, width = q.shape
    rank = up.shape[1]
    packed_rows = 2 * rank + PACK_TAIL
    k_slabs = math.gcd(4, slabs)
    small = slabs <= 16
    q_slabs = k_slabs if small else 1
    kv_shape = (slabs, *pieces[0].shape) if len(pieces) > 1 else (1, 16, width)
    vmem = pl.BlockSpec(memory_space=pltpu.VMEM)
    return pl.pallas_call(
        head_kernel,
        out_shape=jax.ShapeDtypeStruct((copies, per_device, packed_rows, width), bf16),
        in_specs=[pl.BlockSpec(memory_space=pltpu.SMEM)] + [vmem] * (6 + len(pieces)),
        out_specs=vmem,
        scratch_shapes=[
            pltpu.VMEM((slabs // k_slabs, q_slabs * slab, k_slabs * slab), f32),
            pltpu.VMEM((slabs, slab, width), bf16),
            pltpu.VMEM((slabs, slab, width), f32),
            pltpu.VMEM((slabs, slab, width), f32),
            pltpu.VMEM((slabs, slab, rank), f32),
            pltpu.VMEM((slabs, width, width), f32),
            pltpu.VMEM((slabs, slab, width), f32),
            pltpu.VMEM((slabs, slab, 2 * slab), bf16),
            pltpu.VMEM((slabs, slab, 2 * width), bf16),
            pltpu.VMEM((slabs, slab, 2 * width), bf16),
            pltpu.VMEM((slabs, slab, 2 * width), bf16),
            pltpu.VMEM(kv_shape, bf16),
        ],
        compiler_params=pltpu.CompilerParams(
            vmem_limit_bytes=(36 if small else 60) * 1024 * 1024
        ),
    )(place, q, mix, fade, down_t, up, bonus, *pieces)


def pack_queries(q_ref, out_ref):
    slots, _, width = out_ref.shape
    heads = q_ref.shape[1] // width
    for slot in range(slots):
        head = slot * heads // slots
        out_ref[slot] = q_ref[:, head * width : (head + 1) * width]


def pack_memory(groups_ref, k_ref, v_ref, *out_refs):
    width = out_refs[0].shape[-1]
    for n, out_ref in enumerate(out_refs):
        columns = pl.ds(pl.multiple_of(groups_ref[n] * width, width), width)
        out_ref[0, 0] = k_ref[:, columns]
        out_ref[0, 1] = v_ref[:, columns]


def unpack_kernel(place_ref, *refs):
    *pieces, mix_ref, decay_ref, down_ref, up_ref, bonus_ref = refs
    heads, rank, _ = up_ref.shape
    for n in range(heads):
        if len(pieces) == 1:
            head, packed = n, pieces[0][n * (pieces[0].shape[0] // heads)]
        else:
            head, packed = place_ref[0] ^ n, pieces[n][0, 0]
        packed = packed.astype(f32)
        up_ref[head] = packed[:rank]
        down_ref[head] = packed[rank : 2 * rank]
        tail = packed[2 * rank :]
        tail = tail[:6] + tail[6:12]
        for at in range(4):
            mix_ref[at, pl.ds(head, 1), :] = tail[at : at + 1]
        decay_ref[pl.ds(head, 1), :] = tail[4:5]
        bonus_ref[pl.ds(head, 1), :] = tail[5:6]


def exchanged(x, differing, count):
    return lax.ppermute(x, "seq", [(d, d ^ differing) for d in range(count)])


def shards(
    probe_vectors,
    mentor_address_vectors,
    mentor_content_vectors,
    previous_position_blend,
    feature_fading_exponent,
    fading_narrowing_matrix,
    fading_widening_matrix,
    diagonal_extra_amount,
):
    slab = probe_vectors.shape[0]
    heads, width, rank = fading_narrowing_matrix.shape
    place = lax.axis_index("seq")
    count = lax.axis_size("seq")
    copies = max(1, count // heads)
    per_device = max(1, heads // count)
    assert heads * copies == per_device * count
    groups = mentor_address_vectors.shape[1] // width
    by_bits = heads == count and count <= 16 and count & (count - 1) == 0 and count % groups == 0
    far, near = groups, count // groups
    vmem = pl.BlockSpec(memory_space=pltpu.VMEM)
    smem = pl.BlockSpec(memory_space=pltpu.SMEM)
    place = place.astype(jnp.int32)
    if by_bits:
        wanted = jnp.bitwise_xor(place // near, jnp.arange(far, dtype=jnp.int32))
        shared = 1
    else:
        shared = max(1, per_device * groups // heads)
        firsts = [(d // copies) * per_device * groups // heads for d in range(count)]
        wanted = jnp.asarray([g + n for g in firsts for n in range(shared)], jnp.int32)
    slot = jax.ShapeDtypeStruct((1, 2, slab, width), bf16)
    kv = pl.pallas_call(
        pack_memory,
        out_shape=[slot] * wanted.shape[0],
        in_specs=[smem, vmem, vmem],
        out_specs=[vmem] * wanted.shape[0],
    )(wanted, mentor_address_vectors, mentor_content_vectors)
    if by_bits:
        lines = [kv[0]] + [exchanged(kv[n], n * near, count) for n in range(1, far)]
    q = pl.pallas_call(
        pack_queries,
        out_shape=jax.ShapeDtypeStruct((heads * copies, slab, width), bf16),
        in_specs=[vmem],
        out_specs=vmem,
    )(probe_vectors)
    q = q.reshape(count, per_device, slab, width)
    q = lax.all_to_all(q, "seq", split_axis=0, concat_axis=0, tiled=True)
    if by_bits:
        pieces = [
            exchanged(line, n, count) if n else line for line in lines for n in range(near)
        ]
    else:
        kv = jnp.stack(kv).reshape(count, shared, 2, slab, width)
        pieces = [lax.all_to_all(kv, "seq", split_axis=0, concat_axis=0, tiled=True)]
    packed = head_grads(
        q,
        pieces,
        jnp.stack([(place // copies) * per_device, place]),
        previous_position_blend,
        feature_fading_exponent,
        jnp.swapaxes(fading_narrowing_matrix, 1, 2),
        fading_widening_matrix,
        diagonal_extra_amount,
        1 if by_bits else count,
    )
    if by_bits:
        lines = [packed] + [exchanged(packed, n * near, count) for n in range(1, far)]
        packed = [
            exchanged(line, n, count) if n else line for line in lines for n in range(near)
        ]
    else:
        packed = lax.all_to_all(packed, "seq", split_axis=0, concat_axis=0, tiled=True)
        packed = [packed.reshape(heads * copies, 2 * rank + PACK_TAIL, width)]
    vector = jax.ShapeDtypeStruct((heads, width), f32)
    matrix = jax.ShapeDtypeStruct((heads, rank, width), f32)
    mix, decay, down_t, up, bonus = pl.pallas_call(
        unpack_kernel,
        out_shape=(
            jax.ShapeDtypeStruct((4, heads, width), f32),
            vector,
            matrix,
            matrix,
            vector,
        ),
        in_specs=[smem] + [vmem] * len(packed),
        out_specs=[vmem] * 5,
    )(place.reshape(1), *packed)
    return mix, decay, jnp.swapaxes(down_t, 1, 2), up, bonus


def solution(mesh):
    return jax.shard_map(
        shards,
        mesh=mesh,
        in_specs=(
            P("seq", "head"),
            P("seq", "head"),
            P("seq", "head"),
            P(None, "head", None),
            P("head", None),
            P("head", None, None),
            P("head", None, None),
            P("head", None),
        ),
        out_specs=(
            P(None, "head", None),
            P("head", None),
            P("head", None, None),
            P("head", None, None),
            P("head", None),
        ),
        check_vma=False,
    )
```

```python
import math

import jax
import jax.numpy as jnp
from jax import lax
from jax.experimental import pallas as pl
from jax.experimental.pallas import tpu as pltpu
from jax.sharding import PartitionSpec as P

NORM_EPS = 0.00064
NEG_LARGE = -1e30
SAFE_EXPONENT = 30.0
PACK_TAIL = 16
LOG2_E = math.log2(math.e)

f32 = jnp.float32
bf16 = jnp.bfloat16

NN = (((1,), (0,)), ((), ()))
NT = (((1,), (1,)), ((), ()))
TN = (((0,), (0,)), ((), ()))


def dot(a, b, dims):
    return lax.dot_general(a, b, dims, preferred_element_type=f32)


def split2(x):
    high = x.astype(bf16)
    return high, (x - high.astype(f32)).astype(bf16)


def split3(x):
    high = x.astype(bf16)
    rest = x - high.astype(f32)
    middle = rest.astype(bf16)
    return high, middle, (rest - middle.astype(f32)).astype(bf16)


def stacked(parts, contracted):
    return jnp.concatenate(parts, axis=contracted)


def dot3(a, b, dims):
    (at,), (bt,) = dims[0]
    return dot(stacked((a[0], a[1], a[0]), at), stacked((b[0], b[0], b[1]), bt), dims)


def dot4(a, b, dims):
    (at,), (bt,) = dims[0]
    return dot(stacked((*a, *a), at), stacked((b[0], b[0], b[1], b[1]), bt), dims)


def joined(parts):
    return parts[0].astype(f32) + parts[1].astype(f32)


def sums_of(zero_one, parts):
    return dot(stacked((zero_one,) * len(parts), 1), stacked(parts, 0), NN)


def row_ids(shape):
    return lax.broadcasted_iota(jnp.int32, shape, 0)


def lane_ids(shape):
    return lax.broadcasted_iota(jnp.int32, shape, 1)


def zero_one(condition):
    return jnp.where(condition, 1.0, 0.0).astype(bf16)


def with_shift(at, first, slabs=1):
    now = slabs_of(at, first, slabs).astype(f32)
    last = at(jnp.maximum(first - 1, 0))
    tail = last[last.shape[0] - 16 :].astype(f32)[15:16]
    tail = jnp.where(first > 0, tail, 0.0)
    earlier = jnp.where(row_ids(now.shape) == 0, tail, pltpu.roll(now, 1, 0))
    return now, earlier - now


def slabs_of(at, first, slabs):
    return jnp.concatenate([at(first + n) for n in range(slabs)], axis=0)


def teacher_phase(q_at, k_at, v_at, teach, scores):
    slabs, slab, width = teach.shape
    _, q_rows, k_rows = scores.shape
    q_slabs, k_slabs = q_rows // slab, k_rows // slab
    scale = LOG2_E / math.sqrt(width)

    def q_block(i, _):
        q = slabs_of(q_at, i * q_slabs, q_slabs)
        last = (i * q_slabs + q_slabs - 1) // k_slabs

        def score_block(j, top, edge=False):
            s = dot(q, slabs_of(k_at, j * k_slabs, k_slabs), NT) * scale
            if edge:
                seen = i * q_rows + row_ids(s.shape) >= j * k_rows + lane_ids(s.shape)
                s = jnp.where(seen, s, NEG_LARGE)
            scores[j] = s
            for n in range(k_rows // 128):
                top = jnp.maximum(top, s[:, n * 128 : (n + 1) * 128])
            return top

        top = lax.fori_loop(0, last, score_block, jnp.full((q_rows, 128), NEG_LARGE, f32))
        top = score_block(last, top, True)
        row_top = jnp.max(top, axis=1, keepdims=True)

        def value_block(j, carry):
            total, accum = carry
            p = jnp.exp2(scores[j] - row_top)
            for n in range(k_rows // 128):
                total = total + p[:, n * 128 : (n + 1) * 128]
            return total, accum + dot(p.astype(bf16), slabs_of(v_at, j * k_slabs, k_slabs), NN)

        total, accum = lax.fori_loop(
            0,
            last + 1,
            value_block,
            (jnp.zeros((q_rows, 128), f32), jnp.zeros((q_rows, width), f32)),
        )
        out = accum / jnp.sum(total, axis=1, keepdims=True)
        teach[pl.ds(i * q_slabs, q_slabs)] = out.astype(bf16).reshape(q_slabs, slab, width)
        return 0

    lax.fori_loop(0, slabs // q_slabs, q_block, 0)


def decay_phase(q_at, down, up, fade, mix, lw_s, ex_s, hid_s, slabs):
    count, slab, width = lw_s.shape
    square = (slab, slab)
    before = zero_one(row_ids(square) > lane_ids(square))

    def block(i, worst):
        first = i * slabs
        q, q_step = with_shift(q_at, first, slabs)
        hid = jnp.tanh(dot3(split2(q + mix[3] * q_step), down, NT))
        lw = -jnp.exp(fade + dot3(split2(hid), up, NN))
        hid_s[pl.ds(first, slabs)] = hid.reshape(slabs, slab, hid.shape[1])
        lw_s[pl.ds(first, slabs)] = lw.reshape(slabs, slab, width)
        for n in range(slabs):
            part = lw[n * slab : (n + 1) * slab]
            ex = sums_of(before, split3(part))
            ex_s[first + n] = ex
            middle = ex[slab // 2 : slab // 2 + 1]
            total = ex[slab - 1 :] + part[slab - 1 :]
            worst = jnp.maximum(worst, jnp.maximum(-middle, middle - total))
        return worst

    return lax.fori_loop(0, count // slabs, block, jnp.zeros((1, width), f32))


def level_parts(level, lw, r, k):
    square = (lw.shape[0], lw.shape[0])
    t, m = row_ids(square), lane_ids(square)
    edge = ((t >> (level + 1)) << (level + 1)) + (1 << level) - 1
    upper = ((t >> level) & 1) == 1
    lower = ((t >> level) & 1) == 0
    span = zero_one((upper & (m > edge) & (m < t)) | (lower & (m > t) & (m <= edge)))
    factor = jnp.exp(sums_of(span, split3(lw)))
    upper_rows = ((row_ids(r.shape) >> level) & 1) == 1
    r_factor = jnp.where(upper_rows, factor, 0.0)
    k_factor = jnp.where(upper_rows, 0.0, factor)
    same = (t >> (level + 1)) == (m >> (level + 1))
    return r_factor, k_factor, split2(r * r_factor), split2(k * k_factor), same, span


def halves(x):
    width = x.shape[1] // 2
    return x[:, :width], x[:, width:]


def student_phase(fast, refs, mix, bonus, down, up, scratch, unroll):
    q_at, k_at, v_at = refs
    teach, lw_s, ex_s, hid_s, state_s, g_s, a_s, r_s, k_s, v_s = scratch
    chunks, slab, width = lw_s.shape
    tokens = chunks * slab
    levels = slab.bit_length() - 1
    square = (slab, slab)
    t, m = row_ids(square), lane_ids(square)
    below = t > m
    after, before = zero_one(t < m), zero_one(below)
    gain = 2.0 / tokens

    def load(c):
        q, q_step = with_shift(q_at, c)
        k0, k_step = with_shift(k_at, c)
        v0, v_step = with_shift(v_at, c)
        r = q + mix[0] * q_step
        k = k0 + mix[1] * k_step
        v = v0 + mix[2] * v_step
        lw, ex = lw_s[c], ex_s[c]
        total = ex[slab - 1 :] + lw[slab - 1 :]
        if fast:
            middle = ex[slab // 2 : slab // 2 + 1]
            r_factor = jnp.exp(ex - middle)
            k_factor = jnp.exp(middle - ex - lw)
            into, out = jnp.exp(middle), jnp.exp(total - middle)
        else:
            r_factor = jnp.exp(ex)
            k_factor = jnp.exp(sums_of(after, split3(lw)))
            into = out = None
        return q, q_step, k_step, v_step, r, k, v, lw, total, r_factor, k_factor, into, out

    def scaled(x, by):
        return x if by is None else x * by

    def forward(c, state):
        _, _, _, _, r, k, v, lw, total, r_factor, k_factor, into, out = load(c)
        rs, ks, vs = split2(r * r_factor), split2(k * k_factor), split2(v)
        if fast:
            a = jnp.where(below, dot3(rs, ks, NT), 0.0)
        else:

            def one_level(level, a):
                _, _, r_part, k_part, block, _ = level_parts(level, lw, r, k)
                return a + jnp.where(block, dot3(r_part, k_part, NT), 0.0)

            a = lax.fori_loop(0, levels, one_level, jnp.zeros(square, f32))
        own = jnp.sum(r * bonus * k, axis=1, keepdims=True)
        a = split2(a)
        state_s[c] = state
        o = own * v + dot3(a, vs, NN) + dot3(rs, split2(scaled(state, into)), NT)
        o = o - jnp.mean(o, axis=1, keepdims=True)
        rate = lax.rsqrt(jnp.mean(o * o, axis=1, keepdims=True) + NORM_EPS)
        normed = o * rate
        g = gain * (normed - teach[c].astype(f32))
        g = g - jnp.mean(g, axis=1, keepdims=True) - normed * jnp.mean(
            g * normed, axis=1, keepdims=True
        )
        g_s[c] = g * rate
        for held, parts in ((a_s, a), (r_s, rs), (k_s, ks), (v_s, vs)):
            held[c] = jnp.concatenate(parts, axis=1)
        return state * jnp.exp(total) + scaled(dot3(vs, ks, TN), out)

    def forward_some(i, state):
        for n in range(unroll):
            state = forward(i * unroll + n, state)
        return state

    lax.fori_loop(0, chunks // unroll, forward_some, jnp.zeros((width, width), f32))

    def backward(c, carry):
        cot, up_sum, down_sum, sums = carry
        q, q_step, k_step, v_step, r, k, v, lw, total, r_factor, k_factor, into, out = load(c)
        a, rs, ks, vs = (halves(held[c]) for held in (a_s, r_s, k_s, v_s))
        g = g_s[c]
        gs = split2(g)
        pair = dot3(gs, vs, NT)
        cot_out = split2(scaled(cot, out))
        state_in = split2(scaled(state_s[c], into))
        k_hat = joined(ks)
        dv = dot3(a, gs, TN) + dot3(ks, cot_out, NT)
        dk = dot3(vs, cot_out, NN)
        from_earlier = k_hat * dk
        dlw = jnp.sum(state_s[c] * jnp.exp(total) * cot, axis=0, keepdims=True)
        if fast:
            pairs = split2(jnp.where(below, pair, 0.0))
            dr = dot(
                stacked((gs[0], gs[1], pairs[0], pairs[1], gs[0], pairs[0], pairs[1]), 1),
                stacked((state_in[0], state_in[0], ks[0], ks[0], state_in[1], ks[1], ks[1]), 0),
                NN,
            )
            dk_in = dot4(pairs, rs, TN)
            k_in = k_hat * dk_in
            from_later = joined(rs) * dr - k_in
            dlw = dlw - k_in
            dr = r_factor * dr
            dk = k_factor * (dk + dk_in)
        else:
            dr = dot3(gs, state_in, NN)
            from_later = joined(rs) * dr
            dr = r_factor * dr
            dk = k_factor * dk

            def one_level(level, parts):
                dr, dk, dlw = parts
                r_by, k_by, r_part, k_part, block, span = level_parts(level, lw, r, k)
                pairs = split2(jnp.where(block & below, pair, 0.0))
                dr_in = r_by * dot3(pairs, k_part, NN)
                dk_in = k_by * dot3(pairs, r_part, TN)
                inside = split3(r * dr_in + k * dk_in)
                return dr + dr_in, dk + dk_in, dlw + sum(dot(span, part, TN) for part in inside)

            dr, dk, dlw = lax.fori_loop(
                0, levels, one_level, (dr, dk, jnp.broadcast_to(dlw, r.shape))
            )
        both = tuple(
            jnp.concatenate(pair, axis=0) for pair in zip(split3(from_later), split3(from_earlier))
        )
        dlw = dlw + sums_of(jnp.concatenate([after, before], axis=1), both)
        dv = dv + jnp.sum(r * bonus * k, axis=1, keepdims=True) * g
        own = jnp.sum(v * g, axis=1, keepdims=True)
        own_r, own_k = own * r, own * k
        dr = dr + bonus * own_k
        dk = dk + bonus * own_r
        dpre = dlw * lw
        hid = hid_s[c]
        dpres = split2(dpre)
        dz = dot3(dpres, up, NT) * (1.0 - hid * hid)
        dzs = split2(dz)
        dxw = dot3(dzs, down, NN)
        up_sum = up_sum + dot3(split2(hid), dpres, TN)
        down_sum = down_sum + dot3(dzs, split2(q + mix[3] * q_step), TN)
        parts = (dr * q_step, dk * k_step, dv * v_step, dxw * q_step, dpre, own_r * k)
        sums = tuple(
            old + jnp.sum(new.reshape(slab // 8, 8, width), axis=0)
            for old, new in zip(sums, parts)
        )
        cot = cot * jnp.exp(total) + scaled(dot3(gs, rs, TN), into)
        return cot, up_sum, down_sum, sums

    def backward_some(i, carry):
        for n in range(unroll):
            carry = backward(chunks - 1 - (i * unroll + n), carry)
        return carry

    rank = down[0].shape[0]
    empty = jnp.zeros((rank, width), f32)
    start = (jnp.zeros((width, width), f32), empty, empty, (jnp.zeros((8, width), f32),) * 6)
    _, up_sum, down_sum, sums = lax.fori_loop(0, chunks // unroll, backward_some, start)
    tail = [split2(jnp.sum(part, axis=0, keepdims=True)) for part in sums]
    tail = [high.astype(f32) for high, _ in tail] + [low.astype(f32) for _, low in tail]
    tail.append(jnp.zeros((PACK_TAIL - len(tail), width), f32))
    return jnp.concatenate([up_sum, down_sum, *tail], axis=0)


def settings_of(head, mix_ref, bonus_ref):
    mix = [mix_ref[n, pl.ds(head, 1), :] for n in range(4)]
    return mix, bonus_ref[pl.ds(head, 1), :]


def in_order(pieces, scratch, place):
    if len(pieces) == 1:
        return pieces[0]
    near = len(pieces)
    for n, piece in enumerate(pieces):
        for far in range(piece.shape[0]):
            scratch[place ^ (far * near + n)] = piece[far]
    return scratch


def head_kernel(head_ref, q_ref, mix_ref, fade_ref, down_ref, up_ref, bonus_ref, *rest):
    slabs, per_device = q_ref.shape[:2]
    pieces, (out_ref, scores, *held, kv_s) = rest[:-13], rest[-13:]
    kv_ref = in_order(pieces, kv_s, head_ref[1])
    copies, shared = out_ref.shape[0], kv_ref.shape[1]
    for n in range(per_device):
        head = head_ref[0] + n
        mix, bonus = settings_of(head, mix_ref, bonus_ref)
        fade = fade_ref[pl.ds(head, 1), :]
        down, up = split2(down_ref[head]), split2(up_ref[head])
        group = n * shared // per_device
        refs = (
            lambda c, n=n: q_ref[c, n],
            lambda c, group=group: kv_ref[c, group, 0],
            lambda c, group=group: kv_ref[c, group, 1],
        )
        worst = decay_phase(refs[0], down, up, fade, mix, *held[1:4], math.gcd(4, slabs))
        teacher_phase(*refs, held[0], scores)
        safe = jnp.max(worst) <= SAFE_EXPONENT

        def finish(fast, unroll):
            grads = student_phase(fast, refs, mix, bonus, down, up, held, unroll).astype(bf16)

            def copy_out(at, _):
                out_ref[at, n] = grads
                return 0

            lax.fori_loop(0, copies, copy_out, 0)

        @pl.when(safe)
        def _():
            finish(True, math.gcd(8, slabs))

        @pl.when(jnp.logical_not(safe))
        def _():
            finish(False, 1)


def head_grads(q, pieces, place, mix, fade, down_t, up, bonus, copies):
    slabs, per_device, slab, width = q.shape
    rank = up.shape[1]
    packed_rows = 2 * rank + PACK_TAIL
    k_slabs = math.gcd(4, slabs)
    small = slabs <= 16
    q_slabs = k_slabs if small else 1
    kv_shape = (slabs, *pieces[0].shape[1:]) if len(pieces) > 1 else (1, 16, width)
    vmem = pl.BlockSpec(memory_space=pltpu.VMEM)
    return pl.pallas_call(
        head_kernel,
        out_shape=jax.ShapeDtypeStruct((copies, per_device, packed_rows, width), bf16),
        in_specs=[pl.BlockSpec(memory_space=pltpu.SMEM)] + [vmem] * (6 + len(pieces)),
        out_specs=vmem,
        scratch_shapes=[
            pltpu.VMEM((slabs // k_slabs, q_slabs * slab, k_slabs * slab), f32),
            pltpu.VMEM((slabs, slab, width), bf16),
            pltpu.VMEM((slabs, slab, width), f32),
            pltpu.VMEM((slabs, slab, width), f32),
            pltpu.VMEM((slabs, slab, rank), f32),
            pltpu.VMEM((slabs, width, width), f32),
            pltpu.VMEM((slabs, slab, width), f32),
            pltpu.VMEM((slabs, slab, 2 * slab), bf16),
            pltpu.VMEM((slabs, slab, 2 * width), bf16),
            pltpu.VMEM((slabs, slab, 2 * width), bf16),
            pltpu.VMEM((slabs, slab, 2 * width), bf16),
            pltpu.VMEM(kv_shape, bf16),
        ],
        compiler_params=pltpu.CompilerParams(
            vmem_limit_bytes=(36 if small else 60) * 1024 * 1024
        ),
    )(place, q, mix, fade, down_t, up, bonus, *pieces)


def pack_queries(q_ref, out_ref):
    slots, _, width = out_ref.shape
    heads = q_ref.shape[1] // width
    for slot in range(slots):
        head = slot * heads // slots
        out_ref[slot] = q_ref[:, head * width : (head + 1) * width]


def pack_memory(groups_ref, k_ref, v_ref, *out_refs):
    width = out_refs[0].shape[-1]
    for n, out_ref in enumerate(out_refs):
        columns = pl.ds(pl.multiple_of(groups_ref[n] * width, width), width)
        out_ref[0, 0, 0] = k_ref[:, columns]
        out_ref[0, 0, 1] = v_ref[:, columns]


def unpack_kernel(place_ref, *refs):
    *pieces, mix_ref, decay_ref, down_ref, up_ref, bonus_ref = refs
    heads, rank, _ = up_ref.shape
    for n in range(heads):
        if len(pieces) == 1:
            head, packed = n, pieces[0][n * (pieces[0].shape[0] // heads)]
        else:
            near = len(pieces)
            head, packed = place_ref[0] ^ n, pieces[n % near][n // near, 0]
        packed = packed.astype(f32)
        up_ref[head] = packed[:rank]
        down_ref[head] = packed[rank : 2 * rank]
        tail = packed[2 * rank :]
        tail = tail[:6] + tail[6:12]
        for at in range(4):
            mix_ref[at, pl.ds(head, 1), :] = tail[at : at + 1]
        decay_ref[pl.ds(head, 1), :] = tail[4:5]
        bonus_ref[pl.ds(head, 1), :] = tail[5:6]


def exchanged(x, differing, count):
    return lax.ppermute(x, "seq", [(d, d ^ differing) for d in range(count)])


def by_two_steps(parts, far, near, count):
    got = [parts[0]] + [exchanged(parts[n], n * near, count) for n in range(1, far)]
    got = jnp.concatenate(got, axis=0)
    return [got] + [exchanged(got, n, count) for n in range(1, near)]


def shards(
    probe_vectors,
    mentor_address_vectors,
    mentor_content_vectors,
    previous_position_blend,
    feature_fading_exponent,
    fading_narrowing_matrix,
    fading_widening_matrix,
    diagonal_extra_amount,
):
    slab = probe_vectors.shape[0]
    heads, width, rank = fading_narrowing_matrix.shape
    place = lax.axis_index("seq")
    count = lax.axis_size("seq")
    copies = max(1, count // heads)
    per_device = max(1, heads // count)
    assert heads * copies == per_device * count
    groups = mentor_address_vectors.shape[1] // width
    by_bits = heads == count and count <= 16 and count & (count - 1) == 0 and count % groups == 0
    far, near = groups, count // groups
    vmem = pl.BlockSpec(memory_space=pltpu.VMEM)
    smem = pl.BlockSpec(memory_space=pltpu.SMEM)
    place = place.astype(jnp.int32)
    if by_bits:
        wanted = jnp.bitwise_xor(place // near, jnp.arange(far, dtype=jnp.int32))
        shared = 1
    else:
        shared = max(1, per_device * groups // heads)
        firsts = [(d // copies) * per_device * groups // heads for d in range(count)]
        wanted = jnp.asarray([g + n for g in firsts for n in range(shared)], jnp.int32)
    slot = jax.ShapeDtypeStruct((1, 1, 2, slab, width), bf16)
    kv = pl.pallas_call(
        pack_memory,
        out_shape=[slot] * wanted.shape[0],
        in_specs=[smem, vmem, vmem],
        out_specs=[vmem] * wanted.shape[0],
    )(wanted, mentor_address_vectors, mentor_content_vectors)
    if by_bits:
        pieces = by_two_steps(kv, far, near, count)
    kv, probe_vectors = lax.optimization_barrier((kv, probe_vectors))
    q = pl.pallas_call(
        pack_queries,
        out_shape=jax.ShapeDtypeStruct((heads * copies, slab, width), bf16),
        in_specs=[vmem],
        out_specs=vmem,
    )(probe_vectors)
    q = q.reshape(count, per_device, slab, width)
    q = lax.all_to_all(q, "seq", split_axis=0, concat_axis=0, tiled=True)
    if not by_bits:
        kv = jnp.stack(kv).reshape(count, shared, 2, slab, width)
        pieces = [lax.all_to_all(kv, "seq", split_axis=0, concat_axis=0, tiled=True)]
    packed = head_grads(
        q,
        pieces,
        jnp.stack([(place // copies) * per_device, place]),
        previous_position_blend,
        feature_fading_exponent,
        jnp.swapaxes(fading_narrowing_matrix, 1, 2),
        fading_widening_matrix,
        diagonal_extra_amount,
        1 if by_bits else count,
    )
    if by_bits:
        packed = by_two_steps([packed] * far, far, near, count)
    else:
        packed = lax.all_to_all(packed, "seq", split_axis=0, concat_axis=0, tiled=True)
        packed = [packed.reshape(heads * copies, 2 * rank + PACK_TAIL, width)]
    vector = jax.ShapeDtypeStruct((heads, width), f32)
    matrix = jax.ShapeDtypeStruct((heads, rank, width), f32)
    mix, decay, down_t, up, bonus = pl.pallas_call(
        unpack_kernel,
        out_shape=(
            jax.ShapeDtypeStruct((4, heads, width), f32),
            vector,
            matrix,
            matrix,
            vector,
        ),
        in_specs=[smem] + [vmem] * len(packed),
        out_specs=[vmem] * 5,
    )(place.reshape(1), *packed)
    return mix, decay, jnp.swapaxes(down_t, 1, 2), up, bonus


def solution(mesh):
    return jax.shard_map(
        shards,
        mesh=mesh,
        in_specs=(
            P("seq", "head"),
            P("seq", "head"),
            P("seq", "head"),
            P(None, "head", None),
            P("head", None),
            P("head", None, None),
            P("head", None, None),
            P("head", None),
        ),
        out_specs=(
            P(None, "head", None),
            P("head", None),
            P("head", None, None),
            P("head", None, None),
            P("head", None),
        ),
        check_vma=False,
    )
```

```python
import math

import jax
import jax.numpy as jnp
from jax import lax
from jax.experimental import pallas as pl
from jax.experimental.pallas import tpu as pltpu
from jax.sharding import PartitionSpec as P

NORM_EPS = 0.00064
NEG_LARGE = -1e30
SAFE_EXPONENT = 30.0
PACK_TAIL = 16
LOG2_E = math.log2(math.e)

f32 = jnp.float32
bf16 = jnp.bfloat16

NN = (((1,), (0,)), ((), ()))
NT = (((1,), (1,)), ((), ()))
TN = (((0,), (0,)), ((), ()))


def dot(a, b, dims):
    return lax.dot_general(a, b, dims, preferred_element_type=f32)


def split2(x):
    high = x.astype(bf16)
    return high, (x - high.astype(f32)).astype(bf16)


def split3(x):
    high = x.astype(bf16)
    rest = x - high.astype(f32)
    middle = rest.astype(bf16)
    return high, middle, (rest - middle.astype(f32)).astype(bf16)


def stacked(parts, contracted):
    return jnp.concatenate(parts, axis=contracted)


def dot3(a, b, dims):
    (at,), (bt,) = dims[0]
    return dot(stacked((a[0], a[1], a[0]), at), stacked((b[0], b[0], b[1]), bt), dims)


def dot4(a, b, dims):
    (at,), (bt,) = dims[0]
    return dot(stacked((*a, *a), at), stacked((b[0], b[0], b[1], b[1]), bt), dims)


def twice(parts):
    return tuple(jnp.concatenate([part, part], axis=0) for part in parts)


def side_by_side(x):
    high, low = split2(x)
    return jnp.where(lane_ids(x.shape) < x.shape[1] // 2, high, low)


def rank_deep(parts):
    return jnp.concatenate([parts[0], parts[0], parts[1], jnp.zeros_like(parts[1])], axis=0)


def turned(parts):
    return tuple(part.T for part in parts)


def joined(parts):
    return parts[0].astype(f32) + parts[1].astype(f32)


def sums_of(zero_one, parts):
    return dot(stacked((zero_one,) * len(parts), 1), stacked(parts, 0), NN)


def row_ids(shape):
    return lax.broadcasted_iota(jnp.int32, shape, 0)


def lane_ids(shape):
    return lax.broadcasted_iota(jnp.int32, shape, 1)


def zero_one(condition):
    return jnp.where(condition, 1.0, 0.0).astype(bf16)


def with_shift(at, first, slabs=1):
    now = slabs_of(at, first, slabs).astype(f32)
    last = at(jnp.maximum(first - 1, 0))
    tail = last[last.shape[0] - 16 :].astype(f32)[15:16]
    tail = jnp.where(first > 0, tail, 0.0)
    earlier = jnp.where(row_ids(now.shape) == 0, tail, pltpu.roll(now, 1, 0))
    return now, earlier - now


def slabs_of(at, first, slabs):
    return jnp.concatenate([at(first + n) for n in range(slabs)], axis=0)


def teacher_phase(q_at, k_at, v_at, teach, scores):
    slabs, slab, width = teach.shape
    _, q_rows, k_rows = scores.shape
    q_slabs, k_slabs = q_rows // slab, k_rows // slab
    scale = LOG2_E / math.sqrt(width)

    def q_block(i, _):
        q = slabs_of(q_at, i * q_slabs, q_slabs)
        last = (i * q_slabs + q_slabs - 1) // k_slabs

        def score_block(j, top, edge=False):
            s = dot(q, slabs_of(k_at, j * k_slabs, k_slabs), NT) * scale
            if edge:
                seen = i * q_rows + row_ids(s.shape) >= j * k_rows + lane_ids(s.shape)
                s = jnp.where(seen, s, NEG_LARGE)
            scores[j] = s
            for n in range(k_rows // 128):
                top = jnp.maximum(top, s[:, n * 128 : (n + 1) * 128])
            return top

        top = lax.fori_loop(0, last, score_block, jnp.full((q_rows, 128), NEG_LARGE, f32))
        top = score_block(last, top, True)
        row_top = jnp.max(top, axis=1, keepdims=True)

        def value_block(j, carry):
            total, accum = carry
            p = jnp.exp2(scores[j] - row_top)
            for n in range(k_rows // 128):
                total = total + p[:, n * 128 : (n + 1) * 128]
            return total, accum + dot(p.astype(bf16), slabs_of(v_at, j * k_slabs, k_slabs), NN)

        total, accum = lax.fori_loop(
            0,
            last + 1,
            value_block,
            (jnp.zeros((q_rows, 128), f32), jnp.zeros((q_rows, width), f32)),
        )
        out = accum / jnp.sum(total, axis=1, keepdims=True)
        teach[pl.ds(i * q_slabs, q_slabs)] = out.astype(bf16).reshape(q_slabs, slab, width)
        return 0

    lax.fori_loop(0, slabs // q_slabs, q_block, 0)


def decay_phase(q_at, down, up, fade, mix, lw_s, ex_s, hid_s, in_s, slabs):
    count, slab, width = lw_s.shape
    square = (slab, slab)
    before = zero_one(row_ids(square) > lane_ids(square))

    def block(i, worst):
        first = i * slabs
        q, q_step = with_shift(q_at, first, slabs)
        decay_in = split2(q + mix[3] * q_step)
        hid = jnp.tanh(dot3(decay_in, twice(down), NT))
        hid_parts = side_by_side(hid)
        lw = -jnp.exp(fade + dot(stacked((hid_parts,) * 2, 1), rank_deep(up), NN))
        hid_s[pl.ds(first, slabs)] = hid.reshape(slabs, slab, width)
        for n, part in enumerate((*decay_in, hid_parts)):
            in_s[n, pl.ds(first, slabs)] = part.reshape(slabs, slab, width)
        lw_s[pl.ds(first, slabs)] = lw.reshape(slabs, slab, width)
        for n in range(slabs):
            part = lw[n * slab : (n + 1) * slab]
            ex = sums_of(before, split3(part))
            ex_s[first + n] = ex
            middle = ex[slab // 2 : slab // 2 + 1]
            total = ex[slab - 1 :] + part[slab - 1 :]
            worst = jnp.maximum(worst, jnp.maximum(-middle, middle - total))
        return worst

    return lax.fori_loop(0, count // slabs, block, jnp.zeros((1, width), f32))


def level_parts(level, lw, r, k):
    square = (lw.shape[0], lw.shape[0])
    t, m = row_ids(square), lane_ids(square)
    edge = ((t >> (level + 1)) << (level + 1)) + (1 << level) - 1
    upper = ((t >> level) & 1) == 1
    lower = ((t >> level) & 1) == 0
    span = zero_one((upper & (m > edge) & (m < t)) | (lower & (m > t) & (m <= edge)))
    factor = jnp.exp(sums_of(span, split3(lw)))
    upper_rows = ((row_ids(r.shape) >> level) & 1) == 1
    r_factor = jnp.where(upper_rows, factor, 0.0)
    k_factor = jnp.where(upper_rows, 0.0, factor)
    same = (t >> (level + 1)) == (m >> (level + 1))
    return r_factor, k_factor, split2(r * r_factor), split2(k * k_factor), same, span


def halves(x):
    width = x.shape[1] // 2
    return x[:, :width], x[:, width:]


def student_phase(fast, refs, mix, bonus, down, up, scratch, unroll):
    teach, lw_s, ex_s, hid_s, in_s, state_s, g_s, a_s, r_s, k_s, v_s, kept = scratch
    keep = kept.shape[1] == lw_s.shape[0]
    chunks, slab, width = lw_s.shape
    tokens = chunks * slab
    levels = slab.bit_length() - 1
    square = (slab, slab)
    t, m = row_ids(square), lane_ids(square)
    below = t > m
    after, before = zero_one(t < m), zero_one(below)
    sides = jnp.concatenate([after] * 3 + [before] * 2, axis=1)
    up_twice, down_deep = twice(up), rank_deep(down)
    gain = 2.0 / tokens

    def rows_of(c, again):
        if keep and again:
            return tuple(kept[n, c] for n in range(6))
        steps = []
        rows = []
        for n, at in enumerate(refs):
            now, step = with_shift(at, c)
            rows.append(now + mix[n] * step)
            steps.append(step)
        if keep:
            for n, part in enumerate((*rows, *steps)):
                kept[n, c] = part
        return (*rows, *steps)

    def load(c, again=False):
        r, k, v, q_step, k_step, v_step = rows_of(c, again)
        lw, ex = lw_s[c], ex_s[c]
        total = ex[slab - 1 :] + lw[slab - 1 :]
        if fast:
            middle = ex[slab // 2 : slab // 2 + 1]
            r_factor = jnp.exp(ex - middle)
            k_factor = jnp.exp(middle - ex - lw)
            into, out = jnp.exp(middle), jnp.exp(total - middle)
        else:
            r_factor = jnp.exp(ex)
            k_factor = jnp.exp(sums_of(after, split3(lw)))
            into = out = None
        return q_step, k_step, v_step, r, k, v, lw, total, r_factor, k_factor, into, out

    def scaled(x, by):
        return x if by is None else x * by

    def forward(c, state):
        _, _, _, r, k, v, lw, total, r_factor, k_factor, into, out = load(c)
        rs, ks, vs = split2(r * r_factor), split2(k * k_factor), split2(v)
        if fast:
            a = jnp.where(below, dot3(rs, ks, NT), 0.0)
        else:

            def one_level(level, a):
                _, _, r_part, k_part, block, _ = level_parts(level, lw, r, k)
                return a + jnp.where(block, dot3(r_part, k_part, NT), 0.0)

            a = lax.fori_loop(0, levels, one_level, jnp.zeros(square, f32))
        own = jnp.sum(r * bonus * k, axis=1, keepdims=True)
        a = split2(a)
        state_s[c] = state
        o = own * v + dot3(a, vs, NN) + dot3(rs, split2(scaled(state, into)), NT)
        o = o - jnp.mean(o, axis=1, keepdims=True)
        rate = lax.rsqrt(jnp.mean(o * o, axis=1, keepdims=True) + NORM_EPS)
        normed = o * rate
        g = gain * (normed - teach[c].astype(f32))
        g = g - jnp.mean(g, axis=1, keepdims=True) - normed * jnp.mean(
            g * normed, axis=1, keepdims=True
        )
        g_s[c] = g * rate
        for held, parts in ((a_s, a), (r_s, rs), (k_s, ks), (v_s, vs)):
            held[c] = jnp.concatenate(parts, axis=1)
        return state * jnp.exp(total) + scaled(dot3(turned(vs), ks, NN), out)

    def forward_some(i, state):
        for n in range(unroll):
            state = forward(i * unroll + n, state)
        return state

    lax.fori_loop(0, chunks // unroll, forward_some, jnp.zeros((width, width), f32))

    def backward(c, carry):
        cot, up_sum, down_sum, sums = carry
        q_step, k_step, v_step, r, k, v, lw, total, r_factor, k_factor, into, out = load(c, True)
        a, rs, ks, vs = (halves(held[c]) for held in (a_s, r_s, k_s, v_s))
        g = g_s[c]
        gs = split2(g)
        pair = dot3(gs, vs, NT)
        cot_out = split2(scaled(cot, out))
        state_in = split2(scaled(state_s[c], into))
        k_hat = joined(ks)
        dv = dot3(turned(a), gs, NN) + dot3(ks, cot_out, NT)
        dk = dot3(vs, cot_out, NN)
        from_earlier = k_hat * dk
        dlw = jnp.sum(state_s[c] * jnp.exp(total) * cot, axis=0, keepdims=True)
        if fast:
            pairs = split2(jnp.where(below, pair, 0.0))
            dr = dot(
                stacked((gs[0], gs[1], pairs[0], pairs[1], gs[0], pairs[0], pairs[1]), 1),
                stacked((state_in[0], state_in[0], ks[0], ks[0], state_in[1], ks[1], ks[1]), 0),
                NN,
            )
            dk_in = dot4(turned(pairs), rs, NN)
            k_in = k_hat * dk_in
            from_later = joined(rs) * dr - k_in
            dlw = dlw - k_in
            dr = r_factor * dr
            dk = k_factor * (dk + dk_in)
        else:
            dr = dot3(gs, state_in, NN)
            from_later = joined(rs) * dr
            dr = r_factor * dr
            dk = k_factor * dk

            def one_level(level, parts):
                dr, dk, dlw = parts
                r_by, k_by, r_part, k_part, block, span = level_parts(level, lw, r, k)
                pairs = split2(jnp.where(block & below, pair, 0.0))
                dr_in = r_by * dot3(pairs, k_part, NN)
                dk_in = k_by * dot3(pairs, r_part, TN)
                inside = split3(r * dr_in + k * dk_in)
                return dr + dr_in, dk + dk_in, dlw + sum(dot(span, part, TN) for part in inside)

            dr, dk, dlw = lax.fori_loop(
                0, levels, one_level, (dr, dk, jnp.broadcast_to(dlw, r.shape))
            )
        later, earlier = split3(from_later), split2(from_earlier)
        dlw = dlw + dot(sides, jnp.concatenate([*later, *earlier], axis=0), NN)
        dv = dv + jnp.sum(r * bonus * k, axis=1, keepdims=True) * g
        own = jnp.sum(v * g, axis=1, keepdims=True)
        own_r, own_k = own * r, own * k
        dr = dr + bonus * own_k
        dk = dk + bonus * own_r
        dpre = dlw * lw
        dpres = split2(dpre)
        hid = hid_s[c]
        dz = side_by_side(dot3(dpres, up_twice, NT) * (1.0 - hid * hid))
        dxw = dot(stacked((dz, dz), 1), down_deep, NN)
        hid_t, dz_t = in_s[2, c].T, dz.T
        up_sum = up_sum + dot(stacked((hid_t, hid_t), 1), stacked(dpres, 0), NN)
        down_sum = down_sum + dot(
            stacked((dz_t, dz_t), 1), stacked((in_s[0, c], in_s[1, c]), 0), NN
        )
        parts = (dr * q_step, dk * k_step, dv * v_step, dxw * q_step, dpre, own_r * k)
        sums = tuple(
            old + jnp.sum(new.reshape(slab // 8, 8, width), axis=0)
            for old, new in zip(sums, parts)
        )
        cot = cot * jnp.exp(total) + scaled(dot3(turned(gs), rs, NN), into)
        return cot, up_sum, down_sum, sums

    def backward_some(i, carry):
        for n in range(unroll):
            carry = backward(chunks - 1 - (i * unroll + n), carry)
        return carry

    rank = down[0].shape[0]
    empty = jnp.zeros((2 * rank, width), f32)
    start = (jnp.zeros((width, width), f32), empty, empty, (jnp.zeros((8, width), f32),) * 6)
    _, up_sum, down_sum, sums = lax.fori_loop(0, chunks // unroll, backward_some, start)
    tail = [split2(jnp.sum(part, axis=0, keepdims=True)) for part in sums]
    tail = [high.astype(f32) for high, _ in tail] + [low.astype(f32) for _, low in tail]
    tail.append(jnp.zeros((PACK_TAIL - len(tail), width), f32))
    up_sum, down_sum = (part[:rank] + part[rank:] for part in (up_sum, down_sum))
    return jnp.concatenate([up_sum, down_sum, *tail], axis=0)


def settings_of(head, mix_ref, bonus_ref):
    mix = [mix_ref[n, pl.ds(head, 1), :] for n in range(4)]
    return mix, bonus_ref[pl.ds(head, 1), :]


def in_order(pieces, scratch, place):
    if len(pieces) == 1:
        return pieces[0]
    near = len(pieces)
    for n, piece in enumerate(pieces):
        for far in range(piece.shape[0]):
            scratch[place ^ (far * near + n)] = piece[far]
    return scratch


def head_kernel(head_ref, q_ref, mix_ref, fade_ref, down_ref, up_ref, bonus_ref, *rest):
    slabs, per_device = q_ref.shape[:2]
    pieces, (out_ref, scores, *held, kv_s) = rest[:-15], rest[-15:]
    kv_ref = in_order(pieces, kv_s, head_ref[1])
    copies, shared = out_ref.shape[0], kv_ref.shape[1]
    for n in range(per_device):
        head = head_ref[0] + n
        mix, bonus = settings_of(head, mix_ref, bonus_ref)
        fade = fade_ref[pl.ds(head, 1), :]
        down, up = split2(down_ref[head]), split2(up_ref[head])
        group = n * shared // per_device
        refs = (
            lambda c, n=n: q_ref[c, n],
            lambda c, group=group: kv_ref[c, group, 0],
            lambda c, group=group: kv_ref[c, group, 1],
        )
        worst = decay_phase(refs[0], down, up, fade, mix, *held[1:5], math.gcd(4, slabs))
        teacher_phase(*refs, held[0], scores)
        safe = jnp.max(worst) <= SAFE_EXPONENT

        def finish(fast, unroll):
            grads = student_phase(fast, refs, mix, bonus, down, up, held, unroll).astype(bf16)

            def copy_out(at, _):
                out_ref[at, n] = grads
                return 0

            lax.fori_loop(0, copies, copy_out, 0)

        @pl.when(safe)
        def _():
            finish(True, math.gcd(4, slabs))

        @pl.when(jnp.logical_not(safe))
        def _():
            finish(False, 1)


def head_grads(q, pieces, place, mix, fade, down_t, up, bonus, copies):
    slabs, per_device, slab, width = q.shape
    rank = up.shape[1]
    assert 2 * rank == width
    packed_rows = 2 * rank + PACK_TAIL
    k_slabs = math.gcd(4, slabs)
    small = slabs <= 16
    q_slabs = k_slabs if small else 1
    kv_shape = (slabs, *pieces[0].shape[1:]) if len(pieces) > 1 else (1, 16, width)
    vmem = pl.BlockSpec(memory_space=pltpu.VMEM)
    return pl.pallas_call(
        head_kernel,
        out_shape=jax.ShapeDtypeStruct((copies, per_device, packed_rows, width), bf16),
        in_specs=[pl.BlockSpec(memory_space=pltpu.SMEM)] + [vmem] * (6 + len(pieces)),
        out_specs=vmem,
        scratch_shapes=[
            pltpu.VMEM((slabs // k_slabs, q_slabs * slab, k_slabs * slab), f32),
            pltpu.VMEM((slabs, slab, width), bf16),
            pltpu.VMEM((slabs, slab, width), f32),
            pltpu.VMEM((slabs, slab, width), f32),
            pltpu.VMEM((slabs, slab, 2 * rank), f32),
            pltpu.VMEM((3, slabs, slab, width), bf16),
            pltpu.VMEM((slabs, width, width), f32),
            pltpu.VMEM((slabs, slab, width), f32),
            pltpu.VMEM((slabs, slab, 2 * slab), bf16),
            pltpu.VMEM((slabs, slab, 2 * width), bf16),
            pltpu.VMEM((slabs, slab, 2 * width), bf16),
            pltpu.VMEM((slabs, slab, 2 * width), bf16),
            pltpu.VMEM((6, slabs if small else 1, slab, width), f32),
            pltpu.VMEM(kv_shape, bf16),
        ],
        compiler_params=pltpu.CompilerParams(
            vmem_limit_bytes=(40 if small else 60) * 1024 * 1024
        ),
    )(place, q, mix, fade, down_t, up, bonus, *pieces)


def pack_queries(q_ref, out_ref):
    slots, _, width = out_ref.shape
    heads = q_ref.shape[1] // width
    for slot in range(slots):
        head = slot * heads // slots
        out_ref[slot] = q_ref[:, head * width : (head + 1) * width]


def pack_memory(groups_ref, k_ref, v_ref, *out_refs):
    width = out_refs[0].shape[-1]
    for n, out_ref in enumerate(out_refs):
        columns = pl.ds(pl.multiple_of(groups_ref[n] * width, width), width)
        out_ref[0, 0, 0] = k_ref[:, columns]
        out_ref[0, 0, 1] = v_ref[:, columns]


def unpack_kernel(place_ref, *refs):
    *pieces, mix_ref, decay_ref, down_ref, up_ref, bonus_ref = refs
    heads, rank, _ = up_ref.shape
    for n in range(heads):
        if len(pieces) == 1:
            head, packed = n, pieces[0][n * (pieces[0].shape[0] // heads)]
        else:
            near = len(pieces)
            head, packed = place_ref[0] ^ n, pieces[n % near][n // near, 0]
        packed = packed.astype(f32)
        up_ref[head] = packed[:rank]
        down_ref[head] = packed[rank : 2 * rank]
        tail = packed[2 * rank :]
        tail = tail[:6] + tail[6:12]
        for at in range(4):
            mix_ref[at, pl.ds(head, 1), :] = tail[at : at + 1]
        decay_ref[pl.ds(head, 1), :] = tail[4:5]
        bonus_ref[pl.ds(head, 1), :] = tail[5:6]


def exchanged(x, differing, count):
    return lax.ppermute(x, "seq", [(d, d ^ differing) for d in range(count)])


def first_step(parts, near, count):
    got = [exchanged(part, n * near, count) if n else part for n, part in enumerate(parts)]
    return jnp.concatenate(got, axis=0)


def second_step(got, near, count):
    return [exchanged(got, n, count) if n else got for n in range(near)]


def shards(
    probe_vectors,
    mentor_address_vectors,
    mentor_content_vectors,
    previous_position_blend,
    feature_fading_exponent,
    fading_narrowing_matrix,
    fading_widening_matrix,
    diagonal_extra_amount,
):
    slab = probe_vectors.shape[0]
    heads, width, rank = fading_narrowing_matrix.shape
    place = lax.axis_index("seq")
    count = lax.axis_size("seq")
    copies = max(1, count // heads)
    per_device = max(1, heads // count)
    assert heads * copies == per_device * count
    groups = mentor_address_vectors.shape[1] // width
    by_bits = heads == count and count <= 16 and count & (count - 1) == 0 and count % groups == 0
    far, near = groups, count // groups
    vmem = pl.BlockSpec(memory_space=pltpu.VMEM)
    smem = pl.BlockSpec(memory_space=pltpu.SMEM)
    place = place.astype(jnp.int32)
    if by_bits:
        wanted = jnp.bitwise_xor(place // near, jnp.arange(far, dtype=jnp.int32))
        shared = 1
    else:
        shared = max(1, per_device * groups // heads)
        firsts = [(d // copies) * per_device * groups // heads for d in range(count)]
        wanted = jnp.asarray([g + n for g in firsts for n in range(shared)], jnp.int32)
    slot = jax.ShapeDtypeStruct((1, 1, 2, slab, width), bf16)
    kv = pl.pallas_call(
        pack_memory,
        out_shape=[slot] * wanted.shape[0],
        in_specs=[smem, vmem, vmem],
        out_specs=[vmem] * wanted.shape[0],
    )(wanted, mentor_address_vectors, mentor_content_vectors)
    if by_bits:
        kv, probe_vectors = lax.optimization_barrier((kv, probe_vectors))
        kv = first_step(kv, near, count)
    q = pl.pallas_call(
        pack_queries,
        out_shape=jax.ShapeDtypeStruct((heads * copies, slab, width), bf16),
        in_specs=[vmem],
        out_specs=vmem,
    )(probe_vectors)
    q = q.reshape(count, per_device, slab, width)
    if by_bits:
        kv, q = lax.optimization_barrier((kv, q))
        pieces = second_step(kv, near, count)
    q = lax.all_to_all(q, "seq", split_axis=0, concat_axis=0, tiled=True)
    if not by_bits:
        kv = jnp.stack(kv).reshape(count, shared, 2, slab, width)
        pieces = [lax.all_to_all(kv, "seq", split_axis=0, concat_axis=0, tiled=True)]
    packed = head_grads(
        q,
        pieces,
        jnp.stack([(place // copies) * per_device, place]),
        previous_position_blend,
        feature_fading_exponent,
        jnp.swapaxes(fading_narrowing_matrix, 1, 2),
        fading_widening_matrix,
        diagonal_extra_amount,
        1 if by_bits else count,
    )
    if by_bits:
        packed = second_step(first_step([packed] * far, near, count), near, count)
    else:
        packed = lax.all_to_all(packed, "seq", split_axis=0, concat_axis=0, tiled=True)
        packed = [packed.reshape(heads * copies, 2 * rank + PACK_TAIL, width)]
    vector = jax.ShapeDtypeStruct((heads, width), f32)
    matrix = jax.ShapeDtypeStruct((heads, rank, width), f32)
    mix, decay, down_t, up, bonus = pl.pallas_call(
        unpack_kernel,
        out_shape=(
            jax.ShapeDtypeStruct((4, heads, width), f32),
            vector,
            matrix,
            matrix,
            vector,
        ),
        in_specs=[smem] + [vmem] * len(packed),
        out_specs=[vmem] * 5,
    )(place.reshape(1), *packed)
    return mix, decay, jnp.swapaxes(down_t, 1, 2), up, bonus


def solution(mesh):
    return jax.shard_map(
        shards,
        mesh=mesh,
        in_specs=(
            P("seq", "head"),
            P("seq", "head"),
            P("seq", "head"),
            P(None, "head", None),
            P("head", None),
            P("head", None, None),
            P("head", None, None),
            P("head", None),
        ),
        out_specs=(
            P(None, "head", None),
            P("head", None),
            P("head", None, None),
            P("head", None, None),
            P("head", None),
        ),
        check_vma=False,
    )
```

```python
import math

import jax
import jax.numpy as jnp
from jax import lax
from jax.experimental import pallas as pl
from jax.experimental.pallas import tpu as pltpu
from jax.sharding import PartitionSpec as P

NORM_EPS = 0.00064
NEG_LARGE = -1e30
SAFE_EXPONENT = 30.0
PACK_TAIL = 16
LOG2_E = math.log2(math.e)

f32 = jnp.float32
bf16 = jnp.bfloat16

NN = (((1,), (0,)), ((), ()))
NT = (((1,), (1,)), ((), ()))
TN = (((0,), (0,)), ((), ()))


def dot(a, b, dims):
    return lax.dot_general(a, b, dims, preferred_element_type=f32)


def split2(x):
    high = x.astype(bf16)
    return high, (x - high.astype(f32)).astype(bf16)


def split3(x):
    high = x.astype(bf16)
    rest = x - high.astype(f32)
    middle = rest.astype(bf16)
    return high, middle, (rest - middle.astype(f32)).astype(bf16)


def stacked(parts, contracted):
    return jnp.concatenate(parts, axis=contracted)


def dot3(a, b, dims):
    (at,), (bt,) = dims[0]
    return dot(stacked((a[0], a[1], a[0]), at), stacked((b[0], b[0], b[1]), bt), dims)


def dot4(a, b, dims):
    (at,), (bt,) = dims[0]
    return dot(stacked((*a, *a), at), stacked((b[0], b[0], b[1], b[1]), bt), dims)


def twice(parts):
    return tuple(jnp.concatenate([part, part], axis=0) for part in parts)


def side_by_side(x):
    high, low = split2(x)
    return jnp.where(lane_ids(x.shape) < x.shape[1] // 2, high, low)


def rank_deep(parts):
    return jnp.concatenate([parts[0], parts[0], parts[1], jnp.zeros_like(parts[1])], axis=0)


def turned(parts):
    return tuple(part.T for part in parts)


def joined(parts):
    return parts[0].astype(f32) + parts[1].astype(f32)


def sums_of(zero_one, parts):
    return dot(stacked((zero_one,) * len(parts), 1), stacked(parts, 0), NN)


def row_ids(shape):
    return lax.broadcasted_iota(jnp.int32, shape, 0)


def lane_ids(shape):
    return lax.broadcasted_iota(jnp.int32, shape, 1)


def zero_one(condition):
    return jnp.where(condition, 1.0, 0.0).astype(bf16)


def with_shift(at, first, slabs=1):
    now = slabs_of(at, first, slabs).astype(f32)
    last = at(jnp.maximum(first - 1, 0))
    tail = last[last.shape[0] - 16 :].astype(f32)[15:16]
    tail = jnp.where(first > 0, tail, 0.0)
    earlier = jnp.where(row_ids(now.shape) == 0, tail, pltpu.roll(now, 1, 0))
    return now, earlier - now


def slabs_of(at, first, slabs):
    return jnp.concatenate([at(first + n) for n in range(slabs)], axis=0)


def teacher_phase(q_at, k_at, v_at, teach, scores):
    slabs, slab, width = teach.shape
    _, q_rows, k_rows = scores.shape
    q_slabs, k_slabs = q_rows // slab, k_rows // slab
    scale = LOG2_E / math.sqrt(width)

    def q_block(i, _):
        q = slabs_of(q_at, i * q_slabs, q_slabs)
        last = (i * q_slabs + q_slabs - 1) // k_slabs

        def score_block(j, top, edge=False):
            s = dot(q, slabs_of(k_at, j * k_slabs, k_slabs), NT) * scale
            if edge:
                seen = i * q_rows + row_ids(s.shape) >= j * k_rows + lane_ids(s.shape)
                s = jnp.where(seen, s, NEG_LARGE)
            scores[j] = s
            for n in range(k_rows // 128):
                top = jnp.maximum(top, s[:, n * 128 : (n + 1) * 128])
            return top

        top = lax.fori_loop(0, last, score_block, jnp.full((q_rows, 128), NEG_LARGE, f32))
        top = score_block(last, top, True)
        row_top = jnp.max(top, axis=1, keepdims=True)

        def value_block(j, carry):
            total, accum = carry
            p = jnp.exp2(scores[j] - row_top)
            for n in range(k_rows // 128):
                total = total + p[:, n * 128 : (n + 1) * 128]
            return total, accum + dot(p.astype(bf16), slabs_of(v_at, j * k_slabs, k_slabs), NN)

        total, accum = lax.fori_loop(
            0,
            last + 1,
            value_block,
            (jnp.zeros((q_rows, 128), f32), jnp.zeros((q_rows, width), f32)),
        )
        out = accum / jnp.sum(total, axis=1, keepdims=True)
        teach[pl.ds(i * q_slabs, q_slabs)] = out.astype(bf16).reshape(q_slabs, slab, width)
        return 0

    lax.fori_loop(0, slabs // q_slabs, q_block, 0)


def decay_phase(q_at, down, up, fade, mix, lw_s, ex_s, hid_s, in_s, slabs):
    count, slab, width = lw_s.shape
    square = (slab, slab)
    before = zero_one(row_ids(square) > lane_ids(square))

    def block(i, worst):
        first = i * slabs
        q, q_step = with_shift(q_at, first, slabs)
        decay_in = split2(q + mix[3] * q_step)
        hid = jnp.tanh(dot3(decay_in, twice(down), NT))
        hid_parts = side_by_side(hid)
        lw = -jnp.exp(fade + dot(stacked((hid_parts,) * 2, 1), rank_deep(up), NN))
        hid_s[pl.ds(first, slabs)] = hid.reshape(slabs, slab, width)
        for n, part in enumerate((*decay_in, hid_parts)):
            in_s[n, pl.ds(first, slabs)] = part.reshape(slabs, slab, width)
        lw_s[pl.ds(first, slabs)] = lw.reshape(slabs, slab, width)
        for n in range(slabs):
            part = lw[n * slab : (n + 1) * slab]
            ex = sums_of(before, split3(part))
            ex_s[first + n] = ex
            middle = ex[slab // 2 : slab // 2 + 1]
            total = ex[slab - 1 :] + part[slab - 1 :]
            worst = jnp.maximum(worst, jnp.maximum(-middle, middle - total))
        return worst

    return lax.fori_loop(0, count // slabs, block, jnp.zeros((1, width), f32))


def level_parts(level, lw, r, k):
    square = (lw.shape[0], lw.shape[0])
    t, m = row_ids(square), lane_ids(square)
    edge = ((t >> (level + 1)) << (level + 1)) + (1 << level) - 1
    upper = ((t >> level) & 1) == 1
    lower = ((t >> level) & 1) == 0
    span = zero_one((upper & (m > edge) & (m < t)) | (lower & (m > t) & (m <= edge)))
    factor = jnp.exp(sums_of(span, split3(lw)))
    upper_rows = ((row_ids(r.shape) >> level) & 1) == 1
    r_factor = jnp.where(upper_rows, factor, 0.0)
    k_factor = jnp.where(upper_rows, 0.0, factor)
    same = (t >> (level + 1)) == (m >> (level + 1))
    return r_factor, k_factor, split2(r * r_factor), split2(k * k_factor), same, span


def halves(x):
    width = x.shape[1] // 2
    return x[:, :width], x[:, width:]


def in_step(chunks):
    chunks = list(chunks)
    while chunks:
        chunks = [chunk for chunk in chunks if next(chunk, chunk) is None]


def student_phase(fast, refs, mix, bonus, down, up, scratch, unroll):
    teach, lw_s, ex_s, hid_s, in_s, state_s, g_s, a_s, r_s, k_s, v_s, kept = scratch
    keep = kept.shape[1] == lw_s.shape[0]
    chunks, slab, width = lw_s.shape
    tokens = chunks * slab
    levels = slab.bit_length() - 1
    square = (slab, slab)
    t, m = row_ids(square), lane_ids(square)
    below = t > m
    after, before = zero_one(t < m), zero_one(below)
    sides = jnp.concatenate([after] * 3 + [before] * 2, axis=1)
    up_twice, down_deep = twice(up), rank_deep(down)
    gain = 2.0 / tokens

    def rows_of(c, again):
        if keep and again:
            return tuple(kept[n, c] for n in range(6))
        steps = []
        rows = []
        for n, at in enumerate(refs):
            now, step = with_shift(at, c)
            rows.append(now + mix[n] * step)
            steps.append(step)
        if keep:
            for n, part in enumerate((*rows, *steps)):
                kept[n, c] = part
        return (*rows, *steps)

    def load(c, again=False):
        r, k, v, q_step, k_step, v_step = rows_of(c, again)
        lw, ex = lw_s[c], ex_s[c]
        total = ex[slab - 1 :] + lw[slab - 1 :]
        if fast:
            middle = ex[slab // 2 : slab // 2 + 1]
            r_factor = jnp.exp(ex - middle)
            k_factor = jnp.exp(middle - ex - lw)
            into, out = jnp.exp(middle), jnp.exp(total - middle)
        else:
            r_factor = jnp.exp(ex)
            k_factor = jnp.exp(sums_of(after, split3(lw)))
            into = out = None
        return q_step, k_step, v_step, r, k, v, lw, total, r_factor, k_factor, into, out

    def scaled(x, by):
        return x if by is None else x * by

    def forward(c, carry):
        _, _, _, r, k, v, lw, total, r_factor, k_factor, into, out = load(c)
        rs, ks, vs = split2(r * r_factor), split2(k * k_factor), split2(v)
        yield
        memory = dot3(turned(vs), ks, NN)
        if fast:
            a = dot3(rs, ks, NT)
        else:

            def one_level(level, a):
                _, _, r_part, k_part, block, _ = level_parts(level, lw, r, k)
                return a + jnp.where(block, dot3(r_part, k_part, NT), 0.0)

            a = lax.fori_loop(0, levels, one_level, jnp.zeros(square, f32))
        yield
        own = jnp.sum(r * bonus * k, axis=1, keepdims=True)
        a = split2(jnp.where(below, a, 0.0) if fast else a)
        state = carry["state"]
        carry["state"] = state * jnp.exp(total) + scaled(memory, out)
        state_in = split2(scaled(state, into))
        yield
        o = own * v + dot3(a, vs, NN) + dot3(rs, state_in, NT)
        yield
        o = o - jnp.mean(o, axis=1, keepdims=True)
        yield
        rate = lax.rsqrt(jnp.mean(o * o, axis=1, keepdims=True) + NORM_EPS)
        normed = o * rate
        g = gain * (normed - teach[c].astype(f32))
        yield
        g = g - jnp.mean(g, axis=1, keepdims=True) - normed * jnp.mean(
            g * normed, axis=1, keepdims=True
        )
        yield
        state_s[c] = state
        g_s[c] = g * rate
        for held, parts in ((a_s, a), (r_s, rs), (k_s, ks), (v_s, vs)):
            held[c] = jnp.concatenate(parts, axis=1)

    def forward_some(i, state):
        carry = {"state": state}
        in_step(forward(i * unroll + n, carry) for n in range(unroll))
        return carry["state"]

    lax.fori_loop(0, chunks // unroll, forward_some, jnp.zeros((width, width), f32))

    def backward(c, carry):
        q_step, k_step, v_step, r, k, v, lw, total, r_factor, k_factor, into, out = load(c, True)
        a, rs, ks, vs = (halves(held[c]) for held in (a_s, r_s, k_s, v_s))
        g = g_s[c]
        gs = split2(g)
        yield
        memory = dot3(turned(gs), rs, NN)
        pair = dot3(gs, vs, NT)
        yield
        cot = carry["cot"]
        carry["cot"] = cot * jnp.exp(total) + scaled(memory, into)
        cot_out = split2(scaled(cot, out))
        state = state_s[c]
        state_in = split2(scaled(state, into))
        dlw = jnp.sum(state * jnp.exp(total) * cot, axis=0, keepdims=True)
        if fast:
            pairs = split2(jnp.where(below, pair, 0.0))
        yield
        dv = dot3(turned(a), gs, NN) + dot3(ks, cot_out, NT)
        dk = dot3(vs, cot_out, NN)
        if fast:
            dr = dot(
                stacked((gs[0], gs[1], pairs[0], pairs[1], gs[0], pairs[0], pairs[1]), 1),
                stacked((state_in[0], state_in[0], ks[0], ks[0], state_in[1], ks[1], ks[1]), 0),
                NN,
            )
            dk_in = dot4(turned(pairs), rs, NN)
            yield
            k_hat = joined(ks)
            from_earlier = k_hat * dk
            k_in = k_hat * dk_in
            from_later = joined(rs) * dr - k_in
            dlw = dlw - k_in
            dr = r_factor * dr
            dk = k_factor * (dk + dk_in)
        else:
            dr = dot3(gs, state_in, NN)
            from_earlier = joined(ks) * dk
            from_later = joined(rs) * dr
            dr = r_factor * dr
            dk = k_factor * dk

            def one_level(level, parts):
                dr, dk, dlw = parts
                r_by, k_by, r_part, k_part, block, span = level_parts(level, lw, r, k)
                pairs = split2(jnp.where(block & below, pair, 0.0))
                dr_in = r_by * dot3(pairs, k_part, NN)
                dk_in = k_by * dot3(pairs, r_part, TN)
                inside = split3(r * dr_in + k * dk_in)
                return dr + dr_in, dk + dk_in, dlw + sum(dot(span, part, TN) for part in inside)

            dr, dk, dlw = lax.fori_loop(
                0, levels, one_level, (dr, dk, jnp.broadcast_to(dlw, r.shape))
            )
        later, earlier = split3(from_later), split2(from_earlier)
        yield
        dlw = dlw + dot(sides, jnp.concatenate([*later, *earlier], axis=0), NN)
        dv = dv + jnp.sum(r * bonus * k, axis=1, keepdims=True) * g
        own = jnp.sum(v * g, axis=1, keepdims=True)
        yield
        own_r, own_k = own * r, own * k
        dr = dr + bonus * own_k
        dk = dk + bonus * own_r
        dpre = dlw * lw
        dpres = split2(dpre)
        yield
        hid = hid_s[c]
        dz = dot3(dpres, up_twice, NT)
        hid_t = in_s[2, c].T
        carry["up"] += dot(stacked((hid_t, hid_t), 1), stacked(dpres, 0), NN)
        yield
        dz = side_by_side(dz * (1.0 - hid * hid))
        yield
        dxw = dot(stacked((dz, dz), 1), down_deep, NN)
        dz_t = dz.T
        carry["down"] += dot(
            stacked((dz_t, dz_t), 1), stacked((in_s[0, c], in_s[1, c]), 0), NN
        )
        yield
        parts = (dr * q_step, dk * k_step, dv * v_step, dxw * q_step, dpre, own_r * k)
        carry["sums"] = tuple(
            old + jnp.sum(new.reshape(slab // 8, 8, width), axis=0)
            for old, new in zip(carry["sums"], parts)
        )

    def backward_some(i, carry):
        carry = dict(zip(("cot", "up", "down", "sums"), carry))
        in_step(backward(chunks - 1 - (i * unroll + n), carry) for n in range(unroll))
        return tuple(carry.values())

    rank = down[0].shape[0]
    empty = jnp.zeros((2 * rank, width), f32)
    start = (jnp.zeros((width, width), f32), empty, empty, (jnp.zeros((8, width), f32),) * 6)
    _, up_sum, down_sum, sums = lax.fori_loop(0, chunks // unroll, backward_some, start)
    tail = [split2(jnp.sum(part, axis=0, keepdims=True)) for part in sums]
    tail = [high.astype(f32) for high, _ in tail] + [low.astype(f32) for _, low in tail]
    tail.append(jnp.zeros((PACK_TAIL - len(tail), width), f32))
    up_sum, down_sum = (part[:rank] + part[rank:] for part in (up_sum, down_sum))
    return jnp.concatenate([up_sum, down_sum, *tail], axis=0)


def settings_of(head, mix_ref, bonus_ref):
    mix = [mix_ref[n, pl.ds(head, 1), :] for n in range(4)]
    return mix, bonus_ref[pl.ds(head, 1), :]


def in_order(pieces, scratch, place):
    if len(pieces) == 1:
        return pieces[0]
    near = len(pieces)
    for n, piece in enumerate(pieces):
        for far in range(piece.shape[0]):
            scratch[place ^ (far * near + n)] = piece[far]
    return scratch


def head_kernel(head_ref, q_ref, mix_ref, fade_ref, down_ref, up_ref, bonus_ref, *rest):
    slabs, per_device = q_ref.shape[:2]
    pieces, (out_ref, scores, *held, kv_s) = rest[:-15], rest[-15:]
    kv_ref = in_order(pieces, kv_s, head_ref[1])
    copies, shared = out_ref.shape[0], kv_ref.shape[1]
    for n in range(per_device):
        head = head_ref[0] + n
        mix, bonus = settings_of(head, mix_ref, bonus_ref)
        fade = fade_ref[pl.ds(head, 1), :]
        down, up = split2(down_ref[head]), split2(up_ref[head])
        group = n * shared // per_device
        refs = (
            lambda c, n=n: q_ref[c, n],
            lambda c, group=group: kv_ref[c, group, 0],
            lambda c, group=group: kv_ref[c, group, 1],
        )
        worst = decay_phase(refs[0], down, up, fade, mix, *held[1:5], math.gcd(4, slabs))
        teacher_phase(*refs, held[0], scores)
        safe = jnp.max(worst) <= SAFE_EXPONENT

        def finish(fast, unroll):
            grads = student_phase(fast, refs, mix, bonus, down, up, held, unroll).astype(bf16)

            def copy_out(at, _):
                out_ref[at, n] = grads
                return 0

            lax.fori_loop(0, copies, copy_out, 0)

        @pl.when(safe)
        def _():
            finish(True, math.gcd(4, slabs))

        @pl.when(jnp.logical_not(safe))
        def _():
            finish(False, 1)


def head_grads(q, pieces, place, mix, fade, down_t, up, bonus, copies):
    slabs, per_device, slab, width = q.shape
    rank = up.shape[1]
    assert 2 * rank == width
    packed_rows = 2 * rank + PACK_TAIL
    k_slabs = math.gcd(4, slabs)
    small = slabs <= 16
    q_slabs = k_slabs if small else 1
    kv_shape = (slabs, *pieces[0].shape[1:]) if len(pieces) > 1 else (1, 16, width)
    vmem = pl.BlockSpec(memory_space=pltpu.VMEM)
    return pl.pallas_call(
        head_kernel,
        out_shape=jax.ShapeDtypeStruct((copies, per_device, packed_rows, width), bf16),
        in_specs=[pl.BlockSpec(memory_space=pltpu.SMEM)] + [vmem] * (6 + len(pieces)),
        out_specs=vmem,
        scratch_shapes=[
            pltpu.VMEM((slabs // k_slabs, q_slabs * slab, k_slabs * slab), f32),
            pltpu.VMEM((slabs, slab, width), bf16),
            pltpu.VMEM((slabs, slab, width), f32),
            pltpu.VMEM((slabs, slab, width), f32),
            pltpu.VMEM((slabs, slab, 2 * rank), f32),
            pltpu.VMEM((3, slabs, slab, width), bf16),
            pltpu.VMEM((slabs, width, width), f32),
            pltpu.VMEM((slabs, slab, width), f32),
            pltpu.VMEM((slabs, slab, 2 * slab), bf16),
            pltpu.VMEM((slabs, slab, 2 * width), bf16),
            pltpu.VMEM((slabs, slab, 2 * width), bf16),
            pltpu.VMEM((slabs, slab, 2 * width), bf16),
            pltpu.VMEM((6, slabs if small else 1, slab, width), f32),
            pltpu.VMEM(kv_shape, bf16),
        ],
        compiler_params=pltpu.CompilerParams(
            vmem_limit_bytes=(40 if small else 60) * 1024 * 1024
        ),
    )(place, q, mix, fade, down_t, up, bonus, *pieces)


def pack_queries(q_ref, out_ref):
    slots, _, width = out_ref.shape
    heads = q_ref.shape[1] // width
    for slot in range(slots):
        head = slot * heads // slots
        out_ref[slot] = q_ref[:, head * width : (head + 1) * width]


def pack_memory(groups_ref, k_ref, v_ref, *out_refs):
    width = out_refs[0].shape[-1]
    for n, out_ref in enumerate(out_refs):
        columns = pl.ds(pl.multiple_of(groups_ref[n] * width, width), width)
        out_ref[0, 0, 0] = k_ref[:, columns]
        out_ref[0, 0, 1] = v_ref[:, columns]


def unpack_kernel(place_ref, *refs):
    *pieces, mix_ref, decay_ref, down_ref, up_ref, bonus_ref = refs
    heads, rank, _ = up_ref.shape
    for n in range(heads):
        if len(pieces) == 1:
            head, packed = n, pieces[0][n * (pieces[0].shape[0] // heads)]
        else:
            near = len(pieces)
            head, packed = place_ref[0] ^ n, pieces[n % near][n // near, 0]
        packed = packed.astype(f32)
        up_ref[head] = packed[:rank]
        down_ref[head] = packed[rank : 2 * rank]
        tail = packed[2 * rank :]
        tail = tail[:6] + tail[6:12]
        for at in range(4):
            mix_ref[at, pl.ds(head, 1), :] = tail[at : at + 1]
        decay_ref[pl.ds(head, 1), :] = tail[4:5]
        bonus_ref[pl.ds(head, 1), :] = tail[5:6]


def exchanged(x, differing, count):
    return lax.ppermute(x, "seq", [(d, d ^ differing) for d in range(count)])


def first_step(parts, near, count):
    got = [exchanged(part, n * near, count) if n else part for n, part in enumerate(parts)]
    return jnp.concatenate(got, axis=0)


def second_step(got, near, count):
    return [exchanged(got, n, count) if n else got for n in range(near)]


def shards(
    probe_vectors,
    mentor_address_vectors,
    mentor_content_vectors,
    previous_position_blend,
    feature_fading_exponent,
    fading_narrowing_matrix,
    fading_widening_matrix,
    diagonal_extra_amount,
):
    slab = probe_vectors.shape[0]
    heads, width, rank = fading_narrowing_matrix.shape
    place = lax.axis_index("seq")
    count = lax.axis_size("seq")
    copies = max(1, count // heads)
    per_device = max(1, heads // count)
    assert heads * copies == per_device * count
    groups = mentor_address_vectors.shape[1] // width
    by_bits = heads == count and count <= 16 and count & (count - 1) == 0 and count % groups == 0
    far, near = groups, count // groups
    vmem = pl.BlockSpec(memory_space=pltpu.VMEM)
    smem = pl.BlockSpec(memory_space=pltpu.SMEM)
    place = place.astype(jnp.int32)
    if by_bits:
        wanted = jnp.bitwise_xor(place // near, jnp.arange(far, dtype=jnp.int32))
        shared = 1
    else:
        shared = max(1, per_device * groups // heads)
        firsts = [(d // copies) * per_device * groups // heads for d in range(count)]
        wanted = jnp.asarray([g + n for g in firsts for n in range(shared)], jnp.int32)
    slot = jax.ShapeDtypeStruct((1, 1, 2, slab, width), bf16)
    kv = pl.pallas_call(
        pack_memory,
        out_shape=[slot] * wanted.shape[0],
        in_specs=[smem, vmem, vmem],
        out_specs=[vmem] * wanted.shape[0],
    )(wanted, mentor_address_vectors, mentor_content_vectors)
    if by_bits:
        kv, probe_vectors = lax.optimization_barrier((kv, probe_vectors))
        kv = first_step(kv, near, count)
    q = pl.pallas_call(
        pack_queries,
        out_shape=jax.ShapeDtypeStruct((heads * copies, slab, width), bf16),
        in_specs=[vmem],
        out_specs=vmem,
    )(probe_vectors)
    q = q.reshape(count, per_device, slab, width)
    if by_bits:
        kv, q = lax.optimization_barrier((kv, q))
        pieces = second_step(kv, near, count)
    q = lax.all_to_all(q, "seq", split_axis=0, concat_axis=0, tiled=True)
    if not by_bits:
        kv = jnp.stack(kv).reshape(count, shared, 2, slab, width)
        pieces = [lax.all_to_all(kv, "seq", split_axis=0, concat_axis=0, tiled=True)]
    packed = head_grads(
        q,
        pieces,
        jnp.stack([(place // copies) * per_device, place]),
        previous_position_blend,
        feature_fading_exponent,
        jnp.swapaxes(fading_narrowing_matrix, 1, 2),
        fading_widening_matrix,
        diagonal_extra_amount,
        1 if by_bits else count,
    )
    if by_bits:
        packed = second_step(first_step([packed] * far, near, count), near, count)
    else:
        packed = lax.all_to_all(packed, "seq", split_axis=0, concat_axis=0, tiled=True)
        packed = [packed.reshape(heads * copies, 2 * rank + PACK_TAIL, width)]
    vector = jax.ShapeDtypeStruct((heads, width), f32)
    matrix = jax.ShapeDtypeStruct((heads, rank, width), f32)
    mix, decay, down_t, up, bonus = pl.pallas_call(
        unpack_kernel,
        out_shape=(
            jax.ShapeDtypeStruct((4, heads, width), f32),
            vector,
            matrix,
            matrix,
            vector,
        ),
        in_specs=[smem] + [vmem] * len(packed),
        out_specs=[vmem] * 5,
    )(place.reshape(1), *packed)
    return mix, decay, jnp.swapaxes(down_t, 1, 2), up, bonus


def solution(mesh):
    return jax.shard_map(
        shards,
        mesh=mesh,
        in_specs=(
            P("seq", "head"),
            P("seq", "head"),
            P("seq", "head"),
            P(None, "head", None),
            P("head", None),
            P("head", None, None),
            P("head", None, None),
            P("head", None),
        ),
        out_specs=(
            P(None, "head", None),
            P("head", None),
            P("head", None, None),
            P("head", None, None),
            P("head", None),
        ),
        check_vma=False,
    )
```

```python
import functools
import math

import jax
import jax.numpy as jnp
from jax import lax
from jax.experimental import pallas as pl
from jax.experimental.pallas import tpu as pltpu
from jax.sharding import PartitionSpec as P

NORM_EPS = 0.00064
NEG_LARGE = -1e30
SAFE_EXPONENT = 30.0
PACK_TAIL = 16
LOG2_E = math.log2(math.e)

f32 = jnp.float32
bf16 = jnp.bfloat16

NN = (((1,), (0,)), ((), ()))
NT = (((1,), (1,)), ((), ()))
TN = (((0,), (0,)), ((), ()))


def dot(a, b, dims):
    return lax.dot_general(a, b, dims, preferred_element_type=f32)


def split2(x):
    high = x.astype(bf16)
    return high, (x - high.astype(f32)).astype(bf16)


def split3(x):
    high = x.astype(bf16)
    rest = x - high.astype(f32)
    middle = rest.astype(bf16)
    return high, middle, (rest - middle.astype(f32)).astype(bf16)


def stacked(parts, contracted):
    return jnp.concatenate(parts, axis=contracted)


def dot3(a, b, dims):
    (at,), (bt,) = dims[0]
    return dot(stacked((a[0], a[1], a[0]), at), stacked((b[0], b[0], b[1]), bt), dims)


def dot4(a, b, dims):
    (at,), (bt,) = dims[0]
    return dot(stacked((*a, *a), at), stacked((b[0], b[0], b[1], b[1]), bt), dims)


def twice(parts):
    return tuple(jnp.concatenate([part, part], axis=0) for part in parts)


def side_by_side(x):
    high, low = split2(x)
    return jnp.where(lane_ids(x.shape) < x.shape[1] // 2, high, low)


def rank_deep(parts):
    return jnp.concatenate([parts[0], parts[0], parts[1], jnp.zeros_like(parts[1])], axis=0)


def turned(parts):
    return tuple(part.T for part in parts)


def joined(parts):
    return parts[0].astype(f32) + parts[1].astype(f32)


def sums_of(zero_one, parts):
    return dot(stacked((zero_one,) * len(parts), 1), stacked(parts, 0), NN)


def row_ids(shape):
    return lax.broadcasted_iota(jnp.int32, shape, 0)


def lane_ids(shape):
    return lax.broadcasted_iota(jnp.int32, shape, 1)


def zero_one(condition):
    return jnp.where(condition, 1.0, 0.0).astype(bf16)


def with_shift(at, first, slabs=1):
    now = slabs_of(at, first, slabs).astype(f32)
    last = at(jnp.maximum(first - 1, 0))
    tail = last[last.shape[0] - 16 :].astype(f32)[15:16]
    tail = jnp.where(first > 0, tail, 0.0)
    earlier = jnp.where(row_ids(now.shape) == 0, tail, pltpu.roll(now, 1, 0))
    return now, earlier - now


def slabs_of(at, first, slabs):
    return jnp.concatenate([at(first + n) for n in range(slabs)], axis=0)


def teacher_phase(q_at, k_at, v_at, teach, scores):
    slabs, slab, width = teach.shape
    _, q_rows, k_rows = scores.shape
    q_slabs, k_slabs = q_rows // slab, k_rows // slab
    scale = LOG2_E / math.sqrt(width)

    def q_block(i, _):
        q = slabs_of(q_at, i * q_slabs, q_slabs)
        last = (i * q_slabs + q_slabs - 1) // k_slabs

        def score_block(j, top, edge=False):
            s = dot(q, slabs_of(k_at, j * k_slabs, k_slabs), NT) * scale
            if edge:
                seen = i * q_rows + row_ids(s.shape) >= j * k_rows + lane_ids(s.shape)
                s = jnp.where(seen, s, NEG_LARGE)
            scores[j] = s
            for n in range(k_rows // 128):
                top = jnp.maximum(top, s[:, n * 128 : (n + 1) * 128])
            return top

        top = lax.fori_loop(0, last, score_block, jnp.full((q_rows, 128), NEG_LARGE, f32))
        top = score_block(last, top, True)
        row_top = jnp.max(top, axis=1, keepdims=True)

        def value_block(j, carry):
            total, accum = carry
            p = jnp.exp2(scores[j] - row_top)
            for n in range(k_rows // 128):
                total = total + p[:, n * 128 : (n + 1) * 128]
            return total, accum + dot(p.astype(bf16), slabs_of(v_at, j * k_slabs, k_slabs), NN)

        total, accum = lax.fori_loop(
            0,
            last + 1,
            value_block,
            (jnp.zeros((q_rows, 128), f32), jnp.zeros((q_rows, width), f32)),
        )
        out = accum / jnp.sum(total, axis=1, keepdims=True)
        teach[pl.ds(i * q_slabs, q_slabs)] = out.astype(bf16).reshape(q_slabs, slab, width)
        return 0

    lax.fori_loop(0, slabs // q_slabs, q_block, 0)


def decay_phase(q_at, down, up, fade, mix, lw_s, ex_s, hid_s, in_s, slabs):
    count, slab, width = lw_s.shape
    square = (slab, slab)
    before = zero_one(row_ids(square) > lane_ids(square))

    def block(i, worst):
        first = i * slabs
        q, q_step = with_shift(q_at, first, slabs)
        decay_in = split2(q + mix[3] * q_step)
        hid = jnp.tanh(dot3(decay_in, twice(down), NT))
        hid_parts = side_by_side(hid)
        lw = -jnp.exp(fade + dot(stacked((hid_parts,) * 2, 1), rank_deep(up), NN))
        hid_s[pl.ds(first, slabs)] = hid.reshape(slabs, slab, width)
        for n, part in enumerate((*decay_in, hid_parts)):
            in_s[n, pl.ds(first, slabs)] = part.reshape(slabs, slab, width)
        lw_s[pl.ds(first, slabs)] = lw.reshape(slabs, slab, width)
        for n in range(slabs):
            part = lw[n * slab : (n + 1) * slab]
            ex = sums_of(before, split3(part))
            ex_s[first + n] = ex
            middle = ex[slab // 2 : slab // 2 + 1]
            total = ex[slab - 1 :] + part[slab - 1 :]
            worst = jnp.maximum(worst, jnp.maximum(-middle, middle - total))
        return worst

    return lax.fori_loop(0, count // slabs, block, jnp.zeros((1, width), f32))


def level_parts(level, lw, r, k):
    square = (lw.shape[0], lw.shape[0])
    t, m = row_ids(square), lane_ids(square)
    edge = ((t >> (level + 1)) << (level + 1)) + (1 << level) - 1
    upper = ((t >> level) & 1) == 1
    lower = ((t >> level) & 1) == 0
    span = zero_one((upper & (m > edge) & (m < t)) | (lower & (m > t) & (m <= edge)))
    factor = jnp.exp(sums_of(span, split3(lw)))
    upper_rows = ((row_ids(r.shape) >> level) & 1) == 1
    r_factor = jnp.where(upper_rows, factor, 0.0)
    k_factor = jnp.where(upper_rows, 0.0, factor)
    same = (t >> (level + 1)) == (m >> (level + 1))
    return r_factor, k_factor, split2(r * r_factor), split2(k * k_factor), same, span


def halves(x):
    width = x.shape[1] // 2
    return x[:, :width], x[:, width:]


def in_step(chunks):
    chunks = list(chunks)
    while chunks:
        chunks = [chunk for chunk in chunks if next(chunk, chunk) is None]


def student_phase(fast, refs, mix, bonus, down, up, scratch, unroll):
    teach, lw_s, ex_s, hid_s, in_s, state_s, g_s, a_s, r_s, k_s, v_s, kept = scratch
    keep = kept.shape[1] == lw_s.shape[0]
    chunks, slab, width = lw_s.shape
    tokens = chunks * slab
    levels = slab.bit_length() - 1
    square = (slab, slab)
    t, m = row_ids(square), lane_ids(square)
    below = t > m
    after, before = zero_one(t < m), zero_one(below)
    sides = jnp.concatenate([after] * 3 + [before] * 2, axis=1)
    up_twice, down_deep = twice(up), rank_deep(down)
    gain = 2.0 / tokens

    def rows_of(c, again):
        if keep and again:
            return tuple(kept[n, c] for n in range(6))
        steps = []
        rows = []
        for n, at in enumerate(refs):
            now, step = with_shift(at, c)
            rows.append(now + mix[n] * step)
            steps.append(step)
        if keep:
            for n, part in enumerate((*rows, *steps)):
                kept[n, c] = part
        return (*rows, *steps)

    def load(c, again=False):
        r, k, v, q_step, k_step, v_step = rows_of(c, again)
        lw, ex = lw_s[c], ex_s[c]
        total = ex[slab - 1 :] + lw[slab - 1 :]
        if fast:
            middle = ex[slab // 2 : slab // 2 + 1]
            r_factor = jnp.exp(ex - middle)
            k_factor = jnp.exp(middle - ex - lw)
            into, out = jnp.exp(middle), jnp.exp(total - middle)
        else:
            r_factor = jnp.exp(ex)
            k_factor = jnp.exp(sums_of(after, split3(lw)))
            into = out = None
        return q_step, k_step, v_step, r, k, v, lw, total, r_factor, k_factor, into, out

    def scaled(x, by):
        return x if by is None else x * by

    def forward(c, carry):
        _, _, _, r, k, v, lw, total, r_factor, k_factor, into, out = load(c)
        rs, ks, vs = split2(r * r_factor), split2(k * k_factor), split2(v)
        yield
        memory = dot3(turned(vs), ks, NN)
        if fast:
            a = dot3(rs, ks, NT)
        else:

            def one_level(level, a):
                _, _, r_part, k_part, block, _ = level_parts(level, lw, r, k)
                return a + jnp.where(block, dot3(r_part, k_part, NT), 0.0)

            a = lax.fori_loop(0, levels, one_level, jnp.zeros(square, f32))
        yield
        own = jnp.sum(r * bonus * k, axis=1, keepdims=True)
        a = split2(jnp.where(below, a, 0.0) if fast else a)
        state = carry["state"]
        carry["state"] = state * jnp.exp(total) + scaled(memory, out)
        state_in = split2(scaled(state, into))
        yield
        o = own * v + dot3(a, vs, NN) + dot3(rs, state_in, NT)
        yield
        o = o - jnp.mean(o, axis=1, keepdims=True)
        yield
        rate = lax.rsqrt(jnp.mean(o * o, axis=1, keepdims=True) + NORM_EPS)
        normed = o * rate
        g = gain * (normed - teach[c].astype(f32))
        yield
        g = g - jnp.mean(g, axis=1, keepdims=True) - normed * jnp.mean(
            g * normed, axis=1, keepdims=True
        )
        yield
        state_s[c] = state
        g_s[c] = g * rate
        for held, parts in ((a_s, a), (r_s, rs), (k_s, ks), (v_s, vs)):
            held[c] = jnp.concatenate(parts, axis=1)

    def forward_some(i, state):
        carry = {"state": state}
        in_step(forward(i * unroll + n, carry) for n in range(unroll))
        return carry["state"]

    lax.fori_loop(0, chunks // unroll, forward_some, jnp.zeros((width, width), f32))

    def backward(c, carry):
        q_step, k_step, v_step, r, k, v, lw, total, r_factor, k_factor, into, out = load(c, True)
        a, rs, ks, vs = (halves(held[c]) for held in (a_s, r_s, k_s, v_s))
        g = g_s[c]
        gs = split2(g)
        yield
        memory = dot3(turned(gs), rs, NN)
        pair = dot3(gs, vs, NT)
        yield
        cot = carry["cot"]
        carry["cot"] = cot * jnp.exp(total) + scaled(memory, into)
        cot_out = split2(scaled(cot, out))
        state = state_s[c]
        state_in = split2(scaled(state, into))
        dlw = jnp.sum(state * jnp.exp(total) * cot, axis=0, keepdims=True)
        if fast:
            pairs = split2(jnp.where(below, pair, 0.0))
        yield
        dv = dot3(turned(a), gs, NN) + dot3(ks, cot_out, NT)
        dk = dot3(vs, cot_out, NN)
        if fast:
            dr = dot(
                stacked((gs[0], gs[1], pairs[0], pairs[1], gs[0], pairs[0], pairs[1]), 1),
                stacked((state_in[0], state_in[0], ks[0], ks[0], state_in[1], ks[1], ks[1]), 0),
                NN,
            )
            dk_in = dot4(turned(pairs), rs, NN)
            yield
            k_hat = joined(ks)
            from_earlier = k_hat * dk
            k_in = k_hat * dk_in
            from_later = joined(rs) * dr - k_in
            dlw = dlw - k_in
            dr = r_factor * dr
            dk = k_factor * (dk + dk_in)
        else:
            dr = dot3(gs, state_in, NN)
            from_earlier = joined(ks) * dk
            from_later = joined(rs) * dr
            dr = r_factor * dr
            dk = k_factor * dk

            def one_level(level, parts):
                dr, dk, dlw = parts
                r_by, k_by, r_part, k_part, block, span = level_parts(level, lw, r, k)
                pairs = split2(jnp.where(block & below, pair, 0.0))
                dr_in = r_by * dot3(pairs, k_part, NN)
                dk_in = k_by * dot3(pairs, r_part, TN)
                inside = split3(r * dr_in + k * dk_in)
                return dr + dr_in, dk + dk_in, dlw + sum(dot(span, part, TN) for part in inside)

            dr, dk, dlw = lax.fori_loop(
                0, levels, one_level, (dr, dk, jnp.broadcast_to(dlw, r.shape))
            )
        later, earlier = split3(from_later), split2(from_earlier)
        yield
        dlw = dlw + dot(sides, jnp.concatenate([*later, *earlier], axis=0), NN)
        dv = dv + jnp.sum(r * bonus * k, axis=1, keepdims=True) * g
        own = jnp.sum(v * g, axis=1, keepdims=True)
        yield
        own_r, own_k = own * r, own * k
        dr = dr + bonus * own_k
        dk = dk + bonus * own_r
        dpre = dlw * lw
        dpres = split2(dpre)
        yield
        hid = hid_s[c]
        dz = dot3(dpres, up_twice, NT)
        hid_t = in_s[2, c].T
        carry["up"] += dot(stacked((hid_t, hid_t), 1), stacked(dpres, 0), NN)
        yield
        dz = side_by_side(dz * (1.0 - hid * hid))
        yield
        dxw = dot(stacked((dz, dz), 1), down_deep, NN)
        dz_t = dz.T
        carry["down"] += dot(
            stacked((dz_t, dz_t), 1), stacked((in_s[0, c], in_s[1, c]), 0), NN
        )
        yield
        parts = (dr * q_step, dk * k_step, dv * v_step, dxw * q_step, dpre, own_r * k)
        carry["sums"] = tuple(
            old + jnp.sum(new.reshape(slab // 8, 8, width), axis=0)
            for old, new in zip(carry["sums"], parts)
        )

    def backward_some(i, carry):
        carry = dict(zip(("cot", "up", "down", "sums"), carry))
        in_step(backward(chunks - 1 - (i * unroll + n), carry) for n in range(unroll))
        return tuple(carry.values())

    rank = down[0].shape[0]
    empty = jnp.zeros((2 * rank, width), f32)
    start = (jnp.zeros((width, width), f32), empty, empty, (jnp.zeros((8, width), f32),) * 6)
    _, up_sum, down_sum, sums = lax.fori_loop(0, chunks // unroll, backward_some, start)
    tail = [split2(jnp.sum(part, axis=0, keepdims=True)) for part in sums]
    tail = [high.astype(f32) for high, _ in tail] + [low.astype(f32) for _, low in tail]
    tail.append(jnp.zeros((PACK_TAIL - len(tail), width), f32))
    up_sum, down_sum = (part[:rank] + part[rank:] for part in (up_sum, down_sum))
    return jnp.concatenate([up_sum, down_sum, *tail], axis=0)


def settings_of(head, mix_ref, bonus_ref):
    mix = [mix_ref[n, pl.ds(head, 1), :] for n in range(4)]
    return mix, bonus_ref[pl.ds(head, 1), :]


def in_order(pieces, scratch, place):
    if len(pieces) == 1:
        return pieces[0]
    near = len(pieces)
    for n, piece in enumerate(pieces):
        for far in range(piece.shape[0]):
            scratch[place ^ (far * near + n)] = piece[far]
    return scratch


def head_kernel(head_ref, q_ref, mix_ref, fade_ref, down_ref, up_ref, bonus_ref, *rest):
    slabs, per_device = q_ref.shape[:2]
    pieces, (out_ref, scores, *held, kv_s) = rest[:-15], rest[-15:]
    kv_ref = in_order(pieces, kv_s, head_ref[1])
    copies, shared = out_ref.shape[0], kv_ref.shape[1]
    for n in range(per_device):
        head = head_ref[0] + n
        mix, bonus = settings_of(head, mix_ref, bonus_ref)
        fade = fade_ref[pl.ds(head, 1), :]
        down, up = split2(down_ref[head]), split2(up_ref[head])
        group = n * shared // per_device
        refs = (
            lambda c, n=n: q_ref[c, n],
            lambda c, group=group: kv_ref[c, group, 0],
            lambda c, group=group: kv_ref[c, group, 1],
        )
        worst = decay_phase(refs[0], down, up, fade, mix, *held[1:5], math.gcd(4, slabs))
        teacher_phase(*refs, held[0], scores)
        safe = jnp.max(worst) <= SAFE_EXPONENT

        def finish(fast, unroll):
            grads = student_phase(fast, refs, mix, bonus, down, up, held, unroll).astype(bf16)

            def copy_out(at, _):
                out_ref[at, n] = grads
                return 0

            lax.fori_loop(0, copies, copy_out, 0)

        @pl.when(safe)
        def _():
            finish(True, math.gcd(8 if slabs <= 16 else 2, slabs))

        @pl.when(jnp.logical_not(safe))
        def _():
            finish(False, 1)


def head_grads(q, pieces, place, mix, fade, down_t, up, bonus, copies):
    slabs, per_device, slab, width = q.shape
    rank = up.shape[1]
    assert 2 * rank == width
    packed_rows = 2 * rank + PACK_TAIL
    k_slabs = math.gcd(4, slabs)
    small = slabs <= 16
    q_slabs = k_slabs if small else 1
    kv_shape = (slabs, *pieces[0].shape[1:]) if len(pieces) > 1 else (1, 16, width)
    vmem = pl.BlockSpec(memory_space=pltpu.VMEM)
    return pl.pallas_call(
        head_kernel,
        out_shape=jax.ShapeDtypeStruct((copies, per_device, packed_rows, width), bf16),
        in_specs=[pl.BlockSpec(memory_space=pltpu.SMEM)] + [vmem] * (6 + len(pieces)),
        out_specs=vmem,
        scratch_shapes=[
            pltpu.VMEM((slabs // k_slabs, q_slabs * slab, k_slabs * slab), f32),
            pltpu.VMEM((slabs, slab, width), bf16),
            pltpu.VMEM((slabs, slab, width), f32),
            pltpu.VMEM((slabs, slab, width), f32),
            pltpu.VMEM((slabs, slab, 2 * rank), f32),
            pltpu.VMEM((3, slabs, slab, width), bf16),
            pltpu.VMEM((slabs, width, width), f32),
            pltpu.VMEM((slabs, slab, width), f32),
            pltpu.VMEM((slabs, slab, 2 * slab), bf16),
            pltpu.VMEM((slabs, slab, 2 * width), bf16),
            pltpu.VMEM((slabs, slab, 2 * width), bf16),
            pltpu.VMEM((slabs, slab, 2 * width), bf16),
            pltpu.VMEM((6, slabs if small else 1, slab, width), f32),
            pltpu.VMEM(kv_shape, bf16),
        ],
        compiler_params=pltpu.CompilerParams(
            vmem_limit_bytes=(40 if small else 60) * 1024 * 1024
        ),
    )(place, q, mix, fade, down_t, up, bonus, *pieces)


def pack_queries(q_ref, out_ref):
    slots, _, width = out_ref.shape
    heads = q_ref.shape[1] // width
    for slot in range(slots):
        head = slot * heads // slots
        out_ref[slot] = q_ref[:, head * width : (head + 1) * width]


def pack_memory(group_of, place_ref, k_ref, v_ref, *out_refs):
    width = out_refs[0].shape[-1]
    for n, out_ref in enumerate(out_refs):
        start = group_of(place_ref[0], n) * width
        columns = pl.ds(start if isinstance(start, int) else pl.multiple_of(start, width), width)
        out_ref[0, 0, 0] = k_ref[:, columns]
        out_ref[0, 0, 1] = v_ref[:, columns]


def unpack_kernel(place_ref, *refs):
    *pieces, mix_ref, decay_ref, down_ref, up_ref, bonus_ref = refs
    heads, rank, _ = up_ref.shape
    for n in range(heads):
        if len(pieces) == 1:
            head, packed = n, pieces[0][n * (pieces[0].shape[0] // heads)]
        else:
            near = len(pieces)
            head, packed = place_ref[0] ^ n, pieces[n % near][n // near, 0]
        packed = packed.astype(f32)
        up_ref[head] = packed[:rank]
        down_ref[head] = packed[rank : 2 * rank]
        tail = packed[2 * rank :]
        tail = tail[:6] + tail[6:12]
        for at in range(4):
            mix_ref[at, pl.ds(head, 1), :] = tail[at : at + 1]
        decay_ref[pl.ds(head, 1), :] = tail[4:5]
        bonus_ref[pl.ds(head, 1), :] = tail[5:6]


def exchanged(x, differing, count):
    return lax.ppermute(x, "seq", [(d, d ^ differing) for d in range(count)])


def first_step(parts, near, count):
    got = [exchanged(part, n * near, count) if n else part for n, part in enumerate(parts)]
    return jnp.concatenate(got, axis=0)


def second_step(got, near, count):
    return [exchanged(got, n, count) if n else got for n in range(near)]


def shards(
    probe_vectors,
    mentor_address_vectors,
    mentor_content_vectors,
    previous_position_blend,
    feature_fading_exponent,
    fading_narrowing_matrix,
    fading_widening_matrix,
    diagonal_extra_amount,
):
    slab = probe_vectors.shape[0]
    heads, width, rank = fading_narrowing_matrix.shape
    place = lax.axis_index("seq")
    count = lax.axis_size("seq")
    copies = max(1, count // heads)
    per_device = max(1, heads // count)
    assert heads * copies == per_device * count
    groups = mentor_address_vectors.shape[1] // width
    by_bits = heads == count and count <= 16 and count & (count - 1) == 0 and count % groups == 0
    far, near = groups, count // groups
    vmem = pl.BlockSpec(memory_space=pltpu.VMEM)
    smem = pl.BlockSpec(memory_space=pltpu.SMEM)
    place = place.astype(jnp.int32)
    if by_bits:
        group_of = lambda place, n: (place // near) ^ n
        slots = far
    else:
        shared = max(1, per_device * groups // heads)
        firsts = [(d // copies) * per_device * groups // heads for d in range(count)]
        group_of = lambda _, n: firsts[n // shared] + n % shared
        slots = count * shared
    slot = jax.ShapeDtypeStruct((1, 1, 2, slab, width), bf16)
    kv = pl.pallas_call(
        functools.partial(pack_memory, group_of),
        out_shape=[slot] * slots,
        in_specs=[smem, vmem, vmem],
        out_specs=[vmem] * slots,
    )(place.reshape(1), mentor_address_vectors, mentor_content_vectors)
    if by_bits:
        kv, probe_vectors = lax.optimization_barrier((kv, probe_vectors))
        kv = first_step(kv, near, count)
    q = pl.pallas_call(
        pack_queries,
        out_shape=jax.ShapeDtypeStruct((heads * copies, slab, width), bf16),
        in_specs=[vmem],
        out_specs=vmem,
    )(probe_vectors)
    q = q.reshape(count, per_device, slab, width)
    if by_bits:
        kv, q = lax.optimization_barrier((kv, q))
        pieces = second_step(kv, near, count)
    q = lax.all_to_all(q, "seq", split_axis=0, concat_axis=0, tiled=True)
    if not by_bits:
        kv = jnp.stack(kv).reshape(count, shared, 2, slab, width)
        pieces = [lax.all_to_all(kv, "seq", split_axis=0, concat_axis=0, tiled=True)]
    packed = head_grads(
        q,
        pieces,
        jnp.stack([(place // copies) * per_device, place]),
        previous_position_blend,
        feature_fading_exponent,
        jnp.swapaxes(fading_narrowing_matrix, 1, 2),
        fading_widening_matrix,
        diagonal_extra_amount,
        1 if by_bits else count,
    )
    if by_bits:
        packed = second_step(first_step([packed] * far, near, count), near, count)
    else:
        packed = lax.all_to_all(packed, "seq", split_axis=0, concat_axis=0, tiled=True)
        packed = [packed.reshape(heads * copies, 2 * rank + PACK_TAIL, width)]
    vector = jax.ShapeDtypeStruct((heads, width), f32)
    matrix = jax.ShapeDtypeStruct((heads, rank, width), f32)
    mix, decay, down_t, up, bonus = pl.pallas_call(
        unpack_kernel,
        out_shape=(
            jax.ShapeDtypeStruct((4, heads, width), f32),
            vector,
            matrix,
            matrix,
            vector,
        ),
        in_specs=[smem] + [vmem] * len(packed),
        out_specs=[vmem] * 5,
    )(place.reshape(1), *packed)
    return mix, decay, jnp.swapaxes(down_t, 1, 2), up, bonus


def solution(mesh):
    return jax.shard_map(
        shards,
        mesh=mesh,
        in_specs=(
            P("seq", "head"),
            P("seq", "head"),
            P("seq", "head"),
            P(None, "head", None),
            P("head", None),
            P("head", None, None),
            P("head", None, None),
            P("head", None),
        ),
        out_specs=(
            P(None, "head", None),
            P("head", None),
            P("head", None, None),
            P("head", None, None),
            P("head", None),
        ),
        check_vma=False,
    )
```

```python
import functools
import math

import jax
import jax.numpy as jnp
from jax import lax
from jax.experimental import pallas as pl
from jax.experimental.pallas import tpu as pltpu
from jax.sharding import PartitionSpec as P

NORM_EPS = 0.00064
NEG_LARGE = -1e30
SAFE_EXPONENT = 30.0
PACK_TAIL = 16
LOG2_E = math.log2(math.e)

f32 = jnp.float32
bf16 = jnp.bfloat16

NN = (((1,), (0,)), ((), ()))
NT = (((1,), (1,)), ((), ()))
TN = (((0,), (0,)), ((), ()))


def dot(a, b, dims):
    return lax.dot_general(a, b, dims, preferred_element_type=f32)


def split2(x):
    high = x.astype(bf16)
    return high, (x - high.astype(f32)).astype(bf16)


def split3(x):
    high = x.astype(bf16)
    rest = x - high.astype(f32)
    middle = rest.astype(bf16)
    return high, middle, (rest - middle.astype(f32)).astype(bf16)


def stacked(parts, contracted):
    return jnp.concatenate(parts, axis=contracted)


def dot3(a, b, dims):
    (at,), (bt,) = dims[0]
    return dot(stacked((a[0], a[1], a[0]), at), stacked((b[0], b[0], b[1]), bt), dims)


def dot4(a, b, dims):
    (at,), (bt,) = dims[0]
    return dot(stacked((*a, *a), at), stacked((b[0], b[0], b[1], b[1]), bt), dims)


def twice(parts):
    return tuple(jnp.concatenate([part, part], axis=0) for part in parts)


def side_by_side(x):
    high, low = split2(x)
    return jnp.where(lane_ids(x.shape) < x.shape[1] // 2, high, low)


def rank_deep(parts):
    return jnp.concatenate([parts[0], parts[0], parts[1], jnp.zeros_like(parts[1])], axis=0)


def turned(parts):
    return tuple(part.T for part in parts)


def joined(parts):
    return parts[0].astype(f32) + parts[1].astype(f32)


def sums_of(zero_one, parts):
    return dot(stacked((zero_one,) * len(parts), 1), stacked(parts, 0), NN)


def row_ids(shape):
    return lax.broadcasted_iota(jnp.int32, shape, 0)


def lane_ids(shape):
    return lax.broadcasted_iota(jnp.int32, shape, 1)


def zero_one(condition):
    return jnp.where(condition, 1.0, 0.0).astype(bf16)


def with_shift(at, first, slabs=1):
    now = slabs_of(at, first, slabs).astype(f32)
    last = at(jnp.maximum(first - 1, 0))
    tail = last[last.shape[0] - 16 :].astype(f32)[15:16]
    tail = jnp.where(first > 0, tail, 0.0)
    earlier = jnp.where(row_ids(now.shape) == 0, tail, pltpu.roll(now, 1, 0))
    return now, earlier - now


def slabs_of(at, first, slabs):
    return jnp.concatenate([at(first + n) for n in range(slabs)], axis=0)


def teacher_phase(q_at, k_at, v_at, teach, scores):
    slabs, slab, width = teach.shape
    _, q_rows, k_rows = scores.shape
    q_slabs, k_slabs = q_rows // slab, k_rows // slab
    scale = LOG2_E / math.sqrt(width)

    def q_block(i, _):
        q = slabs_of(q_at, i * q_slabs, q_slabs)
        last = (i * q_slabs + q_slabs - 1) // k_slabs

        def score_block(j, top, edge=False):
            s = dot(q, slabs_of(k_at, j * k_slabs, k_slabs), NT) * scale
            if edge:
                seen = i * q_rows + row_ids(s.shape) >= j * k_rows + lane_ids(s.shape)
                s = jnp.where(seen, s, NEG_LARGE)
            scores[j] = s
            for n in range(k_rows // 128):
                top = jnp.maximum(top, s[:, n * 128 : (n + 1) * 128])
            return top

        top = lax.fori_loop(0, last, score_block, jnp.full((q_rows, 128), NEG_LARGE, f32))
        top = score_block(last, top, True)
        row_top = jnp.max(top, axis=1, keepdims=True)

        def value_block(j, carry):
            total, accum = carry
            p = jnp.exp2(scores[j] - row_top)
            for n in range(k_rows // 128):
                total = total + p[:, n * 128 : (n + 1) * 128]
            return total, accum + dot(p.astype(bf16), slabs_of(v_at, j * k_slabs, k_slabs), NN)

        total, accum = lax.fori_loop(
            0,
            last + 1,
            value_block,
            (jnp.zeros((q_rows, 128), f32), jnp.zeros((q_rows, width), f32)),
        )
        out = accum / jnp.sum(total, axis=1, keepdims=True)
        teach[pl.ds(i * q_slabs, q_slabs)] = out.astype(bf16).reshape(q_slabs, slab, width)
        return 0

    lax.fori_loop(0, slabs // q_slabs, q_block, 0)


def teacher_in_step(q_at, k_at, v_at, teach, scores):
    slabs, slab, width = teach.shape
    _, rows, _ = scores.shape
    each = rows // slab
    scale = LOG2_E / math.sqrt(width)

    def lanes(x):
        return [x[:, n * 128 : (n + 1) * 128] for n in range(rows // 128)]

    def q_block(i):
        held = [i * (i + 1) // 2 + j for j in range(i + 1)]
        q = slabs_of(q_at, i * each, each)
        top = jnp.full((rows, 128), NEG_LARGE, f32)
        for j in range(i + 1):
            s = dot(q, slabs_of(k_at, j * each, each), NT) * scale
            if j == i:
                s = jnp.where(row_ids(s.shape) >= lane_ids(s.shape), s, NEG_LARGE)
            scores[held[j]] = s
            top = functools.reduce(jnp.maximum, lanes(s), top)
            yield
        top = jnp.max(top, axis=1, keepdims=True)
        total, accum = jnp.zeros((rows, 128), f32), jnp.zeros((rows, width), f32)
        for j in range(i + 1):
            p = jnp.exp2(scores[held[j]] - top)
            total = sum(lanes(p), total)
            accum = accum + dot(p.astype(bf16), slabs_of(v_at, j * each, each), NN)
            yield
        out = (accum / jnp.sum(total, axis=1, keepdims=True)).astype(bf16)
        teach[i * each : (i + 1) * each] = out.reshape(each, slab, width)

    in_step(q_block(i) for i in range(slabs // each))


def decay_phase(q_at, down, up, fade, mix, lw_s, ex_s, hid_s, in_s, slabs):
    count, slab, width = lw_s.shape
    square = (slab, slab)
    before = zero_one(row_ids(square) > lane_ids(square))

    def block(i, worst):
        first = i * slabs
        q, q_step = with_shift(q_at, first, slabs)
        decay_in = split2(q + mix[3] * q_step)
        hid = jnp.tanh(dot3(decay_in, twice(down), NT))
        hid_parts = side_by_side(hid)
        lw = -jnp.exp(fade + dot(stacked((hid_parts,) * 2, 1), rank_deep(up), NN))
        hid_s[pl.ds(first, slabs)] = hid.reshape(slabs, slab, width)
        for n, part in enumerate((*decay_in, hid_parts)):
            in_s[n, pl.ds(first, slabs)] = part.reshape(slabs, slab, width)
        lw_s[pl.ds(first, slabs)] = lw.reshape(slabs, slab, width)
        for n in range(slabs):
            part = lw[n * slab : (n + 1) * slab]
            ex = sums_of(before, split3(part))
            ex_s[first + n] = ex
            middle = ex[slab // 2 : slab // 2 + 1]
            total = ex[slab - 1 :] + part[slab - 1 :]
            worst = jnp.maximum(worst, jnp.maximum(-middle, middle - total))
        return worst

    return lax.fori_loop(0, count // slabs, block, jnp.zeros((1, width), f32))


def level_parts(level, lw, r, k):
    square = (lw.shape[0], lw.shape[0])
    t, m = row_ids(square), lane_ids(square)
    edge = ((t >> (level + 1)) << (level + 1)) + (1 << level) - 1
    upper = ((t >> level) & 1) == 1
    lower = ((t >> level) & 1) == 0
    span = zero_one((upper & (m > edge) & (m < t)) | (lower & (m > t) & (m <= edge)))
    factor = jnp.exp(sums_of(span, split3(lw)))
    upper_rows = ((row_ids(r.shape) >> level) & 1) == 1
    r_factor = jnp.where(upper_rows, factor, 0.0)
    k_factor = jnp.where(upper_rows, 0.0, factor)
    same = (t >> (level + 1)) == (m >> (level + 1))
    return r_factor, k_factor, split2(r * r_factor), split2(k * k_factor), same, span


def halves(x):
    width = x.shape[1] // 2
    return x[:, :width], x[:, width:]


def in_step(chunks):
    chunks = list(chunks)
    while chunks:
        chunks = [chunk for chunk in chunks if next(chunk, chunk) is None]


def student_phase(fast, refs, mix, bonus, down, up, scratch, unroll):
    teach, lw_s, ex_s, hid_s, in_s, state_s, g_s, a_s, r_s, k_s, v_s, kept = scratch
    keep = kept.shape[1] == lw_s.shape[0]
    chunks, slab, width = lw_s.shape
    tokens = chunks * slab
    levels = slab.bit_length() - 1
    square = (slab, slab)
    t, m = row_ids(square), lane_ids(square)
    below = t > m
    after, before = zero_one(t < m), zero_one(below)
    sides = jnp.concatenate([after] * 3 + [before] * 2, axis=1)
    up_twice, down_deep = twice(up), rank_deep(down)
    gain = 2.0 / tokens

    def rows_of(c, again):
        if keep and again:
            return tuple(kept[n, c] for n in range(6))
        steps = []
        rows = []
        for n, at in enumerate(refs):
            now, step = with_shift(at, c)
            rows.append(now + mix[n] * step)
            steps.append(step)
        if keep:
            for n, part in enumerate((*rows, *steps)):
                kept[n, c] = part
        return (*rows, *steps)

    def load(c, again=False):
        r, k, v, q_step, k_step, v_step = rows_of(c, again)
        lw, ex = lw_s[c], ex_s[c]
        total = ex[slab - 1 :] + lw[slab - 1 :]
        if fast:
            middle = ex[slab // 2 : slab // 2 + 1]
            r_factor = jnp.exp(ex - middle)
            k_factor = jnp.exp(middle - ex - lw)
            into, out = jnp.exp(middle), jnp.exp(total - middle)
        else:
            r_factor = jnp.exp(ex)
            k_factor = jnp.exp(sums_of(after, split3(lw)))
            into = out = None
        return q_step, k_step, v_step, r, k, v, lw, total, r_factor, k_factor, into, out

    def scaled(x, by):
        return x if by is None else x * by

    def forward(c, carry):
        _, _, _, r, k, v, lw, total, r_factor, k_factor, into, out = load(c)
        rs, ks, vs = split2(r * r_factor), split2(k * k_factor), split2(v)
        yield
        memory = dot3(turned(vs), ks, NN)
        if fast:
            a = dot3(rs, ks, NT)
        else:

            def one_level(level, a):
                _, _, r_part, k_part, block, _ = level_parts(level, lw, r, k)
                return a + jnp.where(block, dot3(r_part, k_part, NT), 0.0)

            a = lax.fori_loop(0, levels, one_level, jnp.zeros(square, f32))
        yield
        own = jnp.sum(r * bonus * k, axis=1, keepdims=True)
        a = split2(jnp.where(below, a, 0.0) if fast else a)
        state = carry["state"]
        carry["state"] = state * jnp.exp(total) + scaled(memory, out)
        state_in = split2(scaled(state, into))
        yield
        o = own * v + dot3(a, vs, NN) + dot3(rs, state_in, NT)
        yield
        o = o - jnp.mean(o, axis=1, keepdims=True)
        yield
        rate = lax.rsqrt(jnp.mean(o * o, axis=1, keepdims=True) + NORM_EPS)
        normed = o * rate
        g = gain * (normed - teach[c].astype(f32))
        yield
        g = g - jnp.mean(g, axis=1, keepdims=True) - normed * jnp.mean(
            g * normed, axis=1, keepdims=True
        )
        yield
        state_s[c] = state
        g_s[c] = g * rate
        for held, parts in ((a_s, a), (r_s, rs), (k_s, ks), (v_s, vs)):
            held[c] = jnp.concatenate(parts, axis=1)

    def forward_some(i, state):
        carry = {"state": state}
        in_step(forward(i * unroll + n, carry) for n in range(unroll))
        return carry["state"]

    lax.fori_loop(0, chunks // unroll, forward_some, jnp.zeros((width, width), f32))

    def backward(c, carry):
        q_step, k_step, v_step, r, k, v, lw, total, r_factor, k_factor, into, out = load(c, True)
        a, rs, ks, vs = (halves(held[c]) for held in (a_s, r_s, k_s, v_s))
        g = g_s[c]
        gs = split2(g)
        yield
        memory = dot3(turned(gs), rs, NN)
        pair = dot3(gs, vs, NT)
        yield
        cot = carry["cot"]
        carry["cot"] = cot * jnp.exp(total) + scaled(memory, into)
        cot_out = split2(scaled(cot, out))
        state = state_s[c]
        state_in = split2(scaled(state, into))
        dlw = jnp.sum(state * jnp.exp(total) * cot, axis=0, keepdims=True)
        if fast:
            pairs = split2(jnp.where(below, pair, 0.0))
        yield
        dv = dot3(turned(a), gs, NN) + dot3(ks, cot_out, NT)
        dk = dot3(vs, cot_out, NN)
        if fast:
            dr = dot(
                stacked((gs[0], gs[1], pairs[0], pairs[1], gs[0], pairs[0], pairs[1]), 1),
                stacked((state_in[0], state_in[0], ks[0], ks[0], state_in[1], ks[1], ks[1]), 0),
                NN,
            )
            dk_in = dot4(turned(pairs), rs, NN)
            yield
            k_hat = joined(ks)
            from_earlier = k_hat * dk
            k_in = k_hat * dk_in
            from_later = joined(rs) * dr - k_in
            dlw = dlw - k_in
            dr = r_factor * dr
            dk = k_factor * (dk + dk_in)
        else:
            dr = dot3(gs, state_in, NN)
            from_earlier = joined(ks) * dk
            from_later = joined(rs) * dr
            dr = r_factor * dr
            dk = k_factor * dk

            def one_level(level, parts):
                dr, dk, dlw = parts
                r_by, k_by, r_part, k_part, block, span = level_parts(level, lw, r, k)
                pairs = split2(jnp.where(block & below, pair, 0.0))
                dr_in = r_by * dot3(pairs, k_part, NN)
                dk_in = k_by * dot3(pairs, r_part, TN)
                inside = split3(r * dr_in + k * dk_in)
                return dr + dr_in, dk + dk_in, dlw + sum(dot(span, part, TN) for part in inside)

            dr, dk, dlw = lax.fori_loop(
                0, levels, one_level, (dr, dk, jnp.broadcast_to(dlw, r.shape))
            )
        later, earlier = split3(from_later), split2(from_earlier)
        yield
        dlw = dlw + dot(sides, jnp.concatenate([*later, *earlier], axis=0), NN)
        dv = dv + jnp.sum(r * bonus * k, axis=1, keepdims=True) * g
        own = jnp.sum(v * g, axis=1, keepdims=True)
        yield
        own_r, own_k = own * r, own * k
        dr = dr + bonus * own_k
        dk = dk + bonus * own_r
        dpre = dlw * lw
        dpres = split2(dpre)
        yield
        hid = hid_s[c]
        dz = dot3(dpres, up_twice, NT)
        hid_t = in_s[2, c].T
        carry["up"] += dot(stacked((hid_t, hid_t), 1), stacked(dpres, 0), NN)
        yield
        dz = side_by_side(dz * (1.0 - hid * hid))
        yield
        dxw = dot(stacked((dz, dz), 1), down_deep, NN)
        dz_t = dz.T
        carry["down"] += dot(
            stacked((dz_t, dz_t), 1), stacked((in_s[0, c], in_s[1, c]), 0), NN
        )
        yield
        parts = (dr * q_step, dk * k_step, dv * v_step, dxw * q_step, dpre, own_r * k)
        carry["sums"] = tuple(
            old + jnp.sum(new.reshape(slab // 8, 8, width), axis=0)
            for old, new in zip(carry["sums"], parts)
        )

    def backward_some(i, carry):
        carry = dict(zip(("cot", "up", "down", "sums"), carry))
        in_step(backward(chunks - 1 - (i * unroll + n), carry) for n in range(unroll))
        return tuple(carry.values())

    rank = down[0].shape[0]
    empty = jnp.zeros((2 * rank, width), f32)
    start = (jnp.zeros((width, width), f32), empty, empty, (jnp.zeros((8, width), f32),) * 6)
    _, up_sum, down_sum, sums = lax.fori_loop(0, chunks // unroll, backward_some, start)
    tail = [split2(jnp.sum(part, axis=0, keepdims=True)) for part in sums]
    tail = [high.astype(f32) for high, _ in tail] + [low.astype(f32) for _, low in tail]
    tail.append(jnp.zeros((PACK_TAIL - len(tail), width), f32))
    up_sum, down_sum = (part[:rank] + part[rank:] for part in (up_sum, down_sum))
    return jnp.concatenate([up_sum, down_sum, *tail], axis=0)


def settings_of(head, mix_ref, bonus_ref):
    mix = [mix_ref[n, pl.ds(head, 1), :] for n in range(4)]
    return mix, bonus_ref[pl.ds(head, 1), :]


def in_order(pieces, scratch, place):
    if len(pieces) == 1:
        return pieces[0]
    near = len(pieces)
    for n, piece in enumerate(pieces):
        for far in range(piece.shape[0]):
            scratch[place ^ (far * near + n)] = piece[far]
    return scratch


def head_kernel(head_ref, q_ref, mix_ref, fade_ref, down_ref, up_ref, bonus_ref, *rest):
    slabs, per_device = q_ref.shape[:2]
    pieces, (out_ref, scores, *held, kv_s) = rest[:-15], rest[-15:]
    kv_ref = in_order(pieces, kv_s, head_ref[1])
    copies, shared = out_ref.shape[0], kv_ref.shape[1]
    for n in range(per_device):
        head = head_ref[0] + n
        mix, bonus = settings_of(head, mix_ref, bonus_ref)
        fade = fade_ref[pl.ds(head, 1), :]
        down, up = split2(down_ref[head]), split2(up_ref[head])
        group = n * shared // per_device
        refs = (
            lambda c, n=n: q_ref[c, n],
            lambda c, group=group: kv_ref[c, group, 0],
            lambda c, group=group: kv_ref[c, group, 1],
        )
        worst = decay_phase(refs[0], down, up, fade, mix, *held[1:5], math.gcd(4, slabs))
        (teacher_in_step if slabs <= 16 else teacher_phase)(*refs, held[0], scores)
        safe = jnp.max(worst) <= SAFE_EXPONENT

        def finish(fast, unroll):
            grads = student_phase(fast, refs, mix, bonus, down, up, held, unroll).astype(bf16)

            def copy_out(at, _):
                out_ref[at, n] = grads
                return 0

            lax.fori_loop(0, copies, copy_out, 0)

        @pl.when(safe)
        def _():
            finish(True, math.gcd(8 if slabs <= 16 else 2, slabs))

        @pl.when(jnp.logical_not(safe))
        def _():
            finish(False, 1)


def head_grads(q, pieces, place, mix, fade, down_t, up, bonus, copies):
    slabs, per_device, slab, width = q.shape
    rank = up.shape[1]
    assert 2 * rank == width
    packed_rows = 2 * rank + PACK_TAIL
    k_slabs = math.gcd(4, slabs)
    small = slabs <= 16
    q_slabs = k_slabs if small else 1
    blocks = slabs // k_slabs
    blocks = blocks * (blocks + 1) // 2 if small else blocks
    kv_shape = (slabs, *pieces[0].shape[1:]) if len(pieces) > 1 else (1, 16, width)
    vmem = pl.BlockSpec(memory_space=pltpu.VMEM)
    return pl.pallas_call(
        head_kernel,
        out_shape=jax.ShapeDtypeStruct((copies, per_device, packed_rows, width), bf16),
        in_specs=[pl.BlockSpec(memory_space=pltpu.SMEM)] + [vmem] * (6 + len(pieces)),
        out_specs=vmem,
        scratch_shapes=[
            pltpu.VMEM((blocks, q_slabs * slab, k_slabs * slab), f32),
            pltpu.VMEM((slabs, slab, width), bf16),
            pltpu.VMEM((slabs, slab, width), f32),
            pltpu.VMEM((slabs, slab, width), f32),
            pltpu.VMEM((slabs, slab, 2 * rank), f32),
            pltpu.VMEM((3, slabs, slab, width), bf16),
            pltpu.VMEM((slabs, width, width), f32),
            pltpu.VMEM((slabs, slab, width), f32),
            pltpu.VMEM((slabs, slab, 2 * slab), bf16),
            pltpu.VMEM((slabs, slab, 2 * width), bf16),
            pltpu.VMEM((slabs, slab, 2 * width), bf16),
            pltpu.VMEM((slabs, slab, 2 * width), bf16),
            pltpu.VMEM((6, slabs if small else 1, slab, width), f32),
            pltpu.VMEM(kv_shape, bf16),
        ],
        compiler_params=pltpu.CompilerParams(
            vmem_limit_bytes=(46 if small else 60) * 1024 * 1024
        ),
    )(place, q, mix, fade, down_t, up, bonus, *pieces)


def pack_queries(q_ref, out_ref):
    slots, _, width = out_ref.shape
    heads = q_ref.shape[1] // width
    for slot in range(slots):
        head = slot * heads // slots
        out_ref[slot] = q_ref[:, head * width : (head + 1) * width]


def pack_memory(group_of, place_ref, k_ref, v_ref, *out_refs):
    width = out_refs[0].shape[-1]
    for n, out_ref in enumerate(out_refs):
        start = group_of(place_ref[0], n) * width
        columns = pl.ds(start if isinstance(start, int) else pl.multiple_of(start, width), width)
        out_ref[0, 0, 0] = k_ref[:, columns]
        out_ref[0, 0, 1] = v_ref[:, columns]


def unpack_kernel(place_ref, *refs):
    *pieces, mix_ref, decay_ref, down_ref, up_ref, bonus_ref = refs
    heads, rank, _ = up_ref.shape
    for n in range(heads):
        if len(pieces) == 1:
            head, packed = n, pieces[0][n * (pieces[0].shape[0] // heads)]
        else:
            near = len(pieces)
            head, packed = place_ref[0] ^ n, pieces[n % near][n // near, 0]
        packed = packed.astype(f32)
        up_ref[head] = packed[:rank]
        down_ref[head] = packed[rank : 2 * rank]
        tail = packed[2 * rank :]
        tail = tail[:6] + tail[6:12]
        for at in range(4):
            mix_ref[at, pl.ds(head, 1), :] = tail[at : at + 1]
        decay_ref[pl.ds(head, 1), :] = tail[4:5]
        bonus_ref[pl.ds(head, 1), :] = tail[5:6]


def exchanged(x, differing, count):
    return lax.ppermute(x, "seq", [(d, d ^ differing) for d in range(count)])


def first_step(parts, near, count):
    got = [exchanged(part, n * near, count) if n else part for n, part in enumerate(parts)]
    return jnp.concatenate(got, axis=0)


def second_step(got, near, count):
    return [exchanged(got, n, count) if n else got for n in range(near)]


def shards(
    probe_vectors,
    mentor_address_vectors,
    mentor_content_vectors,
    previous_position_blend,
    feature_fading_exponent,
    fading_narrowing_matrix,
    fading_widening_matrix,
    diagonal_extra_amount,
):
    slab = probe_vectors.shape[0]
    heads, width, rank = fading_narrowing_matrix.shape
    place = lax.axis_index("seq")
    count = lax.axis_size("seq")
    copies = max(1, count // heads)
    per_device = max(1, heads // count)
    assert heads * copies == per_device * count
    groups = mentor_address_vectors.shape[1] // width
    by_bits = heads == count and count <= 16 and count & (count - 1) == 0 and count % groups == 0
    far, near = groups, count // groups
    vmem = pl.BlockSpec(memory_space=pltpu.VMEM)
    smem = pl.BlockSpec(memory_space=pltpu.SMEM)
    place = place.astype(jnp.int32)
    if by_bits:
        group_of = lambda place, n: (place // near) ^ n
        slots = far
    else:
        shared = max(1, per_device * groups // heads)
        firsts = [(d // copies) * per_device * groups // heads for d in range(count)]
        group_of = lambda _, n: firsts[n // shared] + n % shared
        slots = count * shared
    slot = jax.ShapeDtypeStruct((1, 1, 2, slab, width), bf16)
    kv = pl.pallas_call(
        functools.partial(pack_memory, group_of),
        out_shape=[slot] * slots,
        in_specs=[smem, vmem, vmem],
        out_specs=[vmem] * slots,
    )(place.reshape(1), mentor_address_vectors, mentor_content_vectors)
    if by_bits:
        kv, probe_vectors = lax.optimization_barrier((first_step(kv, near, count), probe_vectors))
        pieces = second_step(kv, near, count)
    q = pl.pallas_call(
        pack_queries,
        out_shape=jax.ShapeDtypeStruct((heads * copies, slab, width), bf16),
        in_specs=[vmem],
        out_specs=vmem,
    )(probe_vectors)
    q = q.reshape(count, per_device, slab, width)
    q = lax.all_to_all(q, "seq", split_axis=0, concat_axis=0, tiled=True)
    if not by_bits:
        kv = jnp.stack(kv).reshape(count, shared, 2, slab, width)
        pieces = [lax.all_to_all(kv, "seq", split_axis=0, concat_axis=0, tiled=True)]
    packed = head_grads(
        q,
        pieces,
        jnp.stack([(place // copies) * per_device, place]),
        previous_position_blend,
        feature_fading_exponent,
        jnp.swapaxes(fading_narrowing_matrix, 1, 2),
        fading_widening_matrix,
        diagonal_extra_amount,
        1 if by_bits else count,
    )
    if by_bits:
        packed = second_step(first_step([packed] * far, near, count), near, count)
    else:
        packed = lax.all_to_all(packed, "seq", split_axis=0, concat_axis=0, tiled=True)
        packed = [packed.reshape(heads * copies, 2 * rank + PACK_TAIL, width)]
    vector = jax.ShapeDtypeStruct((heads, width), f32)
    matrix = jax.ShapeDtypeStruct((heads, rank, width), f32)
    mix, decay, down_t, up, bonus = pl.pallas_call(
        unpack_kernel,
        out_shape=(
            jax.ShapeDtypeStruct((4, heads, width), f32),
            vector,
            matrix,
            matrix,
            vector,
        ),
        in_specs=[smem] + [vmem] * len(packed),
        out_specs=[vmem] * 5,
    )(place.reshape(1), *packed)
    return mix, decay, jnp.swapaxes(down_t, 1, 2), up, bonus


def solution(mesh):
    return jax.shard_map(
        shards,
        mesh=mesh,
        in_specs=(
            P("seq", "head"),
            P("seq", "head"),
            P("seq", "head"),
            P(None, "head", None),
            P("head", None),
            P("head", None, None),
            P("head", None, None),
            P("head", None),
        ),
        out_specs=(
            P(None, "head", None),
            P("head", None),
            P("head", None, None),
            P("head", None, None),
            P("head", None),
        ),
        check_vma=False,
    )
```

```python
import functools
import math

import jax
import jax.numpy as jnp
from jax import lax
from jax.experimental import pallas as pl
from jax.experimental.pallas import tpu as pltpu
from jax.sharding import PartitionSpec as P

NORM_EPS = 0.00064
NEG_LARGE = -1e30
SAFE_EXPONENT = 30.0
PACK_TAIL = 16
LOG2_E = math.log2(math.e)

f32 = jnp.float32
bf16 = jnp.bfloat16

NN = (((1,), (0,)), ((), ()))
NT = (((1,), (1,)), ((), ()))
TN = (((0,), (0,)), ((), ()))


def dot(a, b, dims):
    return lax.dot_general(a, b, dims, preferred_element_type=f32)


def split2(x):
    high = x.astype(bf16)
    return high, (x - high.astype(f32)).astype(bf16)


def split3(x):
    high = x.astype(bf16)
    rest = x - high.astype(f32)
    middle = rest.astype(bf16)
    return high, middle, (rest - middle.astype(f32)).astype(bf16)


def stacked(parts, contracted):
    return jnp.concatenate(parts, axis=contracted)


def dot3(a, b, dims):
    (at,), (bt,) = dims[0]
    return dot(stacked((a[0], a[1], a[0]), at), stacked((b[0], b[0], b[1]), bt), dims)


def dot4(a, b, dims):
    (at,), (bt,) = dims[0]
    return dot(stacked((*a, *a), at), stacked((b[0], b[0], b[1], b[1]), bt), dims)


def twice(parts):
    return tuple(jnp.concatenate([part, part], axis=0) for part in parts)


def side_by_side(x):
    high, low = split2(x)
    return jnp.where(lane_ids(x.shape) < x.shape[1] // 2, high, low)


def rank_deep(parts):
    return jnp.concatenate([parts[0], parts[0], parts[1], jnp.zeros_like(parts[1])], axis=0)


def turned(parts):
    return tuple(part.T for part in parts)


def joined(parts):
    return parts[0].astype(f32) + parts[1].astype(f32)


def sums_of(zero_one, parts):
    return dot(stacked((zero_one,) * len(parts), 1), stacked(parts, 0), NN)


def row_ids(shape):
    return lax.broadcasted_iota(jnp.int32, shape, 0)


def lane_ids(shape):
    return lax.broadcasted_iota(jnp.int32, shape, 1)


def zero_one(condition):
    return jnp.where(condition, 1.0, 0.0).astype(bf16)


def with_shift(at, first, slabs=1):
    now = slabs_of(at, first, slabs).astype(f32)
    fixed = isinstance(first, int)
    last = at(max(first - 1, 0) if fixed else jnp.maximum(first - 1, 0))
    tail = last[last.shape[0] - 16 :].astype(f32)[15:16]
    if not fixed:
        tail = jnp.where(first > 0, tail, 0.0)
    elif first == 0:
        tail = jnp.zeros_like(tail)
    earlier = jnp.where(row_ids(now.shape) == 0, tail, pltpu.roll(now, 1, 0))
    return now, earlier - now


def slabs_of(at, first, slabs):
    return jnp.concatenate([at(first + n) for n in range(slabs)], axis=0)


def teacher_phase(q_at, k_at, v_at, teach, scores):
    slabs, slab, width = teach.shape
    _, q_rows, k_rows = scores.shape
    q_slabs, k_slabs = q_rows // slab, k_rows // slab
    scale = LOG2_E / math.sqrt(width)

    def q_block(i, _):
        q = slabs_of(q_at, i * q_slabs, q_slabs)
        last = (i * q_slabs + q_slabs - 1) // k_slabs

        def score_block(j, top, edge=False):
            s = dot(q, slabs_of(k_at, j * k_slabs, k_slabs), NT) * scale
            if edge:
                seen = i * q_rows + row_ids(s.shape) >= j * k_rows + lane_ids(s.shape)
                s = jnp.where(seen, s, NEG_LARGE)
            scores[j] = s
            for n in range(k_rows // 128):
                top = jnp.maximum(top, s[:, n * 128 : (n + 1) * 128])
            return top

        top = lax.fori_loop(0, last, score_block, jnp.full((q_rows, 128), NEG_LARGE, f32))
        top = score_block(last, top, True)
        row_top = jnp.max(top, axis=1, keepdims=True)

        def value_block(j, carry):
            total, accum = carry
            p = jnp.exp2(scores[j] - row_top)
            for n in range(k_rows // 128):
                total = total + p[:, n * 128 : (n + 1) * 128]
            return total, accum + dot(p.astype(bf16), slabs_of(v_at, j * k_slabs, k_slabs), NN)

        total, accum = lax.fori_loop(
            0,
            last + 1,
            value_block,
            (jnp.zeros((q_rows, 128), f32), jnp.zeros((q_rows, width), f32)),
        )
        out = accum / jnp.sum(total, axis=1, keepdims=True)
        teach[pl.ds(i * q_slabs, q_slabs)] = out.astype(bf16).reshape(q_slabs, slab, width)
        return 0

    lax.fori_loop(0, slabs // q_slabs, q_block, 0)


def teacher_in_step(q_at, k_at, v_at, teach, scores):
    slabs, slab, width = teach.shape
    _, rows, _ = scores.shape
    each = rows // slab
    scale = LOG2_E / math.sqrt(width)

    def lanes(x):
        return [x[:, n * 128 : (n + 1) * 128] for n in range(rows // 128)]

    def q_block(i):
        held = [i * (i + 1) // 2 + j for j in range(i + 1)]
        q = slabs_of(q_at, i * each, each)
        top = jnp.full((rows, 128), NEG_LARGE, f32)
        for j in range(i + 1):
            s = dot(q, slabs_of(k_at, j * each, each), NT) * scale
            if j == i:
                s = jnp.where(row_ids(s.shape) >= lane_ids(s.shape), s, NEG_LARGE)
            scores[held[j]] = s
            top = functools.reduce(jnp.maximum, lanes(s), top)
            yield
        top = jnp.max(top, axis=1, keepdims=True)
        total, accum = jnp.zeros((rows, 128), f32), jnp.zeros((rows, width), f32)
        for j in range(i + 1):
            p = jnp.exp2(scores[held[j]] - top)
            total = sum(lanes(p), total)
            accum = accum + dot(p.astype(bf16), slabs_of(v_at, j * each, each), NN)
            yield
        out = (accum / jnp.sum(total, axis=1, keepdims=True)).astype(bf16)
        teach[i * each : (i + 1) * each] = out.reshape(each, slab, width)

    return [q_block(i) for i in range(slabs // each)]


def decay_phase(q_at, down, up, fade, mix, lw_s, ex_s, hid_s, in_s, slabs, together):
    count, slab, width = lw_s.shape
    square = (slab, slab)
    before = zero_one(row_ids(square) > lane_ids(square))

    def block(i, carry):
        first = i * slabs
        q, q_step = with_shift(q_at, first, slabs)
        decay_in = split2(q + mix[3] * q_step)
        yield
        hid = dot3(decay_in, twice(down), NT)
        yield
        hid = jnp.tanh(hid)
        hid_parts = side_by_side(hid)
        yield
        lw = dot(stacked((hid_parts,) * 2, 1), rank_deep(up), NN)
        yield
        lw = -jnp.exp(fade + lw)
        hid_s[pl.ds(first, slabs)] = hid.reshape(slabs, slab, width)
        for n, part in enumerate((*decay_in, hid_parts)):
            in_s[n, pl.ds(first, slabs)] = part.reshape(slabs, slab, width)
        lw_s[pl.ds(first, slabs)] = lw.reshape(slabs, slab, width)
        yield
        for n in range(slabs):
            part = lw[n * slab : (n + 1) * slab]
            ex = sums_of(before, split3(part))
            ex_s[first + n] = ex
            middle = ex[slab // 2 : slab // 2 + 1]
            total = ex[slab - 1 :] + part[slab - 1 :]
            carry["worst"] = jnp.maximum(
                carry["worst"], jnp.maximum(-middle, middle - total)
            )

    def alone(i, worst):
        carry = {"worst": worst}
        in_step([block(i, carry)])
        return carry["worst"]

    none = jnp.zeros((1, width), f32)
    if together is None:
        return lax.fori_loop(0, count // slabs, alone, none)
    carry = {"worst": none}
    in_step([*(block(i, carry) for i in range(count // slabs)), *together])
    return carry["worst"]


def level_parts(level, lw, r, k):
    square = (lw.shape[0], lw.shape[0])
    t, m = row_ids(square), lane_ids(square)
    edge = ((t >> (level + 1)) << (level + 1)) + (1 << level) - 1
    upper = ((t >> level) & 1) == 1
    lower = ((t >> level) & 1) == 0
    span = zero_one((upper & (m > edge) & (m < t)) | (lower & (m > t) & (m <= edge)))
    factor = jnp.exp(sums_of(span, split3(lw)))
    upper_rows = ((row_ids(r.shape) >> level) & 1) == 1
    r_factor = jnp.where(upper_rows, factor, 0.0)
    k_factor = jnp.where(upper_rows, 0.0, factor)
    same = (t >> (level + 1)) == (m >> (level + 1))
    return r_factor, k_factor, split2(r * r_factor), split2(k * k_factor), same, span


def halves(x):
    width = x.shape[1] // 2
    return x[:, :width], x[:, width:]


def in_step(chunks):
    chunks = list(chunks)
    while chunks:
        chunks = [chunk for chunk in chunks if next(chunk, chunk) is None]


def student_phase(fast, refs, mix, bonus, down, up, scratch, unroll):
    teach, lw_s, ex_s, hid_s, in_s, state_s, g_s, a_s, r_s, k_s, v_s, kept = scratch
    keep = kept.shape[1] == lw_s.shape[0]
    chunks, slab, width = lw_s.shape
    tokens = chunks * slab
    levels = slab.bit_length() - 1
    square = (slab, slab)
    t, m = row_ids(square), lane_ids(square)
    below = t > m
    after, before = zero_one(t < m), zero_one(below)
    sides = jnp.concatenate([after] * 3 + [before] * 2, axis=1)
    up_twice, down_deep = twice(up), rank_deep(down)
    gain = 2.0 / tokens

    def rows_of(c, again):
        if keep and again:
            return tuple(kept[n, c] for n in range(6))
        steps = []
        rows = []
        for n, at in enumerate(refs):
            now, step = with_shift(at, c)
            rows.append(now + mix[n] * step)
            steps.append(step)
        if keep:
            for n, part in enumerate((*rows, *steps)):
                kept[n, c] = part
        return (*rows, *steps)

    def load(c, again=False):
        r, k, v, q_step, k_step, v_step = rows_of(c, again)
        lw, ex = lw_s[c], ex_s[c]
        total = ex[slab - 1 :] + lw[slab - 1 :]
        if fast:
            middle = ex[slab // 2 : slab // 2 + 1]
            r_factor = jnp.exp(ex - middle)
            k_factor = jnp.exp(middle - ex - lw)
            into, out = jnp.exp(middle), jnp.exp(total - middle)
        else:
            r_factor = jnp.exp(ex)
            k_factor = jnp.exp(sums_of(after, split3(lw)))
            into = out = None
        return q_step, k_step, v_step, r, k, v, lw, total, r_factor, k_factor, into, out

    def scaled(x, by):
        return x if by is None else x * by

    def forward(c, carry):
        _, _, _, r, k, v, lw, total, r_factor, k_factor, into, out = load(c)
        rs, ks, vs = split2(r * r_factor), split2(k * k_factor), split2(v)
        yield
        memory = dot3(turned(vs), ks, NN)
        if fast:
            a = dot3(rs, ks, NT)
        else:

            def one_level(level, a):
                _, _, r_part, k_part, block, _ = level_parts(level, lw, r, k)
                return a + jnp.where(block, dot3(r_part, k_part, NT), 0.0)

            a = lax.fori_loop(0, levels, one_level, jnp.zeros(square, f32))
        yield
        own = jnp.sum(r * bonus * k, axis=1, keepdims=True)
        a = split2(jnp.where(below, a, 0.0) if fast else a)
        state = carry["state"]
        carry["state"] = state * jnp.exp(total) + scaled(memory, out)
        state_in = split2(scaled(state, into))
        yield
        o = own * v + dot3(a, vs, NN) + dot3(rs, state_in, NT)
        yield
        o = o - jnp.mean(o, axis=1, keepdims=True)
        yield
        rate = lax.rsqrt(jnp.mean(o * o, axis=1, keepdims=True) + NORM_EPS)
        normed = o * rate
        g = gain * (normed - teach[c].astype(f32))
        yield
        g = g - jnp.mean(g, axis=1, keepdims=True) - normed * jnp.mean(
            g * normed, axis=1, keepdims=True
        )
        yield
        state_s[c] = state
        g_s[c] = g * rate
        for held, parts in ((a_s, a), (r_s, rs), (k_s, ks), (v_s, vs)):
            held[c] = jnp.concatenate(parts, axis=1)

    def forward_some(i, state):
        carry = {"state": state}
        in_step(forward(i * unroll + n, carry) for n in range(unroll))
        return carry["state"]

    lax.fori_loop(0, chunks // unroll, forward_some, jnp.zeros((width, width), f32))

    def backward(c, carry):
        q_step, k_step, v_step, r, k, v, lw, total, r_factor, k_factor, into, out = load(c, True)
        a, rs, ks, vs = (halves(held[c]) for held in (a_s, r_s, k_s, v_s))
        g = g_s[c]
        gs = split2(g)
        yield
        memory = dot3(turned(gs), rs, NN)
        pair = dot3(gs, vs, NT)
        yield
        cot = carry["cot"]
        carry["cot"] = cot * jnp.exp(total) + scaled(memory, into)
        cot_out = split2(scaled(cot, out))
        state = state_s[c]
        state_in = split2(scaled(state, into))
        dlw = jnp.sum(state * jnp.exp(total) * cot, axis=0, keepdims=True)
        if fast:
            pairs = split2(jnp.where(below, pair, 0.0))
        yield
        dv = dot3(turned(a), gs, NN) + dot3(ks, cot_out, NT)
        dk = dot3(vs, cot_out, NN)
        if fast:
            dr = dot(
                stacked((gs[0], gs[1], pairs[0], pairs[1], gs[0], pairs[0], pairs[1]), 1),
                stacked((state_in[0], state_in[0], ks[0], ks[0], state_in[1], ks[1], ks[1]), 0),
                NN,
            )
            dk_in = dot4(turned(pairs), rs, NN)
            yield
            k_hat = joined(ks)
            from_earlier = k_hat * dk
            k_in = k_hat * dk_in
            from_later = joined(rs) * dr - k_in
            dlw = dlw - k_in
            dr = r_factor * dr
            dk = k_factor * (dk + dk_in)
        else:
            dr = dot3(gs, state_in, NN)
            from_earlier = joined(ks) * dk
            from_later = joined(rs) * dr
            dr = r_factor * dr
            dk = k_factor * dk

            def one_level(level, parts):
                dr, dk, dlw = parts
                r_by, k_by, r_part, k_part, block, span = level_parts(level, lw, r, k)
                pairs = split2(jnp.where(block & below, pair, 0.0))
                dr_in = r_by * dot3(pairs, k_part, NN)
                dk_in = k_by * dot3(pairs, r_part, TN)
                inside = split3(r * dr_in + k * dk_in)
                return dr + dr_in, dk + dk_in, dlw + sum(dot(span, part, TN) for part in inside)

            dr, dk, dlw = lax.fori_loop(
                0, levels, one_level, (dr, dk, jnp.broadcast_to(dlw, r.shape))
            )
        later, earlier = split3(from_later), split2(from_earlier)
        yield
        dlw = dlw + dot(sides, jnp.concatenate([*later, *earlier], axis=0), NN)
        dv = dv + jnp.sum(r * bonus * k, axis=1, keepdims=True) * g
        own = jnp.sum(v * g, axis=1, keepdims=True)
        yield
        own_r, own_k = own * r, own * k
        dr = dr + bonus * own_k
        dk = dk + bonus * own_r
        dpre = dlw * lw
        dpres = split2(dpre)
        yield
        hid = hid_s[c]
        dz = dot3(dpres, up_twice, NT)
        hid_t = in_s[2, c].T
        carry["up"] += dot(stacked((hid_t, hid_t), 1), stacked(dpres, 0), NN)
        yield
        dz = side_by_side(dz * (1.0 - hid * hid))
        yield
        dxw = dot(stacked((dz, dz), 1), down_deep, NN)
        dz_t = dz.T
        carry["down"] += dot(
            stacked((dz_t, dz_t), 1), stacked((in_s[0, c], in_s[1, c]), 0), NN
        )
        yield
        parts = (dr * q_step, dk * k_step, dv * v_step, dxw * q_step, dpre, own_r * k)
        carry["sums"] = tuple(
            old + jnp.sum(new.reshape(slab // 8, 8, width), axis=0)
            for old, new in zip(carry["sums"], parts)
        )

    def backward_some(i, carry):
        carry = dict(zip(("cot", "up", "down", "sums"), carry))
        in_step(backward(chunks - 1 - (i * unroll + n), carry) for n in range(unroll))
        return tuple(carry.values())

    rank = down[0].shape[0]
    empty = jnp.zeros((2 * rank, width), f32)
    start = (jnp.zeros((width, width), f32), empty, empty, (jnp.zeros((8, width), f32),) * 6)
    _, up_sum, down_sum, sums = lax.fori_loop(0, chunks // unroll, backward_some, start)
    tail = [split2(jnp.sum(part, axis=0, keepdims=True)) for part in sums]
    tail = [high.astype(f32) for high, _ in tail] + [low.astype(f32) for _, low in tail]
    tail.append(jnp.zeros((PACK_TAIL - len(tail), width), f32))
    up_sum, down_sum = (part[:rank] + part[rank:] for part in (up_sum, down_sum))
    return jnp.concatenate([up_sum, down_sum, *tail], axis=0)


def settings_of(head, mix_ref, bonus_ref):
    mix = [mix_ref[n, pl.ds(head, 1), :] for n in range(4)]
    return mix, bonus_ref[pl.ds(head, 1), :]


def in_order(pieces, scratch, place):
    if len(pieces) == 1:
        return pieces[0]
    near = len(pieces)
    for n, piece in enumerate(pieces):
        for far in range(piece.shape[0]):
            scratch[place ^ (far * near + n)] = piece[far]
    return scratch


def head_kernel(head_ref, q_ref, mix_ref, fade_ref, down_ref, up_ref, bonus_ref, *rest):
    slabs, per_device = q_ref.shape[:2]
    pieces, (out_ref, scores, *held, kv_s) = rest[:-15], rest[-15:]
    kv_ref = in_order(pieces, kv_s, head_ref[1])
    copies, shared = out_ref.shape[0], kv_ref.shape[1]
    for n in range(per_device):
        head = head_ref[0] + n
        mix, bonus = settings_of(head, mix_ref, bonus_ref)
        fade = fade_ref[pl.ds(head, 1), :]
        down, up = split2(down_ref[head]), split2(up_ref[head])
        group = n * shared // per_device
        refs = (
            lambda c, n=n: q_ref[c, n],
            lambda c, group=group: kv_ref[c, group, 0],
            lambda c, group=group: kv_ref[c, group, 1],
        )
        teacher = teacher_in_step(*refs, held[0], scores) if slabs <= 16 else None
        worst = decay_phase(
            refs[0], down, up, fade, mix, *held[1:5], math.gcd(4, slabs), teacher
        )
        if teacher is None:
            teacher_phase(*refs, held[0], scores)
        safe = jnp.max(worst) <= SAFE_EXPONENT

        def finish(fast, unroll):
            grads = student_phase(fast, refs, mix, bonus, down, up, held, unroll).astype(bf16)

            def copy_out(at, _):
                out_ref[at, n] = grads
                return 0

            lax.fori_loop(0, copies, copy_out, 0)

        @pl.when(safe)
        def _():
            finish(True, math.gcd(8 if slabs <= 16 else 2, slabs))

        @pl.when(jnp.logical_not(safe))
        def _():
            finish(False, 1)


def head_grads(q, pieces, place, mix, fade, down_t, up, bonus, copies):
    slabs, per_device, slab, width = q.shape
    rank = up.shape[1]
    assert 2 * rank == width
    packed_rows = 2 * rank + PACK_TAIL
    k_slabs = math.gcd(4, slabs)
    small = slabs <= 16
    q_slabs = k_slabs if small else 1
    blocks = slabs // k_slabs
    blocks = blocks * (blocks + 1) // 2 if small else blocks
    kv_shape = (slabs, *pieces[0].shape[1:]) if len(pieces) > 1 else (1, 16, width)
    vmem = pl.BlockSpec(memory_space=pltpu.VMEM)
    return pl.pallas_call(
        head_kernel,
        out_shape=jax.ShapeDtypeStruct((copies, per_device, packed_rows, width), bf16),
        in_specs=[pl.BlockSpec(memory_space=pltpu.SMEM)] + [vmem] * (6 + len(pieces)),
        out_specs=vmem,
        scratch_shapes=[
            pltpu.VMEM((blocks, q_slabs * slab, k_slabs * slab), f32),
            pltpu.VMEM((slabs, slab, width), bf16),
            pltpu.VMEM((slabs, slab, width), f32),
            pltpu.VMEM((slabs, slab, width), f32),
            pltpu.VMEM((slabs, slab, 2 * rank), f32),
            pltpu.VMEM((3, slabs, slab, width), bf16),
            pltpu.VMEM((slabs, width, width), f32),
            pltpu.VMEM((slabs, slab, width), f32),
            pltpu.VMEM((slabs, slab, 2 * slab), bf16),
            pltpu.VMEM((slabs, slab, 2 * width), bf16),
            pltpu.VMEM((slabs, slab, 2 * width), bf16),
            pltpu.VMEM((slabs, slab, 2 * width), bf16),
            pltpu.VMEM((6, slabs if small else 1, slab, width), f32),
            pltpu.VMEM(kv_shape, bf16),
        ],
        compiler_params=pltpu.CompilerParams(
            vmem_limit_bytes=(46 if small else 60) * 1024 * 1024
        ),
    )(place, q, mix, fade, down_t, up, bonus, *pieces)


def pack_queries(q_ref, out_ref):
    slots, _, width = out_ref.shape
    heads = q_ref.shape[1] // width
    for slot in range(slots):
        head = slot * heads // slots
        out_ref[slot] = q_ref[:, head * width : (head + 1) * width]


def pack_memory(group_of, place_ref, k_ref, v_ref, *out_refs):
    width = out_refs[0].shape[-1]
    for n, out_ref in enumerate(out_refs):
        start = group_of(place_ref[0], n) * width
        columns = pl.ds(start if isinstance(start, int) else pl.multiple_of(start, width), width)
        out_ref[0, 0, 0] = k_ref[:, columns]
        out_ref[0, 0, 1] = v_ref[:, columns]


def unpack_kernel(place_ref, *refs):
    *pieces, mix_ref, decay_ref, down_ref, up_ref, bonus_ref = refs
    heads, rank, _ = up_ref.shape
    for n in range(heads):
        if len(pieces) == 1:
            head, packed = n, pieces[0][n * (pieces[0].shape[0] // heads)]
        else:
            near = len(pieces)
            head, packed = place_ref[0] ^ n, pieces[n % near][n // near, 0]
        packed = packed.astype(f32)
        up_ref[head] = packed[:rank]
        down_ref[head] = packed[rank : 2 * rank]
        tail = packed[2 * rank :]
        tail = tail[:6] + tail[6:12]
        for at in range(4):
            mix_ref[at, pl.ds(head, 1), :] = tail[at : at + 1]
        decay_ref[pl.ds(head, 1), :] = tail[4:5]
        bonus_ref[pl.ds(head, 1), :] = tail[5:6]


def exchanged(x, differing, count):
    return lax.ppermute(x, "seq", [(d, d ^ differing) for d in range(count)])


def first_step(parts, near, count):
    got = [exchanged(part, n * near, count) if n else part for n, part in enumerate(parts)]
    return jnp.concatenate(got, axis=0)


def second_step(got, near, count):
    return [exchanged(got, n, count) if n else got for n in range(near)]


def shards(
    probe_vectors,
    mentor_address_vectors,
    mentor_content_vectors,
    previous_position_blend,
    feature_fading_exponent,
    fading_narrowing_matrix,
    fading_widening_matrix,
    diagonal_extra_amount,
):
    slab = probe_vectors.shape[0]
    heads, width, rank = fading_narrowing_matrix.shape
    place = lax.axis_index("seq")
    count = lax.axis_size("seq")
    copies = max(1, count // heads)
    per_device = max(1, heads // count)
    assert heads * copies == per_device * count
    groups = mentor_address_vectors.shape[1] // width
    by_bits = heads == count and count <= 16 and count & (count - 1) == 0 and count % groups == 0
    far, near = groups, count // groups
    vmem = pl.BlockSpec(memory_space=pltpu.VMEM)
    smem = pl.BlockSpec(memory_space=pltpu.SMEM)
    place = place.astype(jnp.int32)
    if by_bits:
        group_of = lambda place, n: (place // near) ^ n
        slots = far
    else:
        shared = max(1, per_device * groups // heads)
        firsts = [(d // copies) * per_device * groups // heads for d in range(count)]
        group_of = lambda _, n: firsts[n // shared] + n % shared
        slots = count * shared
    slot = jax.ShapeDtypeStruct((1, 1, 2, slab, width), bf16)
    kv = pl.pallas_call(
        functools.partial(pack_memory, group_of),
        out_shape=[slot] * slots,
        in_specs=[smem, vmem, vmem],
        out_specs=[vmem] * slots,
    )(place.reshape(1), mentor_address_vectors, mentor_content_vectors)
    if by_bits:
        kv, probe_vectors = lax.optimization_barrier((kv, probe_vectors))
        kv = first_step(kv, near, count)
    q = pl.pallas_call(
        pack_queries,
        out_shape=jax.ShapeDtypeStruct((heads * copies, slab, width), bf16),
        in_specs=[vmem],
        out_specs=vmem,
    )(probe_vectors)
    q = q.reshape(count, per_device, slab, width)
    if by_bits:
        kv, q = lax.optimization_barrier((kv, q))
        pieces = second_step(kv, near, count)
    q = lax.all_to_all(q, "seq", split_axis=0, concat_axis=0, tiled=True)
    if not by_bits:
        kv = jnp.stack(kv).reshape(count, shared, 2, slab, width)
        pieces = [lax.all_to_all(kv, "seq", split_axis=0, concat_axis=0, tiled=True)]
    packed = head_grads(
        q,
        pieces,
        jnp.stack([(place // copies) * per_device, place]),
        previous_position_blend,
        feature_fading_exponent,
        jnp.swapaxes(fading_narrowing_matrix, 1, 2),
        fading_widening_matrix,
        diagonal_extra_amount,
        1 if by_bits else count,
    )
    if by_bits:
        packed = second_step(first_step([packed] * far, near, count), near, count)
    else:
        packed = lax.all_to_all(packed, "seq", split_axis=0, concat_axis=0, tiled=True)
        packed = [packed.reshape(heads * copies, 2 * rank + PACK_TAIL, width)]
    vector = jax.ShapeDtypeStruct((heads, width), f32)
    matrix = jax.ShapeDtypeStruct((heads, rank, width), f32)
    mix, decay, down_t, up, bonus = pl.pallas_call(
        unpack_kernel,
        out_shape=(
            jax.ShapeDtypeStruct((4, heads, width), f32),
            vector,
            matrix,
            matrix,
            vector,
        ),
        in_specs=[smem] + [vmem] * len(packed),
        out_specs=[vmem] * 5,
    )(place.reshape(1), *packed)
    return mix, decay, jnp.swapaxes(down_t, 1, 2), up, bonus


def solution(mesh):
    return jax.shard_map(
        shards,
        mesh=mesh,
        in_specs=(
            P("seq", "head"),
            P("seq", "head"),
            P("seq", "head"),
            P(None, "head", None),
            P("head", None),
            P("head", None, None),
            P("head", None, None),
            P("head", None),
        ),
        out_specs=(
            P(None, "head", None),
            P("head", None),
            P("head", None, None),
            P("head", None, None),
            P("head", None),
        ),
        check_vma=False,
    )
```

```python
import functools
import math

import jax
import jax.numpy as jnp
from jax import lax
from jax.experimental import pallas as pl
from jax.experimental.pallas import tpu as pltpu
from jax.sharding import PartitionSpec as P

NORM_EPS = 0.00064
NEG_LARGE = -1e30
SAFE_EXPONENT = 30.0
PACK_TAIL = 16
LOG2_E = math.log2(math.e)

f32 = jnp.float32
bf16 = jnp.bfloat16

NN = (((1,), (0,)), ((), ()))
NT = (((1,), (1,)), ((), ()))
TN = (((0,), (0,)), ((), ()))


def dot(a, b, dims):
    return lax.dot_general(a, b, dims, preferred_element_type=f32)


def split2(x):
    high = x.astype(bf16)
    return high, (x - high.astype(f32)).astype(bf16)


def split3(x):
    high = x.astype(bf16)
    rest = x - high.astype(f32)
    middle = rest.astype(bf16)
    return high, middle, (rest - middle.astype(f32)).astype(bf16)


def stacked(parts, contracted):
    return jnp.concatenate(parts, axis=contracted)


def dot3(a, b, dims):
    (at,), (bt,) = dims[0]
    return dot(stacked((a[0], a[1], a[0]), at), stacked((b[0], b[0], b[1]), bt), dims)


def dot4(a, b, dims):
    (at,), (bt,) = dims[0]
    return dot(stacked((*a, *a), at), stacked((b[0], b[0], b[1], b[1]), bt), dims)


def twice(parts):
    return tuple(jnp.concatenate([part, part], axis=0) for part in parts)


def side_by_side(x):
    high, low = split2(x)
    return jnp.where(lane_ids(x.shape) < x.shape[1] // 2, high, low)


def rank_deep(parts):
    return jnp.concatenate([parts[0], parts[0], parts[1], jnp.zeros_like(parts[1])], axis=0)


def turned(parts):
    return tuple(part.T for part in parts)


def joined(parts):
    return parts[0].astype(f32) + parts[1].astype(f32)


def sums_of(zero_one, parts):
    return dot(stacked((zero_one,) * len(parts), 1), stacked(parts, 0), NN)


def row_ids(shape):
    return lax.broadcasted_iota(jnp.int32, shape, 0)


def lane_ids(shape):
    return lax.broadcasted_iota(jnp.int32, shape, 1)


def zero_one(condition):
    return jnp.where(condition, 1.0, 0.0).astype(bf16)


def with_shift(at, first, slabs=1):
    now = slabs_of(at, first, slabs).astype(f32)
    fixed = isinstance(first, int)
    last = at(max(first - 1, 0) if fixed else jnp.maximum(first - 1, 0))
    tail = last[last.shape[0] - 16 :].astype(f32)[15:16]
    if not fixed:
        tail = jnp.where(first > 0, tail, 0.0)
    elif first == 0:
        tail = jnp.zeros_like(tail)
    earlier = jnp.where(row_ids(now.shape) == 0, tail, pltpu.roll(now, 1, 0))
    return now, earlier - now


def slabs_of(at, first, slabs):
    return jnp.concatenate([at(first + n) for n in range(slabs)], axis=0)


def teacher_phase(q_at, k_at, v_at, teach, scores):
    slabs, slab, width = teach.shape
    _, q_rows, k_rows = scores.shape
    q_slabs, k_slabs = q_rows // slab, k_rows // slab
    scale = LOG2_E / math.sqrt(width)

    def q_block(i, _):
        q = slabs_of(q_at, i * q_slabs, q_slabs)
        last = (i * q_slabs + q_slabs - 1) // k_slabs

        def score_block(j, top, edge=False):
            s = dot(q, slabs_of(k_at, j * k_slabs, k_slabs), NT) * scale
            if edge:
                seen = i * q_rows + row_ids(s.shape) >= j * k_rows + lane_ids(s.shape)
                s = jnp.where(seen, s, NEG_LARGE)
            scores[j] = s
            for n in range(k_rows // 128):
                top = jnp.maximum(top, s[:, n * 128 : (n + 1) * 128])
            return top

        top = lax.fori_loop(0, last, score_block, jnp.full((q_rows, 128), NEG_LARGE, f32))
        top = score_block(last, top, True)
        row_top = jnp.max(top, axis=1, keepdims=True)

        def value_block(j, carry):
            total, accum = carry
            p = jnp.exp2(scores[j] - row_top)
            for n in range(k_rows // 128):
                total = total + p[:, n * 128 : (n + 1) * 128]
            return total, accum + dot(p.astype(bf16), slabs_of(v_at, j * k_slabs, k_slabs), NN)

        total, accum = lax.fori_loop(
            0,
            last + 1,
            value_block,
            (jnp.zeros((q_rows, 128), f32), jnp.zeros((q_rows, width), f32)),
        )
        out = accum / jnp.sum(total, axis=1, keepdims=True)
        teach[pl.ds(i * q_slabs, q_slabs)] = out.astype(bf16).reshape(q_slabs, slab, width)
        return 0

    lax.fori_loop(0, slabs // q_slabs, q_block, 0)


def teacher_in_step(q_at, k_at, v_at, teach, scores):
    slabs, slab, width = teach.shape
    _, rows, _ = scores.shape
    each = rows // slab
    scale = LOG2_E / math.sqrt(width)

    def lanes(x):
        return [x[:, n * 128 : (n + 1) * 128] for n in range(rows // 128)]

    def q_block(i):
        held = [i * (i + 1) // 2 + j for j in range(i + 1)]
        q = slabs_of(q_at, i * each, each)
        top = jnp.full((rows, 128), NEG_LARGE, f32)
        for j in range(i + 1):
            s = dot(q, slabs_of(k_at, j * each, each), NT) * scale
            if j == i:
                s = jnp.where(row_ids(s.shape) >= lane_ids(s.shape), s, NEG_LARGE)
            scores[held[j]] = s
            top = functools.reduce(jnp.maximum, lanes(s), top)
            yield
        top = jnp.max(top, axis=1, keepdims=True)
        total, accum = jnp.zeros((rows, 128), f32), jnp.zeros((rows, width), f32)
        for j in range(i + 1):
            p = jnp.exp2(scores[held[j]] - top)
            total = sum(lanes(p), total)
            accum = accum + dot(p.astype(bf16), slabs_of(v_at, j * each, each), NN)
            yield
        out = (accum / jnp.sum(total, axis=1, keepdims=True)).astype(bf16)
        teach[i * each : (i + 1) * each] = out.reshape(each, slab, width)

    return [q_block(i) for i in range(slabs // each)]


def decay_phase(q_at, down, up, fade, mix, lw_s, ex_s, hid_s, in_s, slabs, together):
    count, slab, width = lw_s.shape
    square = (slab, slab)
    before = zero_one(row_ids(square) > lane_ids(square))

    def block(i, carry):
        first = i * slabs
        q, q_step = with_shift(q_at, first, slabs)
        decay_in = split2(q + mix[3] * q_step)
        yield
        hid = dot3(decay_in, twice(down), NT)
        yield
        hid = jnp.tanh(hid)
        hid_parts = side_by_side(hid)
        yield
        lw = dot(stacked((hid_parts,) * 2, 1), rank_deep(up), NN)
        yield
        lw = -jnp.exp(fade + lw)
        hid_s[pl.ds(first, slabs)] = hid.reshape(slabs, slab, width)
        for n, part in enumerate((*decay_in, hid_parts)):
            in_s[n, pl.ds(first, slabs)] = part.reshape(slabs, slab, width)
        lw_s[pl.ds(first, slabs)] = lw.reshape(slabs, slab, width)
        yield
        for n in range(slabs):
            part = lw[n * slab : (n + 1) * slab]
            ex = sums_of(before, split3(part))
            ex_s[first + n] = ex
            middle = ex[slab // 2 : slab // 2 + 1]
            total = ex[slab - 1 :] + part[slab - 1 :]
            carry["worst"] = jnp.maximum(
                carry["worst"], jnp.maximum(-middle, middle - total)
            )

    def alone(i, worst):
        carry = {"worst": worst}
        in_step([block(i, carry)])
        return carry["worst"]

    none = jnp.zeros((1, width), f32)
    if together is None:
        return lax.fori_loop(0, count // slabs, alone, none)
    carry = {"worst": none}
    in_step([*(block(i, carry) for i in range(count // slabs)), *together])
    return carry["worst"]


def level_parts(level, lw, r, k):
    square = (lw.shape[0], lw.shape[0])
    t, m = row_ids(square), lane_ids(square)
    edge = ((t >> (level + 1)) << (level + 1)) + (1 << level) - 1
    upper = ((t >> level) & 1) == 1
    lower = ((t >> level) & 1) == 0
    span = zero_one((upper & (m > edge) & (m < t)) | (lower & (m > t) & (m <= edge)))
    factor = jnp.exp(sums_of(span, split3(lw)))
    upper_rows = ((row_ids(r.shape) >> level) & 1) == 1
    r_factor = jnp.where(upper_rows, factor, 0.0)
    k_factor = jnp.where(upper_rows, 0.0, factor)
    same = (t >> (level + 1)) == (m >> (level + 1))
    return r_factor, k_factor, split2(r * r_factor), split2(k * k_factor), same, span


def halves(x):
    width = x.shape[1] // 2
    return x[:, :width], x[:, width:]


def in_step(chunks):
    chunks = list(chunks)
    while chunks:
        chunks = [chunk for chunk in chunks if next(chunk, chunk) is None]


def student_phase(fast, refs, mix, bonus, down, up, scratch, unroll):
    teach, lw_s, ex_s, hid_s, in_s, state_s, g_s, a_s, r_s, k_s, v_s, kept = scratch
    keep = kept.shape[1] == lw_s.shape[0]
    chunks, slab, width = lw_s.shape
    tokens = chunks * slab
    levels = slab.bit_length() - 1
    square = (slab, slab)
    t, m = row_ids(square), lane_ids(square)
    below = t > m
    after, before = zero_one(t < m), zero_one(below)
    sides = jnp.concatenate([after] * 3 + [before] * 2, axis=1)
    up_twice, down_deep = twice(up), rank_deep(down)
    gain = 2.0 / tokens

    def rows_of(c, again):
        if keep and again:
            return tuple(kept[n, c] for n in range(6))
        steps = []
        rows = []
        for n, at in enumerate(refs):
            now, step = with_shift(at, c)
            rows.append(now + mix[n] * step)
            steps.append(step)
        if keep:
            for n, part in enumerate((*rows, *steps)):
                kept[n, c] = part
        return (*rows, *steps)

    def load(c, again=False):
        r, k, v, q_step, k_step, v_step = rows_of(c, again)
        lw, ex = lw_s[c], ex_s[c]
        total = ex[slab - 1 :] + lw[slab - 1 :]
        if fast:
            middle = ex[slab // 2 : slab // 2 + 1]
            r_factor = jnp.exp(ex - middle)
            k_factor = jnp.exp(middle - ex - lw)
            into, out = jnp.exp(middle), jnp.exp(total - middle)
        else:
            r_factor = jnp.exp(ex)
            k_factor = jnp.exp(sums_of(after, split3(lw)))
            into = out = None
        return q_step, k_step, v_step, r, k, v, lw, total, r_factor, k_factor, into, out

    def scaled(x, by):
        return x if by is None else x * by

    def forward(c, carry):
        _, _, _, r, k, v, lw, total, r_factor, k_factor, into, out = load(c)
        rs, ks, vs = split2(r * r_factor), split2(k * k_factor), split2(v)
        yield
        memory = dot3(turned(vs), ks, NN)
        if fast:
            a = dot3(rs, ks, NT)
        else:

            def one_level(level, a):
                _, _, r_part, k_part, block, _ = level_parts(level, lw, r, k)
                return a + jnp.where(block, dot3(r_part, k_part, NT), 0.0)

            a = lax.fori_loop(0, levels, one_level, jnp.zeros(square, f32))
        yield
        own = jnp.sum(r * bonus * k, axis=1, keepdims=True)
        a = split2(jnp.where(below, a, 0.0) if fast else a)
        state = carry["state"]
        carry["state"] = state * jnp.exp(total) + scaled(memory, out)
        state_in = split2(scaled(state, into))
        yield
        o = own * v + dot3(a, vs, NN) + dot3(rs, state_in, NT)
        yield
        o = o - jnp.mean(o, axis=1, keepdims=True)
        yield
        rate = lax.rsqrt(jnp.mean(o * o, axis=1, keepdims=True) + NORM_EPS)
        normed = o * rate
        g = gain * (normed - teach[c].astype(f32))
        yield
        g = g - jnp.mean(g, axis=1, keepdims=True) - normed * jnp.mean(
            g * normed, axis=1, keepdims=True
        )
        yield
        state_s[c] = state
        g_s[c] = g * rate
        for held, parts in ((a_s, a), (r_s, rs), (k_s, ks), (v_s, vs)):
            held[c] = jnp.concatenate(parts, axis=1)

    def forward_some(i, state):
        carry = {"state": state}
        in_step(forward(i * unroll + n, carry) for n in range(unroll))
        return carry["state"]

    lax.fori_loop(0, chunks // unroll, forward_some, jnp.zeros((width, width), f32))

    def backward(c, carry):
        q_step, k_step, v_step, r, k, v, lw, total, r_factor, k_factor, into, out = load(c, True)
        a, rs, ks, vs = (halves(held[c]) for held in (a_s, r_s, k_s, v_s))
        g = g_s[c]
        gs = split2(g)
        yield
        memory = dot3(turned(gs), rs, NN)
        pair = dot3(gs, vs, NT)
        yield
        cot = carry["cot"]
        carry["cot"] = cot * jnp.exp(total) + scaled(memory, into)
        cot_out = split2(scaled(cot, out))
        state = state_s[c]
        state_in = split2(scaled(state, into))
        dlw = jnp.sum(state * jnp.exp(total) * cot, axis=0, keepdims=True)
        if fast:
            pairs = split2(jnp.where(below, pair, 0.0))
        yield
        dv = dot3(turned(a), gs, NN) + dot3(ks, cot_out, NT)
        dk = dot3(vs, cot_out, NN)
        if fast:
            dr = dot(
                stacked((gs[0], gs[1], pairs[0], pairs[1], gs[0], pairs[0], pairs[1]), 1),
                stacked((state_in[0], state_in[0], ks[0], ks[0], state_in[1], ks[1], ks[1]), 0),
                NN,
            )
            dk_in = dot4(turned(pairs), rs, NN)
            yield
            k_hat = joined(ks)
            from_earlier = k_hat * dk
            k_in = k_hat * dk_in
            from_later = joined(rs) * dr - k_in
            dlw = dlw - k_in
            dr = r_factor * dr
            dk = k_factor * (dk + dk_in)
        else:
            dr = dot3(gs, state_in, NN)
            from_earlier = joined(ks) * dk
            from_later = joined(rs) * dr
            dr = r_factor * dr
            dk = k_factor * dk

            def one_level(level, parts):
                dr, dk, dlw = parts
                r_by, k_by, r_part, k_part, block, span = level_parts(level, lw, r, k)
                pairs = split2(jnp.where(block & below, pair, 0.0))
                dr_in = r_by * dot3(pairs, k_part, NN)
                dk_in = k_by * dot3(pairs, r_part, TN)
                inside = split3(r * dr_in + k * dk_in)
                return dr + dr_in, dk + dk_in, dlw + sum(dot(span, part, TN) for part in inside)

            dr, dk, dlw = lax.fori_loop(
                0, levels, one_level, (dr, dk, jnp.broadcast_to(dlw, r.shape))
            )
        later, earlier = split3(from_later), split2(from_earlier)
        yield
        dlw = dlw + dot(sides, jnp.concatenate([*later, *earlier], axis=0), NN)
        dv = dv + jnp.sum(r * bonus * k, axis=1, keepdims=True) * g
        own = jnp.sum(v * g, axis=1, keepdims=True)
        yield
        own_r, own_k = own * r, own * k
        dr = dr + bonus * own_k
        dk = dk + bonus * own_r
        dpre = dlw * lw
        dpres = split2(dpre)
        yield
        hid = hid_s[c]
        dz = dot3(dpres, up_twice, NT)
        hid_t = in_s[2, c].T
        carry["up"] += dot(stacked((hid_t, hid_t), 1), stacked(dpres, 0), NN)
        yield
        dz = side_by_side(dz * (1.0 - hid * hid))
        yield
        dxw = dot(stacked((dz, dz), 1), down_deep, NN)
        dz_t = dz.T
        carry["down"] += dot(
            stacked((dz_t, dz_t), 1), stacked((in_s[0, c], in_s[1, c]), 0), NN
        )
        yield
        parts = (dr * q_step, dk * k_step, dv * v_step, dxw * q_step, dpre, own_r * k)
        carry["sums"] = tuple(
            old + jnp.sum(new.reshape(slab // 8, 8, width), axis=0)
            for old, new in zip(carry["sums"], parts)
        )

    def backward_some(i, carry):
        carry = dict(zip(("cot", "up", "down", "sums"), carry))
        in_step(backward(chunks - 1 - (i * unroll + n), carry) for n in range(unroll))
        return tuple(carry.values())

    rank = down[0].shape[0]
    empty = jnp.zeros((2 * rank, width), f32)
    start = (jnp.zeros((width, width), f32), empty, empty, (jnp.zeros((8, width), f32),) * 6)
    _, up_sum, down_sum, sums = lax.fori_loop(0, chunks // unroll, backward_some, start)
    tail = [split2(jnp.sum(part, axis=0, keepdims=True)) for part in sums]
    tail = [high.astype(f32) for high, _ in tail] + [low.astype(f32) for _, low in tail]
    tail.append(jnp.zeros((PACK_TAIL - len(tail), width), f32))
    up_sum, down_sum = (part[:rank] + part[rank:] for part in (up_sum, down_sum))
    return jnp.concatenate([up_sum, down_sum, *tail], axis=0)


def settings_of(head, mix_ref, bonus_ref):
    mix = [mix_ref[n, pl.ds(head, 1), :] for n in range(4)]
    return mix, bonus_ref[pl.ds(head, 1), :]


def in_order(pieces, scratch, place):
    if len(pieces) == 1:
        return pieces[0]
    near = len(pieces)
    for n, piece in enumerate(pieces):
        for far in range(piece.shape[0]):
            scratch[place ^ (far * near + n)] = piece[far]
    return scratch


def head_kernel(head_ref, q_ref, mix_ref, fade_ref, down_ref, up_ref, bonus_ref, *rest):
    slabs, per_device = q_ref.shape[:2]
    pieces, (out_ref, scores, *held, kv_s) = rest[:-15], rest[-15:]
    kv_ref = in_order(pieces, kv_s, head_ref[1])
    copies, shared = out_ref.shape[0], kv_ref.shape[1]
    for n in range(per_device):
        head = head_ref[0] + n
        mix, bonus = settings_of(head, mix_ref, bonus_ref)
        fade = fade_ref[pl.ds(head, 1), :]
        down, up = split2(down_ref[head]), split2(up_ref[head])
        group = n * shared // per_device
        refs = (
            lambda c, n=n: q_ref[c, n],
            lambda c, group=group: kv_ref[c, group, 0],
            lambda c, group=group: kv_ref[c, group, 1],
        )
        teacher = teacher_in_step(*refs, held[0], scores) if slabs <= 16 else None
        worst = decay_phase(
            refs[0], down, up, fade, mix, *held[1:5], math.gcd(4, slabs), teacher
        )
        if teacher is None:
            teacher_phase(*refs, held[0], scores)
        safe = jnp.max(worst) <= SAFE_EXPONENT

        def finish(fast, unroll):
            grads = student_phase(fast, refs, mix, bonus, down, up, held, unroll).astype(bf16)

            def copy_out(at, _):
                out_ref[at, n] = grads
                return 0

            lax.fori_loop(0, copies, copy_out, 0)

        @pl.when(safe)
        def _():
            finish(True, math.gcd(16 if slabs <= 16 else 2, slabs))

        @pl.when(jnp.logical_not(safe))
        def _():
            finish(False, 1)


def head_grads(q, pieces, place, mix, fade, down_t, up, bonus, copies):
    slabs, per_device, slab, width = q.shape
    rank = up.shape[1]
    assert 2 * rank == width
    packed_rows = 2 * rank + PACK_TAIL
    k_slabs = math.gcd(4, slabs)
    small = slabs <= 16
    q_slabs = k_slabs if small else 1
    blocks = slabs // k_slabs
    blocks = blocks * (blocks + 1) // 2 if small else blocks
    kv_shape = (slabs, *pieces[0].shape[1:]) if len(pieces) > 1 else (1, 16, width)
    vmem = pl.BlockSpec(memory_space=pltpu.VMEM)
    return pl.pallas_call(
        head_kernel,
        out_shape=jax.ShapeDtypeStruct((copies, per_device, packed_rows, width), bf16),
        in_specs=[pl.BlockSpec(memory_space=pltpu.SMEM)] + [vmem] * (6 + len(pieces)),
        out_specs=vmem,
        scratch_shapes=[
            pltpu.VMEM((blocks, q_slabs * slab, k_slabs * slab), f32),
            pltpu.VMEM((slabs, slab, width), bf16),
            pltpu.VMEM((slabs, slab, width), f32),
            pltpu.VMEM((slabs, slab, width), f32),
            pltpu.VMEM((slabs, slab, 2 * rank), f32),
            pltpu.VMEM((3, slabs, slab, width), bf16),
            pltpu.VMEM((slabs, width, width), f32),
            pltpu.VMEM((slabs, slab, width), f32),
            pltpu.VMEM((slabs, slab, 2 * slab), bf16),
            pltpu.VMEM((slabs, slab, 2 * width), bf16),
            pltpu.VMEM((slabs, slab, 2 * width), bf16),
            pltpu.VMEM((slabs, slab, 2 * width), bf16),
            pltpu.VMEM((6, slabs if small else 1, slab, width), f32),
            pltpu.VMEM(kv_shape, bf16),
        ],
        compiler_params=pltpu.CompilerParams(
            vmem_limit_bytes=(46 if small else 60) * 1024 * 1024
        ),
    )(place, q, mix, fade, down_t, up, bonus, *pieces)


def pack_queries(q_ref, out_ref):
    slots, _, width = out_ref.shape
    heads = q_ref.shape[1] // width
    for slot in range(slots):
        head = slot * heads // slots
        out_ref[slot] = q_ref[:, head * width : (head + 1) * width]


def pack_memory(group_of, place_ref, k_ref, v_ref, *out_refs):
    width = out_refs[0].shape[-1]
    for n, out_ref in enumerate(out_refs):
        start = group_of(place_ref[0], n) * width
        columns = pl.ds(start if isinstance(start, int) else pl.multiple_of(start, width), width)
        out_ref[0, 0, 0] = k_ref[:, columns]
        out_ref[0, 0, 1] = v_ref[:, columns]


def unpack_kernel(place_ref, *refs):
    *pieces, mix_ref, decay_ref, down_ref, up_ref, bonus_ref = refs
    heads, rank, _ = up_ref.shape
    for n in range(heads):
        if len(pieces) == 1:
            head, packed = n, pieces[0][n * (pieces[0].shape[0] // heads)]
        else:
            near = len(pieces)
            head, packed = place_ref[0] ^ n, pieces[n % near][n // near, 0]
        packed = packed.astype(f32)
        up_ref[head] = packed[:rank]
        down_ref[head] = packed[rank : 2 * rank]
        tail = packed[2 * rank :]
        tail = tail[:6] + tail[6:12]
        for at in range(4):
            mix_ref[at, pl.ds(head, 1), :] = tail[at : at + 1]
        decay_ref[pl.ds(head, 1), :] = tail[4:5]
        bonus_ref[pl.ds(head, 1), :] = tail[5:6]


def exchanged(x, differing, count):
    return lax.ppermute(x, "seq", [(d, d ^ differing) for d in range(count)])


def first_step(parts, near, count):
    got = [exchanged(part, n * near, count) if n else part for n, part in enumerate(parts)]
    return jnp.concatenate(got, axis=0)


def second_step(got, near, count):
    return [exchanged(got, n, count) if n else got for n in range(near)]


def shards(
    probe_vectors,
    mentor_address_vectors,
    mentor_content_vectors,
    previous_position_blend,
    feature_fading_exponent,
    fading_narrowing_matrix,
    fading_widening_matrix,
    diagonal_extra_amount,
):
    slab = probe_vectors.shape[0]
    heads, width, rank = fading_narrowing_matrix.shape
    place = lax.axis_index("seq")
    count = lax.axis_size("seq")
    copies = max(1, count // heads)
    per_device = max(1, heads // count)
    assert heads * copies == per_device * count
    groups = mentor_address_vectors.shape[1] // width
    by_bits = heads == count and count <= 16 and count & (count - 1) == 0 and count % groups == 0
    far, near = groups, count // groups
    vmem = pl.BlockSpec(memory_space=pltpu.VMEM)
    smem = pl.BlockSpec(memory_space=pltpu.SMEM)
    place = place.astype(jnp.int32)
    if by_bits:
        group_of = lambda place, n: (place // near) ^ n
        slots = far
    else:
        shared = max(1, per_device * groups // heads)
        firsts = [(d // copies) * per_device * groups // heads for d in range(count)]
        group_of = lambda _, n: firsts[n // shared] + n % shared
        slots = count * shared
    slot = jax.ShapeDtypeStruct((1, 1, 2, slab, width), bf16)
    kv = pl.pallas_call(
        functools.partial(pack_memory, group_of),
        out_shape=[slot] * slots,
        in_specs=[smem, vmem, vmem],
        out_specs=[vmem] * slots,
    )(place.reshape(1), mentor_address_vectors, mentor_content_vectors)
    if by_bits:
        kv, probe_vectors = lax.optimization_barrier((kv, probe_vectors))
        kv = first_step(kv, near, count)
    q = pl.pallas_call(
        pack_queries,
        out_shape=jax.ShapeDtypeStruct((heads * copies, slab, width), bf16),
        in_specs=[vmem],
        out_specs=vmem,
    )(probe_vectors)
    q = q.reshape(count, per_device, slab, width)
    if by_bits:
        kv, q = lax.optimization_barrier((kv, q))
        pieces = second_step(kv, near, count)
    q = lax.all_to_all(q, "seq", split_axis=0, concat_axis=0, tiled=True)
    if not by_bits:
        kv = jnp.stack(kv).reshape(count, shared, 2, slab, width)
        pieces = [lax.all_to_all(kv, "seq", split_axis=0, concat_axis=0, tiled=True)]
    packed = head_grads(
        q,
        pieces,
        jnp.stack([(place // copies) * per_device, place]),
        previous_position_blend,
        feature_fading_exponent,
        jnp.swapaxes(fading_narrowing_matrix, 1, 2),
        fading_widening_matrix,
        diagonal_extra_amount,
        1 if by_bits else count,
    )
    if by_bits:
        packed = second_step(first_step([packed] * far, near, count), near, count)
    else:
        packed = lax.all_to_all(packed, "seq", split_axis=0, concat_axis=0, tiled=True)
        packed = [packed.reshape(heads * copies, 2 * rank + PACK_TAIL, width)]
    vector = jax.ShapeDtypeStruct((heads, width), f32)
    matrix = jax.ShapeDtypeStruct((heads, rank, width), f32)
    mix, decay, down_t, up, bonus = pl.pallas_call(
        unpack_kernel,
        out_shape=(
            jax.ShapeDtypeStruct((4, heads, width), f32),
            vector,
            matrix,
            matrix,
            vector,
        ),
        in_specs=[smem] + [vmem] * len(packed),
        out_specs=[vmem] * 5,
    )(place.reshape(1), *packed)
    return mix, decay, jnp.swapaxes(down_t, 1, 2), up, bonus


def solution(mesh):
    return jax.shard_map(
        shards,
        mesh=mesh,
        in_specs=(
            P("seq", "head"),
            P("seq", "head"),
            P("seq", "head"),
            P(None, "head", None),
            P("head", None),
            P("head", None, None),
            P("head", None, None),
            P("head", None),
        ),
        out_specs=(
            P(None, "head", None),
            P("head", None),
            P("head", None, None),
            P("head", None, None),
            P("head", None),
        ),
        check_vma=False,
    )
```

```python
import functools
import math

import jax
import jax.numpy as jnp
from jax import lax
from jax.experimental import pallas as pl
from jax.experimental.pallas import tpu as pltpu
from jax.sharding import PartitionSpec as P

NORM_EPS = 0.00064
NEG_LARGE = -1e30
SAFE_EXPONENT = 30.0
PACK_TAIL = 16
LOG2_E = math.log2(math.e)

f32 = jnp.float32
bf16 = jnp.bfloat16

NN = (((1,), (0,)), ((), ()))
NT = (((1,), (1,)), ((), ()))
TN = (((0,), (0,)), ((), ()))


def dot(a, b, dims):
    return lax.dot_general(a, b, dims, preferred_element_type=f32)


def split2(x):
    high = x.astype(bf16)
    return high, (x - high.astype(f32)).astype(bf16)


def split3(x):
    high = x.astype(bf16)
    rest = x - high.astype(f32)
    middle = rest.astype(bf16)
    return high, middle, (rest - middle.astype(f32)).astype(bf16)


def stacked(parts, contracted):
    return jnp.concatenate(parts, axis=contracted)


def dot3(a, b, dims):
    (at,), (bt,) = dims[0]
    return dot(stacked((a[0], a[1], a[0]), at), stacked((b[0], b[0], b[1]), bt), dims)


def dot4(a, b, dims):
    (at,), (bt,) = dims[0]
    return dot(stacked((*a, *a), at), stacked((b[0], b[0], b[1], b[1]), bt), dims)


def twice(parts):
    return tuple(jnp.concatenate([part, part], axis=0) for part in parts)


def side_by_side(x):
    high, low = split2(x)
    return jnp.where(lane_ids(x.shape) < x.shape[1] // 2, high, low)


def rank_deep(parts):
    return jnp.concatenate([parts[0], parts[0], parts[1], jnp.zeros_like(parts[1])], axis=0)


def turned(parts):
    return tuple(part.T for part in parts)


def joined(parts):
    return parts[0].astype(f32) + parts[1].astype(f32)


def sums_of(zero_one, parts):
    return dot(stacked((zero_one,) * len(parts), 1), stacked(parts, 0), NN)


def row_ids(shape):
    return lax.broadcasted_iota(jnp.int32, shape, 0)


def lane_ids(shape):
    return lax.broadcasted_iota(jnp.int32, shape, 1)


def zero_one(condition):
    return jnp.where(condition, 1.0, 0.0).astype(bf16)


def with_shift(at, first, slabs=1):
    now = slabs_of(at, first, slabs).astype(f32)
    fixed = isinstance(first, int)
    last = at(max(first - 1, 0) if fixed else jnp.maximum(first - 1, 0))
    tail = last[last.shape[0] - 16 :].astype(f32)[15:16]
    if not fixed:
        tail = jnp.where(first > 0, tail, 0.0)
    elif first == 0:
        tail = jnp.zeros_like(tail)
    earlier = jnp.where(row_ids(now.shape) == 0, tail, pltpu.roll(now, 1, 0))
    return now, earlier - now


def slabs_of(at, first, slabs):
    return jnp.concatenate([at(first + n) for n in range(slabs)], axis=0)


def teacher_phase(q_at, k_at, v_at, teach, scores):
    slabs, slab, width = teach.shape
    _, q_rows, k_rows = scores.shape
    q_slabs, k_slabs = q_rows // slab, k_rows // slab
    scale = LOG2_E / math.sqrt(width)

    def q_block(i, _):
        q = slabs_of(q_at, i * q_slabs, q_slabs)
        last = (i * q_slabs + q_slabs - 1) // k_slabs

        def score_block(j, top, edge=False):
            s = dot(q, slabs_of(k_at, j * k_slabs, k_slabs), NT) * scale
            if edge:
                seen = i * q_rows + row_ids(s.shape) >= j * k_rows + lane_ids(s.shape)
                s = jnp.where(seen, s, NEG_LARGE)
            scores[j] = s
            for n in range(k_rows // 128):
                top = jnp.maximum(top, s[:, n * 128 : (n + 1) * 128])
            return top

        top = lax.fori_loop(0, last, score_block, jnp.full((q_rows, 128), NEG_LARGE, f32))
        top = score_block(last, top, True)
        row_top = jnp.max(top, axis=1, keepdims=True)

        def value_block(j, carry):
            total, accum = carry
            p = jnp.exp2(scores[j] - row_top)
            for n in range(k_rows // 128):
                total = total + p[:, n * 128 : (n + 1) * 128]
            return total, accum + dot(p.astype(bf16), slabs_of(v_at, j * k_slabs, k_slabs), NN)

        total, accum = lax.fori_loop(
            0,
            last + 1,
            value_block,
            (jnp.zeros((q_rows, 128), f32), jnp.zeros((q_rows, width), f32)),
        )
        out = accum / jnp.sum(total, axis=1, keepdims=True)
        teach[pl.ds(i * q_slabs, q_slabs)] = out.astype(bf16).reshape(q_slabs, slab, width)
        return 0

    lax.fori_loop(0, slabs // q_slabs, q_block, 0)


def teacher_in_step(q_at, k_at, v_at, teach, scores):
    slabs, slab, width = teach.shape
    _, rows, _ = scores.shape
    each = rows // slab
    scale = LOG2_E / math.sqrt(width)

    def lanes(x):
        return [x[:, n * 128 : (n + 1) * 128] for n in range(rows // 128)]

    def q_block(i):
        held = [i * (i + 1) // 2 + j for j in range(i + 1)]
        q = slabs_of(q_at, i * each, each)
        top = jnp.full((rows, 128), NEG_LARGE, f32)
        for j in range(i + 1):
            s = dot(q, slabs_of(k_at, j * each, each), NT) * scale
            if j == i:
                s = jnp.where(row_ids(s.shape) >= lane_ids(s.shape), s, NEG_LARGE)
            scores[held[j]] = s
            top = functools.reduce(jnp.maximum, lanes(s), top)
            yield
        top = jnp.max(top, axis=1, keepdims=True)
        total, accum = jnp.zeros((rows, 128), f32), jnp.zeros((rows, width), f32)
        for j in range(i + 1):
            p = jnp.exp2(scores[held[j]] - top)
            total = sum(lanes(p), total)
            accum = accum + dot(p.astype(bf16), slabs_of(v_at, j * each, each), NN)
            yield
        out = (accum / jnp.sum(total, axis=1, keepdims=True)).astype(bf16)
        teach[i * each : (i + 1) * each] = out.reshape(each, slab, width)

    return [q_block(i) for i in range(slabs // each)]


def decay_phase(q_at, down, up, fade, mix, lw_s, ex_s, hid_s, in_s, slabs, together):
    count, slab, width = lw_s.shape
    square = (slab, slab)
    before = zero_one(row_ids(square) > lane_ids(square))

    def block(i, carry):
        first = i * slabs
        q, q_step = with_shift(q_at, first, slabs)
        decay_in = split2(q + mix[3] * q_step)
        yield
        hid = dot3(decay_in, twice(down), NT)
        yield
        hid = jnp.tanh(hid)
        hid_parts = side_by_side(hid)
        yield
        lw = dot(stacked((hid_parts,) * 2, 1), rank_deep(up), NN)
        yield
        lw = -jnp.exp(fade + lw)
        hid_s[pl.ds(first, slabs)] = hid.reshape(slabs, slab, width)
        for n, part in enumerate((*decay_in, hid_parts)):
            in_s[n, pl.ds(first, slabs)] = part.reshape(slabs, slab, width)
        lw_s[pl.ds(first, slabs)] = lw.reshape(slabs, slab, width)
        yield
        for n in range(slabs):
            part = lw[n * slab : (n + 1) * slab]
            ex = sums_of(before, split3(part))
            ex_s[first + n] = ex
            middle = ex[slab // 2 : slab // 2 + 1]
            total = ex[slab - 1 :] + part[slab - 1 :]
            carry["worst"] = jnp.maximum(
                carry["worst"], jnp.maximum(-middle, middle - total)
            )

    def alone(i, worst):
        carry = {"worst": worst}
        in_step([block(i, carry)])
        return carry["worst"]

    none = jnp.zeros((1, width), f32)
    if together is None:
        return lax.fori_loop(0, count // slabs, alone, none)
    carry = {"worst": none}
    in_step([*(block(i, carry) for i in range(count // slabs)), *together])
    return carry["worst"]


def level_parts(level, lw, r, k):
    square = (lw.shape[0], lw.shape[0])
    t, m = row_ids(square), lane_ids(square)
    edge = ((t >> (level + 1)) << (level + 1)) + (1 << level) - 1
    upper = ((t >> level) & 1) == 1
    lower = ((t >> level) & 1) == 0
    span = zero_one((upper & (m > edge) & (m < t)) | (lower & (m > t) & (m <= edge)))
    factor = jnp.exp(sums_of(span, split3(lw)))
    upper_rows = ((row_ids(r.shape) >> level) & 1) == 1
    r_factor = jnp.where(upper_rows, factor, 0.0)
    k_factor = jnp.where(upper_rows, 0.0, factor)
    same = (t >> (level + 1)) == (m >> (level + 1))
    return r_factor, k_factor, split2(r * r_factor), split2(k * k_factor), same, span


def halves(x):
    width = x.shape[1] // 2
    return x[:, :width], x[:, width:]


def in_step(chunks):
    chunks = list(chunks)
    while chunks:
        chunks = [chunk for chunk in chunks if next(chunk, chunk) is None]


def student_phase(fast, refs, mix, bonus, down, up, scratch, unroll):
    teach, lw_s, ex_s, hid_s, in_s, state_s, g_s, a_s, r_s, k_s, v_s, kept = scratch
    keep = kept.shape[1] == lw_s.shape[0]
    chunks, slab, width = lw_s.shape
    tokens = chunks * slab
    levels = slab.bit_length() - 1
    square = (slab, slab)
    t, m = row_ids(square), lane_ids(square)
    below = t > m
    after, before = zero_one(t < m), zero_one(below)
    sides = jnp.concatenate([after] * 3 + [before] * 2, axis=1)
    up_twice, down_deep = twice(up), rank_deep(down)
    gain = 2.0 / tokens

    def rows_of(c, again):
        if keep and again:
            return tuple(kept[n, c] for n in range(6))
        steps = []
        rows = []
        for n, at in enumerate(refs):
            now, step = with_shift(at, c)
            rows.append(now + mix[n] * step)
            steps.append(step)
        if keep:
            for n, part in enumerate((*rows, *steps)):
                kept[n, c] = part
        return (*rows, *steps)

    def load(c, again=False):
        r, k, v, q_step, k_step, v_step = rows_of(c, again)
        lw, ex = lw_s[c], ex_s[c]
        total = ex[slab - 1 :] + lw[slab - 1 :]
        if fast:
            middle = ex[slab // 2 : slab // 2 + 1]
            r_factor = jnp.exp(ex - middle)
            k_factor = jnp.exp(middle - ex - lw)
            into, out = jnp.exp(middle), jnp.exp(total - middle)
        else:
            r_factor = jnp.exp(ex)
            k_factor = jnp.exp(sums_of(after, split3(lw)))
            into = out = None
        return q_step, k_step, v_step, r, k, v, lw, total, r_factor, k_factor, into, out

    def scaled(x, by):
        return x if by is None else x * by

    def forward(c, carry):
        _, _, _, r, k, v, lw, total, r_factor, k_factor, into, out = load(c)
        rs, ks, vs = split2(r * r_factor), split2(k * k_factor), split2(v)
        yield
        memory = dot3(turned(vs), ks, NN)
        if fast:
            a = dot3(rs, ks, NT)
        else:

            def one_level(level, a):
                _, _, r_part, k_part, block, _ = level_parts(level, lw, r, k)
                return a + jnp.where(block, dot3(r_part, k_part, NT), 0.0)

            a = lax.fori_loop(0, levels, one_level, jnp.zeros(square, f32))
        yield
        own = jnp.sum(r * bonus * k, axis=1, keepdims=True)
        a = split2(jnp.where(below, a, 0.0) if fast else a)
        state = carry["state"]
        carry["state"] = state * jnp.exp(total) + scaled(memory, out)
        state_in = split2(scaled(state, into))
        yield
        o = own * v + dot3(a, vs, NN) + dot3(rs, state_in, NT)
        yield
        o = o - jnp.mean(o, axis=1, keepdims=True)
        yield
        rate = lax.rsqrt(jnp.mean(o * o, axis=1, keepdims=True) + NORM_EPS)
        normed = o * rate
        g = gain * (normed - teach[c].astype(f32))
        yield
        g = g - jnp.mean(g, axis=1, keepdims=True) - normed * jnp.mean(
            g * normed, axis=1, keepdims=True
        )
        yield
        state_s[c] = state
        g_s[c] = g * rate
        for held, parts in ((a_s, a), (r_s, rs), (k_s, ks), (v_s, vs)):
            held[c] = jnp.concatenate(parts, axis=1)

    def forward_some(i, state):
        carry = {"state": state}
        in_step(forward(i * unroll + n, carry) for n in range(unroll))
        return carry["state"]

    lax.fori_loop(0, chunks // unroll, forward_some, jnp.zeros((width, width), f32))

    def backward(c, carry):
        q_step, k_step, v_step, r, k, v, lw, total, r_factor, k_factor, into, out = load(c, True)
        a, rs, ks, vs = (halves(held[c]) for held in (a_s, r_s, k_s, v_s))
        g = g_s[c]
        gs = split2(g)
        yield
        memory = dot3(turned(gs), rs, NN)
        pair = dot3(gs, vs, NT)
        yield
        cot = carry["cot"]
        carry["cot"] = cot * jnp.exp(total) + scaled(memory, into)
        cot_out = split2(scaled(cot, out))
        state = state_s[c]
        state_in = split2(scaled(state, into))
        dlw = jnp.sum(state * jnp.exp(total) * cot, axis=0, keepdims=True)
        if fast:
            pairs = split2(jnp.where(below, pair, 0.0))
        yield
        dv = dot3(turned(a), gs, NN) + dot3(ks, cot_out, NT)
        dk = dot3(vs, cot_out, NN)
        if fast:
            dr = dot(
                stacked((gs[0], gs[1], pairs[0], pairs[1], gs[0], pairs[0], pairs[1]), 1),
                stacked((state_in[0], state_in[0], ks[0], ks[0], state_in[1], ks[1], ks[1]), 0),
                NN,
            )
            dk_in = dot4(turned(pairs), rs, NN)
            yield
            k_hat = joined(ks)
            from_earlier = k_hat * dk
            k_in = k_hat * dk_in
            from_later = joined(rs) * dr - k_in
            dlw = dlw - k_in
            dr = r_factor * dr
            dk = k_factor * (dk + dk_in)
        else:
            dr = dot3(gs, state_in, NN)
            from_earlier = joined(ks) * dk
            from_later = joined(rs) * dr
            dr = r_factor * dr
            dk = k_factor * dk

            def one_level(level, parts):
                dr, dk, dlw = parts
                r_by, k_by, r_part, k_part, block, span = level_parts(level, lw, r, k)
                pairs = split2(jnp.where(block & below, pair, 0.0))
                dr_in = r_by * dot3(pairs, k_part, NN)
                dk_in = k_by * dot3(pairs, r_part, TN)
                inside = split3(r * dr_in + k * dk_in)
                return dr + dr_in, dk + dk_in, dlw + sum(dot(span, part, TN) for part in inside)

            dr, dk, dlw = lax.fori_loop(
                0, levels, one_level, (dr, dk, jnp.broadcast_to(dlw, r.shape))
            )
        later, earlier = split3(from_later), split2(from_earlier)
        yield
        dlw = dlw + dot(sides, jnp.concatenate([*later, *earlier], axis=0), NN)
        dv = dv + jnp.sum(r * bonus * k, axis=1, keepdims=True) * g
        own = jnp.sum(v * g, axis=1, keepdims=True)
        yield
        own_r, own_k = own * r, own * k
        dr = dr + bonus * own_k
        dk = dk + bonus * own_r
        dpre = dlw * lw
        dpres = split2(dpre)
        yield
        hid = hid_s[c]
        dz = dot3(dpres, up_twice, NT)
        hid_t = in_s[2, c].T
        carry["up"] += dot(stacked((hid_t, hid_t), 1), stacked(dpres, 0), NN)
        yield
        dz = side_by_side(dz * (1.0 - hid * hid))
        yield
        dxw = dot(stacked((dz, dz), 1), down_deep, NN)
        dz_t = dz.T
        carry["down"] += dot(
            stacked((dz_t, dz_t), 1), stacked((in_s[0, c], in_s[1, c]), 0), NN
        )
        yield
        parts = (dr * q_step, dk * k_step, dv * v_step, dxw * q_step, dpre, own_r * k)
        carry["sums"] = tuple(
            old + jnp.sum(new.reshape(slab // 8, 8, width), axis=0)
            for old, new in zip(carry["sums"], parts)
        )

    def backward_some(i, carry):
        carry = dict(zip(("cot", "up", "down", "sums"), carry))
        in_step(backward(chunks - 1 - (i * unroll + n), carry) for n in range(unroll))
        return tuple(carry.values())

    rank = down[0].shape[0]
    empty = jnp.zeros((2 * rank, width), f32)
    start = (jnp.zeros((width, width), f32), empty, empty, (jnp.zeros((8, width), f32),) * 6)
    _, up_sum, down_sum, sums = lax.fori_loop(0, chunks // unroll, backward_some, start)
    tail = [split2(jnp.sum(part, axis=0, keepdims=True)) for part in sums]
    tail = [high.astype(f32) for high, _ in tail] + [low.astype(f32) for _, low in tail]
    tail.append(jnp.zeros((PACK_TAIL - len(tail), width), f32))
    up_sum, down_sum = (part[:rank] + part[rank:] for part in (up_sum, down_sum))
    return jnp.concatenate([up_sum, down_sum, *tail], axis=0)


def settings_of(head, mix_ref, bonus_ref):
    mix = [mix_ref[n, pl.ds(head, 1), :] for n in range(4)]
    return mix, bonus_ref[pl.ds(head, 1), :]


def in_order(pieces, scratch, place):
    if len(pieces) == 1:
        return pieces[0]
    near = len(pieces)
    for n, piece in enumerate(pieces):
        for far in range(piece.shape[0]):
            scratch[place ^ (far * near + n)] = piece[far]
    return scratch


def head_kernel(head_ref, q_ref, mix_ref, fade_ref, down_ref, up_ref, bonus_ref, *rest):
    slabs, per_device = q_ref.shape[:2]
    pieces, (out_ref, scores, *held, kv_s) = rest[:-15], rest[-15:]
    kv_ref = in_order(pieces, kv_s, head_ref[1])
    copies, shared = out_ref.shape[0], kv_ref.shape[1]
    for n in range(per_device):
        head = head_ref[0] + n
        mix, bonus = settings_of(head, mix_ref, bonus_ref)
        fade = fade_ref[pl.ds(head, 1), :]
        down, up = split2(down_ref[head]), split2(up_ref[head])
        group = n * shared // per_device
        refs = (
            lambda c, n=n: q_ref[c, n],
            lambda c, group=group: kv_ref[c, group, 0],
            lambda c, group=group: kv_ref[c, group, 1],
        )
        teacher = teacher_in_step(*refs, held[0], scores) if slabs <= 16 else None
        worst = decay_phase(
            refs[0], down, up, fade, mix, *held[1:5], math.gcd(4, slabs), teacher
        )
        if teacher is None:
            teacher_phase(*refs, held[0], scores)
        safe = jnp.max(worst) <= SAFE_EXPONENT

        def finish(fast, unroll):
            grads = student_phase(fast, refs, mix, bonus, down, up, held, unroll).astype(bf16)

            def copy_out(at, _):
                out_ref[at, n] = grads
                return 0

            lax.fori_loop(0, copies, copy_out, 0)

        @pl.when(safe)
        def _():
            finish(True, math.gcd(8 if slabs <= 16 else 2, slabs))

        @pl.when(jnp.logical_not(safe))
        def _():
            finish(False, 1)


def head_grads(q, pieces, place, mix, fade, down_t, up, bonus, copies):
    slabs, per_device, slab, width = q.shape
    rank = up.shape[1]
    assert 2 * rank == width
    packed_rows = 2 * rank + PACK_TAIL
    small = slabs <= 16
    k_slabs = math.gcd(2 if small else 4, slabs)
    q_slabs = k_slabs if small else 1
    blocks = slabs // k_slabs
    blocks = blocks * (blocks + 1) // 2 if small else blocks
    kv_shape = (slabs, *pieces[0].shape[1:]) if len(pieces) > 1 else (1, 16, width)
    vmem = pl.BlockSpec(memory_space=pltpu.VMEM)
    return pl.pallas_call(
        head_kernel,
        out_shape=jax.ShapeDtypeStruct((copies, per_device, packed_rows, width), bf16),
        in_specs=[pl.BlockSpec(memory_space=pltpu.SMEM)] + [vmem] * (6 + len(pieces)),
        out_specs=vmem,
        scratch_shapes=[
            pltpu.VMEM((blocks, q_slabs * slab, k_slabs * slab), f32),
            pltpu.VMEM((slabs, slab, width), bf16),
            pltpu.VMEM((slabs, slab, width), f32),
            pltpu.VMEM((slabs, slab, width), f32),
            pltpu.VMEM((slabs, slab, 2 * rank), f32),
            pltpu.VMEM((3, slabs, slab, width), bf16),
            pltpu.VMEM((slabs, width, width), f32),
            pltpu.VMEM((slabs, slab, width), f32),
            pltpu.VMEM((slabs, slab, 2 * slab), bf16),
            pltpu.VMEM((slabs, slab, 2 * width), bf16),
            pltpu.VMEM((slabs, slab, 2 * width), bf16),
            pltpu.VMEM((slabs, slab, 2 * width), bf16),
            pltpu.VMEM((6, slabs if small else 1, slab, width), f32),
            pltpu.VMEM(kv_shape, bf16),
        ],
        compiler_params=pltpu.CompilerParams(
            vmem_limit_bytes=(46 if small else 60) * 1024 * 1024
        ),
    )(place, q, mix, fade, down_t, up, bonus, *pieces)


def pack_queries(q_ref, out_ref):
    slots, _, width = out_ref.shape
    heads = q_ref.shape[1] // width
    for slot in range(slots):
        head = slot * heads // slots
        out_ref[slot] = q_ref[:, head * width : (head + 1) * width]


def pack_memory(group_of, place_ref, k_ref, v_ref, *out_refs):
    width = out_refs[0].shape[-1]
    for n, out_ref in enumerate(out_refs):
        start = group_of(place_ref[0], n) * width
        columns = pl.ds(start if isinstance(start, int) else pl.multiple_of(start, width), width)
        out_ref[0, 0, 0] = k_ref[:, columns]
        out_ref[0, 0, 1] = v_ref[:, columns]


def unpack_kernel(place_ref, *refs):
    *pieces, mix_ref, decay_ref, down_ref, up_ref, bonus_ref = refs
    heads, rank, _ = up_ref.shape
    for n in range(heads):
        if len(pieces) == 1:
            head, packed = n, pieces[0][n * (pieces[0].shape[0] // heads)]
        else:
            near = len(pieces)
            head, packed = place_ref[0] ^ n, pieces[n % near][n // near, 0]
        packed = packed.astype(f32)
        up_ref[head] = packed[:rank]
        down_ref[head] = packed[rank : 2 * rank]
        tail = packed[2 * rank :]
        tail = tail[:6] + tail[6:12]
        for at in range(4):
            mix_ref[at, pl.ds(head, 1), :] = tail[at : at + 1]
        decay_ref[pl.ds(head, 1), :] = tail[4:5]
        bonus_ref[pl.ds(head, 1), :] = tail[5:6]


def exchanged(x, differing, count):
    return lax.ppermute(x, "seq", [(d, d ^ differing) for d in range(count)])


def first_step(parts, near, count):
    got = [exchanged(part, n * near, count) if n else part for n, part in enumerate(parts)]
    return jnp.concatenate(got, axis=0)


def second_step(got, near, count):
    return [exchanged(got, n, count) if n else got for n in range(near)]


def shards(
    probe_vectors,
    mentor_address_vectors,
    mentor_content_vectors,
    previous_position_blend,
    feature_fading_exponent,
    fading_narrowing_matrix,
    fading_widening_matrix,
    diagonal_extra_amount,
):
    slab = probe_vectors.shape[0]
    heads, width, rank = fading_narrowing_matrix.shape
    place = lax.axis_index("seq")
    count = lax.axis_size("seq")
    copies = max(1, count // heads)
    per_device = max(1, heads // count)
    assert heads * copies == per_device * count
    groups = mentor_address_vectors.shape[1] // width
    by_bits = heads == count and count <= 16 and count & (count - 1) == 0 and count % groups == 0
    far, near = groups, count // groups
    vmem = pl.BlockSpec(memory_space=pltpu.VMEM)
    smem = pl.BlockSpec(memory_space=pltpu.SMEM)
    place = place.astype(jnp.int32)
    if by_bits:
        group_of = lambda place, n: (place // near) ^ n
        slots = far
    else:
        shared = max(1, per_device * groups // heads)
        firsts = [(d // copies) * per_device * groups // heads for d in range(count)]
        group_of = lambda _, n: firsts[n // shared] + n % shared
        slots = count * shared
    slot = jax.ShapeDtypeStruct((1, 1, 2, slab, width), bf16)
    kv = pl.pallas_call(
        functools.partial(pack_memory, group_of),
        out_shape=[slot] * slots,
        in_specs=[smem, vmem, vmem],
        out_specs=[vmem] * slots,
    )(place.reshape(1), mentor_address_vectors, mentor_content_vectors)
    if by_bits:
        kv, probe_vectors = lax.optimization_barrier((kv, probe_vectors))
        kv = first_step(kv, near, count)
    q = pl.pallas_call(
        pack_queries,
        out_shape=jax.ShapeDtypeStruct((heads * copies, slab, width), bf16),
        in_specs=[vmem],
        out_specs=vmem,
    )(probe_vectors)
    q = q.reshape(count, per_device, slab, width)
    if by_bits:
        kv, q = lax.optimization_barrier((kv, q))
        pieces = second_step(kv, near, count)
    q = lax.all_to_all(q, "seq", split_axis=0, concat_axis=0, tiled=True)
    if not by_bits:
        kv = jnp.stack(kv).reshape(count, shared, 2, slab, width)
        pieces = [lax.all_to_all(kv, "seq", split_axis=0, concat_axis=0, tiled=True)]
    packed = head_grads(
        q,
        pieces,
        jnp.stack([(place // copies) * per_device, place]),
        previous_position_blend,
        feature_fading_exponent,
        jnp.swapaxes(fading_narrowing_matrix, 1, 2),
        fading_widening_matrix,
        diagonal_extra_amount,
        1 if by_bits else count,
    )
    if by_bits:
        packed = second_step(first_step([packed] * far, near, count), near, count)
    else:
        packed = lax.all_to_all(packed, "seq", split_axis=0, concat_axis=0, tiled=True)
        packed = [packed.reshape(heads * copies, 2 * rank + PACK_TAIL, width)]
    vector = jax.ShapeDtypeStruct((heads, width), f32)
    matrix = jax.ShapeDtypeStruct((heads, rank, width), f32)
    mix, decay, down_t, up, bonus = pl.pallas_call(
        unpack_kernel,
        out_shape=(
            jax.ShapeDtypeStruct((4, heads, width), f32),
            vector,
            matrix,
            matrix,
            vector,
        ),
        in_specs=[smem] + [vmem] * len(packed),
        out_specs=[vmem] * 5,
    )(place.reshape(1), *packed)
    return mix, decay, jnp.swapaxes(down_t, 1, 2), up, bonus


def solution(mesh):
    return jax.shard_map(
        shards,
        mesh=mesh,
        in_specs=(
            P("seq", "head"),
            P("seq", "head"),
            P("seq", "head"),
            P(None, "head", None),
            P("head", None),
            P("head", None, None),
            P("head", None, None),
            P("head", None),
        ),
        out_specs=(
            P(None, "head", None),
            P("head", None),
            P("head", None, None),
            P("head", None, None),
            P("head", None),
        ),
        check_vma=False,
    )
```
